32 devices in a mesh: dp: 8 (over z, x), perm: 2 (over y), blk: 2 (over core).
Axes of the slice: x: 2, y: 2, z: 4, core: 2. Of those that a mesh axis runs over, the one named last changes fastest.
Arguments:
- tokens: bfloat16 [16, 1024, 768], P('dp', 'blk'), may hold values from -6 to 6
- lengths: int32 [16], P('dp'), may hold values from 513 to 1024, as said below
- head_route: int32 [12], P('perm'), may hold values from 0 to 1, as said below
- w_query: bfloat16 [768, 768], P('blk', 'perm'), may hold values from -0.21875 to 0.21875
- b_query: bfloat16 [768], P(('perm', 'blk')), may hold values from -3 to 3
- w_key: bfloat16 [768, 768], P('blk', 'perm'), may hold values from -0.21875 to 0.21875
- w_value: bfloat16 [768, 768], P('blk', 'perm'), may hold values from -0.21875 to 0.21875
- b_value: bfloat16 [768], P(('perm', 'blk')), may hold values from -3 to 3
- w_out: bfloat16 [768, 768], P('perm', 'blk'), may hold values from -3.5 to 3.5
- b_out: bfloat16 [768], P('blk'), may hold values from -3 to 3
- first_gain: bfloat16 [768], P('blk'), may hold values from 0.25 to 1.75
- first_shift: bfloat16 [768], P('blk'), may hold values from -3 to 3
- w_inner: bfloat16 [768, 3072], P('blk', 'perm'), may hold values from -0.21875 to 0.21875
- b_inner: bfloat16 [3072], P(('perm', 'blk')), may hold values from -3 to 3
- w_outer: bfloat16 [3072, 768], P('perm', 'blk'), may hold values from -0.109375 to 0.109375
- b_outer: bfloat16 [768], P('blk'), may hold values from -3 to 3
- second_gain: bfloat16 [768], P('blk'), may hold values from 0.25 to 1.75
- second_shift: bfloat16 [768], P('blk'), may hold values from -3 to 3
- cotangent: bfloat16 [16, 1024, 768], P('dp', 'blk'), may hold values from -6 to 6
Outputs:
- layer_out: bfloat16 [16, 1024, 768], P('dp', 'blk')
- grad_tokens: bfloat16 [16, 1024, 768], P('dp', 'blk')
- grad_w_query: float32 [768, 768], P('blk', 'perm')
- grad_b_query: float32 [768], P(('perm', 'blk'))
- grad_w_key: float32 [768, 768], P('blk', 'perm')
- grad_w_value: float32 [768, 768], P('blk', 'perm')
- grad_b_value: float32 [768], P(('perm', 'blk'))
- grad_w_out: float32 [768, 768], P('perm', 'blk')
- grad_b_out: float32 [768], P('blk')
- grad_first_gain: float32 [768], P('blk')
- grad_first_shift: float32 [768], P('blk')
- grad_w_inner: float32 [768, 3072], P('blk', 'perm')
- grad_b_inner: float32 [3072], P(('perm', 'blk'))
- grad_w_outer: float32 [3072, 768], P('perm', 'blk')
- grad_b_outer: float32 [768], P('blk')
- grad_second_gain: float32 [768], P('blk')
- grad_second_shift: float32 [768], P('blk')
The draws below stay inside these ranges and needn't reach their ends.
Inputs may be any that keep to these rules, and one draw needn't show every extreme that they name: `lengths`: every sequence holds more than 512 real tokens; in every draw some sequence is full. `head_route`: among the first 6 heads exactly half have 1, and likewise among the last 6.
All inputs are finite; a program needn't handle non-finite values.
Results may differ from the reference program's by a relative error of at most 0.018.
Values may be sent and summed in bfloat16 or wider, within the bound.
A program may use at most 192 MiB of HBM per device.

```python
import math
import jax
import jax.numpy as jnp
from jax import lax

D = 768
HEADS = 12
HD = 64
FF = 3072
BLOCKS = 2
SEQLEN = 1024
BL = 512
SEQS = 16


def draw_lengths(key, part):
    key = jax.random.fold_in(key, 11)
    key_base, key_pick = jax.random.split(key)
    span_half = SEQLEN // 2
    base_draw = jax.random.randint(key_base, (SEQS,), 0, span_half)
    shortened = base_draw * base_draw * base_draw // (span_half * span_half)
    seq_lengths = SEQLEN - shortened
    full_index = jax.random.randint(key_pick, (), 0, SEQS)
    return jnp.where(jnp.arange(SEQS) == full_index, SEQLEN, seq_lengths).astype(jnp.int32)


def draw_head_route(key, part):
    key = jax.random.fold_in(key, 23)
    key_first, key_second = jax.random.split(key)
    group_heads = HEADS // 2
    first_half = (jax.random.permutation(key_first, group_heads) < group_heads // 2).astype(jnp.int32)
    second_half = (jax.random.permutation(key_second, group_heads) < group_heads // 2).astype(jnp.int32)
    return jnp.concatenate([first_half, second_half])


def block_levels(key, shape, pieces, low, largest):
    level, own = 1.0, jax.random.fold_in(key, 6)
    for axis_at, blocks in pieces:
        steps = jnp.exp(jax.random.uniform(jax.random.fold_in(own, axis_at), (blocks,), jnp.float32, low / len(pieces), largest / len(pieces)))
        level = level * jnp.repeat(steps, shape[axis_at] // blocks).reshape([-1 if axis == axis_at else 1 for axis in range(len(shape))])
    return level


def scatter_about(key, extent, scale, bound, shards=(), kind=jnp.bfloat16):
    drawn = jax.random.normal(key, extent, jnp.float32) * scale
    if len(shards) > 0:
        drawn = block_levels(key, extent, shards, -0.22, 0.18) * drawn
    return jnp.clip(drawn, min=-bound, max=bound).astype(kind)


def setup_inputs(seed: int = 0) -> dict:
    streams_of = jax.random.split(jax.random.key(seed), 20)
    tokens = scatter_about(streams_of[0], (SEQS, SEQLEN, D), 1.0, 6.0, ((0, 8), (1, 2)))
    lengths = draw_lengths(jax.random.fold_in(streams_of[19], 71), 0)
    head_route = draw_head_route(jax.random.fold_in(streams_of[19], 71), 0)
    w_query = scatter_about(streams_of[3], (D, D), D ** -0.5, 0.21875, ((0, 2), (1, 2)))
    b_query = scatter_about(streams_of[4], (D,), 0.5, 3.0, ((0, 4),))
    w_key = scatter_about(streams_of[5], (D, D), D ** -0.5, 0.21875, ((0, 2), (1, 2)))
    w_value = scatter_about(streams_of[6], (D, D), D ** -0.5, 0.21875, ((0, 2), (1, 2)))
    b_value = scatter_about(streams_of[7], (D,), 0.5, 3.0, ((0, 4),))
    w_out = scatter_about(streams_of[8], (D, D), (max(D // 256, 1)) ** -0.5, 3.5, ((0, 2), (1, 2)))
    b_out = scatter_about(streams_of[9], (D,), 0.5, 3.0, ((0, 2),))
    first_gain = jnp.clip(1.0 + 0.15 * jax.random.normal(streams_of[10], (D,), jnp.float32), 0.25, 1.75).astype(jnp.bfloat16)
    first_shift = scatter_about(streams_of[11], (D,), 0.5, 3.0, ((0, 2),))
    w_inner = scatter_about(streams_of[12], (D, FF), D ** -0.5, 0.21875, ((0, 2), (1, 2)))
    b_inner = scatter_about(streams_of[13], (FF,), 0.5, 3.0, ((0, 4),))
    w_outer = scatter_about(streams_of[14], (FF, D), FF ** -0.5, 0.109375, ((0, 2), (1, 2)))
    b_outer = scatter_about(streams_of[15], (D,), 0.5, 3.0, ((0, 2),))
    second_gain = jnp.clip(1.0 + 0.15 * jax.random.normal(streams_of[16], (D,), jnp.float32), 0.25, 1.75).astype(jnp.bfloat16)
    second_shift = scatter_about(streams_of[17], (D,), 0.5, 3.0, ((0, 2),))
    cotangent = scatter_about(streams_of[18], (SEQS, SEQLEN, D), 1.0, 6.0, ((0, 8), (1, 2)))
    return {"tokens": tokens, "lengths": lengths, "head_route": head_route, "w_query": w_query, "b_query": b_query, "w_key": w_key, "w_value": w_value, "b_value": b_value, "w_out": w_out, "b_out": b_out, "first_gain": first_gain, "first_shift": first_shift, "w_inner": w_inner, "b_inner": b_inner, "w_outer": w_outer, "b_outer": b_outer, "second_gain": second_gain, "second_shift": second_shift, "cotangent": cotangent}


@jax.custom_vjp
def low(v):
    return lax.optimization_barrier(v.astype(jnp.bfloat16)).astype(jnp.float32)

@jax.custom_vjp
def low_back(v):
    return v

def low_keep(v):
    return (low(v), None)

def low_pass(kept, grad):
    return (grad,)

def back_keep(v):
    return (v, None)

def back_low(kept, grad):
    return (low(grad),)
low.defvjp(low_keep, low_pass)
low_back.defvjp(back_keep, back_low)
HIGHEST = lax.Precision.HIGHEST
EPSILON = 1e-05
MASKED_SCORE = -1e+30

def normalize(values, norm_gain, norm_shift):
    centre = values - lax.optimization_barrier(jnp.mean(values, axis=-1, keepdims=True))
    spread = lax.optimization_barrier(jnp.mean(centre * centre, axis=-1, keepdims=True))
    return centre * lax.rsqrt(spread + EPSILON) * norm_gain + norm_shift

def project(inputs, weight):
    return jnp.einsum('nd,de->ne', inputs, weight, precision=HIGHEST)

def layer(params, inputs, group_lengths, head_route):
    w_query, b_query, w_key, w_value, b_value, w_out, b_out, first_gain, first_shift, w_inner, b_inner, w_outer, b_outer, second_gain, second_shift = params
    seq_count = inputs.shape[0]
    token_rows = inputs.reshape(seq_count * SEQLEN, D)
    queries = low_back(low(project(token_rows, w_query) + b_query))
    key_rows = low_back(low(project(token_rows, w_key)))
    values = low_back(low(project(token_rows, w_value) + b_value))
    block_shape = (seq_count, BLOCKS, BL, HEADS, HD)
    queries = queries.reshape(block_shape)
    key_rows = key_rows.reshape(block_shape)
    values = values.reshape(block_shape)
    swapped = head_route.reshape(1, 1, 1, HEADS, 1) == 1
    key_rows = jnp.where(swapped, key_rows[:, ::-1], key_rows)
    values = jnp.where(swapped, values[:, ::-1], values)
    positions = jnp.arange(SEQLEN).reshape(BLOCKS, BL)
    key_valid = positions[None] < group_lengths[:, None, None]
    key_valid = jnp.where(head_route.reshape(1, 1, HEADS, 1) == 1, key_valid[:, ::-1][:, :, None, :], key_valid[:, :, None, :])
    score_scale = 1.0 / math.sqrt(HD)
    scores = low_back(jnp.einsum('cbqhe,cbkhe->cbhqk', queries, key_rows, precision=HIGHEST) * score_scale)
    masked = jnp.where(key_valid[:, :, :, None, :], scores, MASKED_SCORE)
    row_peak = lax.optimization_barrier(jnp.max(masked, axis=-1, keepdims=True))
    raised = jnp.exp(masked - row_peak)
    probabilities = raised / lax.optimization_barrier(jnp.sum(raised, axis=-1, keepdims=True))
    context = jnp.einsum('cbhqk,cbkhe->cbqhe', low(probabilities), values, precision=HIGHEST)
    context = low_back(low(context.reshape(seq_count * SEQLEN, D)))
    attended = low_back(project(context, w_out) + b_out)
    first_out = normalize(token_rows + attended, first_gain, first_shift)
    inner_pre = low_back(project(low(first_out), w_inner) + b_inner)
    active = jax.nn.gelu(inner_pre, approximate=True)
    outer_out = low_back(project(low(active), w_outer) + b_outer)
    result = normalize(first_out + outer_out, second_gain, second_shift)
    return result.reshape(seq_count, SEQLEN, D)

def reference(tokens, lengths, head_route, w_query, b_query, w_key, w_value, b_value, w_out, b_out, first_gain, first_shift, w_inner, b_inner, w_outer, b_outer, second_gain, second_shift, cotangent):
    params = tuple((member.astype(jnp.float32) for member in (w_query, b_query, w_key, w_value, b_value, w_out, b_out, first_gain, first_shift, w_inner, b_inner, w_outer, b_outer, second_gain, second_shift)))
    group_size = math.gcd(SEQS, 4)
    group_count = SEQS // group_size

    def one_group(totals, group_batch):
        group_inputs, group_lengths, group_cot = group_batch

        def forward(layer_params, layer_inputs):
            return layer(layer_params, layer_inputs, group_lengths, head_route)
        result, backward = jax.vjp(forward, params, group_inputs.astype(jnp.float32))
        grad_params, grad_inputs = backward(group_cot.astype(jnp.float32))
        totals = jax.tree.map(jnp.add, totals, grad_params)
        return (totals, (result.astype(jnp.bfloat16), grad_inputs.astype(jnp.bfloat16)))
    zeros = tuple((jnp.zeros_like(member) for member in params))
    totals, (outputs, grad_inputs) = lax.scan(one_group, zeros, (tokens.reshape(group_count, group_size, SEQLEN, D), lengths.reshape(group_count, group_size), cotangent.reshape(group_count, group_size, SEQLEN, D)))
    layer_out = outputs.reshape(SEQS, SEQLEN, D)
    grad_tokens = grad_inputs.reshape(SEQS, SEQLEN, D)
    return (layer_out, grad_tokens, totals[0], totals[1], totals[2], totals[3], totals[4], totals[5], totals[6], totals[7], totals[8], totals[9], totals[10], totals[11], totals[12], totals[13], totals[14])
```

```python
import functools
import math

import jax
import jax.numpy as jnp
from jax import lax
from jax.experimental import pallas as pl
from jax.experimental.pallas import tpu as pltpu
from jax.sharding import PartitionSpec as P

EPSILON = 1e-05
MASKED_SCORE = -1e30
MESH = pl.DeviceIdType.MESH
F32 = jnp.float32
BF16 = jnp.bfloat16
GELU_C = math.sqrt(2.0 / math.pi)


def nn(left, right):
    return lax.dot_general(left, right, (((1,), (0,)), ((), ())), preferred_element_type=F32)


def nt(left, right):
    return lax.dot_general(left, right, (((1,), (1,)), ((), ())), preferred_element_type=F32)


def al(value, multiple):
    return pl.multiple_of(value, multiple)


R_BQ, R_BV, R_BO, R_G1, R_S1, R_B2, R_G2, R_S2, R_B1, R_LANE, R_HEAD = 0, 1, 2, 3, 4, 5, 6, 7, 8, 12, 16


def layer_kernel(
    heads,
    tokens, cot, lengths, vec, wq, wk, wv, wo, w1, w2,
    layer_out, grad_tokens, gk, gs, gv,
    xo, xx, cotb, gwq, gwk, gwv, gwo, gw1, gw2, vecs, vecf, biasb,
    q, k, v, c, flow, xh1, rs1, lse, act, dact, acc, go, tA, tB, dc, dq, dk, dv, lob, wide, backs, backr, hrow, b1r, gb1,
    sem_l, sem_s, sem_r,
):
    d, p, b = lax.axis_index("dp"), lax.axis_index("perm"), lax.axis_index("blk")
    D = xo.shape[1]
    L = xo.shape[0]
    FF = gw2.shape[0]
    DH, FH = D // 2, FF // 2
    NP = heads // 4
    xbit = lax.rem(d, 2)
    core, ypeer, diag = (d, p, 1 - b), (d, 1 - p, b), (d, 1 - p, 1 - b)
    xpeer = (d + 1 - 2 * xbit, p, b)

    bar = pltpu.get_barrier_semaphore()
    peers = (core, ypeer, diag, xpeer)
    for peer in peers:
        pl.semaphore_signal(bar, 1, device_id=peer, device_id_type=MESH)
    pl.semaphore_wait(bar, len(peers))

    count = [0]
    sent = []

    def rc(src, dst, peer):
        i = count[0]
        count[0] += 1
        cp = pltpu.make_async_remote_copy(
            src_ref=src, dst_ref=dst, send_sem=sem_s.at[i], recv_sem=sem_r.at[i],
            device_id=peer, device_id_type=MESH)
        cp.start()
        sent.append(cp)
        return cp

    nl = [0]

    def lc(src, dst):
        i = nl[0]
        nl[0] += 1
        cp = pltpu.make_async_copy(src, dst, sem_l.at[i])
        cp.start()
        return cp

    shards = (wq, wk, wv, wo, w1, w2)
    full = (gwq, gwk, gwv, gwo, gw1, gw2)
    rows_by_blk = (True, True, True, False, True, False)

    def place(n, pp, bb):
        sr, sc = shards[n].shape
        if rows_by_blk[n]:
            return bb * sr, pp * sc, sr, sc
        return pp * sr, bb * sc, sr, sc

    def region(n, pp, bb):
        r0, c0, sr, sc = place(n, pp, bb)
        return full[n].at[pl.ds(al(r0, 128), sr), pl.ds(al(c0, 128), sc)]

    def region_half(n, pp, bb, xh):
        r0, c0, sr, sc = place(n, pp, bb)
        return full[n].at[pl.ds(al(r0 + xh * (sr // 2), 64), sr // 2), pl.ds(al(c0, 128), sc)]

    vecs[0] = vec[...]
    cp_x = lc(tokens.at[p], xo)
    own = [lc(shards[n], region(n, p, b)) for n in range(6)]
    cp_cot = lc(cot.at[p], cotb)
    v_c = rc(vecs.at[0], vecs.at[1], core)
    v_y = rc(vecs.at[0], vecs.at[2], ypeer)
    v_d = rc(vecs.at[0], vecs.at[3], diag)
    x_c = rc(tokens.at[p], xx, core)
    to_core = []
    to_y = []
    for n in range(6):
        sr = shards[n].shape[0]
        to_core.append(rc(shards[n], region(n, p, b), core))
        to_y.append(rc(shards[n].at[pl.ds(al(xbit * (sr // 2), 64), sr // 2)], region_half(n, p, b, xbit), ypeer))
    to_x = [None] * 6
    to_c1 = [None] * 6
    to_c2 = [None] * 6

    def svc1(n):
        to_y[n].wait_recv()
        src = region_half(n, 1 - p, b, xbit)
        to_x[n] = rc(src, src, xpeer)
        to_c1[n] = rc(src, src, core)

    def svc2(n):
        to_x[n].wait_recv()
        src = region_half(n, 1 - p, b, 1 - xbit)
        to_c2[n] = rc(src, src, core)

    def need(n):
        to_c1[n].wait_recv()
        to_c2[n].wait_recv()

    cp_x.wait()
    for cp in (v_c, v_y, v_d):
        cp.wait_recv()
    vecf[...] = (vecs[0] + vecs[1]) + (vecs[2] + vecs[3])
    for head in range(heads):
        hrow[head] = vecf[R_HEAD + head:R_HEAD + head + 1, 0:128]
    for t in range(FF // D):
        b1r[t] = vecf[R_B1 + t:R_B1 + t + 1, :]
    length = lengths[p]
    pos = lax.broadcasted_iota(jnp.int32, (L, 128), 0)
    for which in range(2):
        start = (b if which == 0 else 1 - b) * L
        biasb[which] = jnp.where(pos + start < length, 0.0, MASKED_SCORE)
    x_c.wait_recv()

    lane = lax.broadcasted_iota(jnp.int32, (1, 128), 1)

    def head_lanes(hh):
        return (lane < 64) if hh == 0 else (lane >= 64)

    def head_bias(head):
        return jnp.where(hrow[head] > 0.5, biasb[1], biasb[0])

    def project(h):
        cols = pl.ds(al(h * DH, 128), DH)
        swapped = vecf[R_LANE:R_LANE + 1, cols] > 0.5
        q[:, cols] = (nn(xo[...], gwq[:, cols]) + vecf[R_BQ:R_BQ + 1, cols]).astype(BF16) * jnp.asarray(0.125, BF16)
        k[:, cols] = jnp.where(swapped, nn(xx[...], gwk[:, cols]), nn(xo[...], gwk[:, cols])).astype(BF16)
        v[:, cols] = (jnp.where(swapped, nn(xx[...], gwv[:, cols]), nn(xo[...], gwv[:, cols]))
                      + vecf[R_BV:R_BV + 1, cols]).astype(BF16)

    def attend(h, j):
        cols = pl.ds(al(h * DH + j * 128, 128), 128)
        kp, vp = k[:, cols], v[:, cols]
        vT = vp.T
        tops = []
        for hh in range(2):
            head = h * (heads // 2) + 2 * j + hh
            km = jnp.where(head_lanes(hh), kp, jnp.zeros_like(kp))
            bias = head_bias(head)
            bias = jnp.concatenate([bias, bias], axis=1)
            parts = []
            for t in range(L // 256):
                s = nt(km, q[t * 256:(t + 1) * 256, cols]) + bias
                peak = jnp.max(s, axis=0, keepdims=True)
                e = jnp.exp(s - peak)
                total = jnp.sum(e, axis=0, keepdims=True)
                lse[head, :, t * 256:(t + 1) * 256] = peak + jnp.log(total)
                parts.append(nn(vT[hh * 64:(hh + 1) * 64, :], e.astype(BF16)) * (1.0 / total))
            tops.append(jnp.concatenate(parts, axis=1))
        c[:, cols] = jnp.concatenate(tops, axis=0).T.astype(BF16)

    for n in range(4):
        own[n].wait()
        to_core[n].wait_recv()
    project(p)
    svc1(0)
    svc1(1)

    def own_pair(j, carry):
        attend(p, j)
        return carry

    lax.fori_loop(0, NP, own_pair, 0)
    svc1(2)
    svc1(3)
    for n in range(4):
        svc2(n)
    for n in range(4):
        need(n)
    project(1 - p)

    def other_pair(j, carry):
        attend(1 - p, j)
        return carry

    lax.fori_loop(0, NP, other_pair, 0)
    svc1(4)
    svc1(5)

    acc[...] = nn(c[...], gwo[...])
    TR = 128

    def rows_of(i):
        return pl.ds(al(i * TR, TR), TR)

    def norm1(i, carry):
        r = rows_of(i)
        val = xo[r, :].astype(F32) + (acc[r, :] + vecf[R_BO:R_BO + 1, :])
        centre = val - jnp.mean(val, axis=1, keepdims=True)
        spread = jnp.mean(centre * centre, axis=1, keepdims=True)
        rs = lax.rsqrt(spread + EPSILON)
        xh = centre * rs
        xh1[r, :] = xh
        rs1[r, :] = jnp.broadcast_to(rs, (TR, 128))
        flow[r, :] = (xh * vecf[R_G1:R_G1 + 1, :] + vecf[R_S1:R_S1 + 1, :]).astype(BF16)
        return carry

    lax.fori_loop(0, L // TR, norm1, 0)
    tA[...] = flow[...].T

    NT = FH // D

    def ff_tile(h, i, first):
        hid = pl.ds(al(h * FH + i * D, 128), D)
        wide[...] = nn(flow[...], gw1[:, hid])

        def gelu_rows(j, carry):
            r = pl.ds(al(j * 32, 32), 32)
            u = wide[r, :] + b1r[h * NT + i]
            uu = u * u
            th = jnp.tanh(GELU_C * u * (1.0 + 0.044715 * uu))
            half = 0.5 * (1.0 + th)
            act[r, hid] = (u * half).astype(BF16)
            slope = half + 0.5 * u * (1.0 - th * th) * (GELU_C * (1.0 + 3 * 0.044715 * uu))
            dact[r, hid] = slope.astype(BF16)
            return carry

        lax.fori_loop(0, L // 32, gelu_rows, 0)
        out = nn(act[:, hid], gw2[hid, :])
        if first:
            acc[...] = out
        else:
            acc[...] += out

    for n in (4, 5):
        own[n].wait()
        to_core[n].wait_recv()
    ff_tile(p, 0, True)
    for i in range(1, NT):
        ff_tile(p, i, False)
    svc2(4)
    svc2(5)
    need(4)
    need(5)

    def ff_other(i, carry):
        ff_tile(1 - p, i, False)
        return carry

    lax.fori_loop(0, NT, ff_other, 0)

    cp_cot.wait()
    zero = jnp.zeros((1, D), F32)
    for r0 in range(gv.shape[0]):
        gv[r0:r0 + 1, :] = zero

    def colsum(x):
        return jnp.sum(x, axis=0, keepdims=True)

    def norm2(i, carry):
        dg, ds, db = carry
        r = rows_of(i)
        fo = xh1[r, :] * vecf[R_G1:R_G1 + 1, :] + vecf[R_S1:R_S1 + 1, :]
        val = fo + (acc[r, :] + vecf[R_B2:R_B2 + 1, :])
        centre = val - jnp.mean(val, axis=1, keepdims=True)
        spread = jnp.mean(centre * centre, axis=1, keepdims=True)
        rs = lax.rsqrt(spread + EPSILON)
        xh = centre * rs
        g2 = vecf[R_G2:R_G2 + 1, :]
        lob[r, :] = (xh * g2 + vecf[R_S2:R_S2 + 1, :]).astype(BF16)
        up = cotb[r, :].astype(F32)
        dxh = up * g2
        gin = rs * (dxh - jnp.mean(dxh, axis=1, keepdims=True) - xh * jnp.mean(dxh * xh, axis=1, keepdims=True))
        acc[r, :] = gin
        low = gin.astype(BF16)
        go[r, :] = low
        return dg + colsum(up * xh), ds + colsum(up), db + colsum(low.astype(F32))

    dg, ds, db = lax.fori_loop(0, L // TR, norm2, (zero, zero, zero))
    gv[R_G2:R_G2 + 1, :] = dg
    gv[R_S2:R_S2 + 1, :] = ds
    gv[R_B2:R_B2 + 1, :] = db
    lo_local = lc(lob, layer_out.at[p])
    lo_y = rc(lob, layer_out.at[p], ypeer)

    tB[...] = go[...].T
    keep_rows = pl.ds(al(b * DH, 128), DH)
    send_rows = pl.ds(al((1 - b) * DH, 128), DH)

    def weight_grad(leftT, right, h, col, width):
        at = pl.ds(al(col, 128), width)
        gs[h, :, at] = nn(leftT[send_rows, :], right).astype(BF16)
        gk[h, :, at] = nn(leftT[keep_rows, :], right).astype(BF16)

    def ff_back(h, i):
        hid = pl.ds(al(h * FH + i * D, 128), D)
        du = (nt(go[...], gw2[hid, :]) * dact[:, hid].astype(F32)).astype(BF16)
        gb1[h * NT + i] = colsum(du.astype(F32))
        dact[:, hid] = du
        acc[...] += nt(dact[:, hid], gw1[:, hid])
        weight_grad(tA, dact[:, hid], h, i * D, D)
        weight_grad(tB, act[:, hid], h, FH + i * D, D)

    def ff_back_own(i, carry):
        ff_back(p, i)
        return carry

    def ff_back_other(i, carry):
        ff_back(1 - p, i)
        return carry

    lax.fori_loop(0, NT, ff_back_other, 0)
    lax.fori_loop(0, NT, ff_back_own, 0)

    for t in range(FF // D):
        gv[R_B1 + t:R_B1 + t + 1, :] = gb1[t]

    def norm1_back(i, carry):
        dg, ds, db = carry
        r = rows_of(i)
        up = acc[r, :]
        xh = xh1[r, :]
        dxh = up * vecf[R_G1:R_G1 + 1, :]
        gin = rs1[r, 0:1] * (dxh - jnp.mean(dxh, axis=1, keepdims=True) - xh * jnp.mean(dxh * xh, axis=1, keepdims=True))
        acc[r, :] = gin
        low = gin.astype(BF16)
        go[r, :] = low
        return dg + colsum(up * xh), ds + colsum(up), db + colsum(low.astype(F32))

    dg, ds, db = lax.fori_loop(0, L // TR, norm1_back, (zero, zero, zero))
    gv[R_G1:R_G1 + 1, :] = dg
    gv[R_S1:R_S1 + 1, :] = ds
    gv[R_BO:R_BO + 1, :] = db
    tB[...] = go[...].T
    dc[...] = nt(go[...], gwo[...]).astype(BF16)
    for h in range(2):
        weight_grad(tB, c[:, h * DH:(h + 1) * DH], h, 2 * FH, DH)
    tA[...] = xo[...].T
    tB[...] = xx[...].T

    def attend_back(j, carry):
        cols = pl.ds(al(j * 128, 128), 128)
        kp, vp, qp, dcp = k[:, cols], v[:, cols], q[:, cols], dc[:, cols]
        kT = kp.T
        dkv = [jnp.zeros((L, 128), F32), jnp.zeros((L, 128), F32)]
        tops = []
        for hh in range(2):
            head = 2 * j + hh
            mine = head_lanes(hh)
            none = jnp.zeros_like(kp)
            km, vm = jnp.where(mine, kp, none), jnp.where(mine, vp, none)
            qm, dcm = jnp.where(mine, qp, none), jnp.where(mine, dcp, none)
            bias = head_bias(head)
            bias = jnp.concatenate([bias, bias], axis=1)
            parts = []
            for t in range(L // 256):
                ts = slice(t * 256, (t + 1) * 256)
                prob = jnp.exp(nt(km, qp[ts]) + bias - lse[head, :, ts])
                dprob = nt(vm, dcp[ts])
                delta = jnp.sum(prob * dprob, axis=0, keepdims=True)
                dscore = (prob * (dprob - delta)).astype(BF16)
                dkv[1] += nn(prob.astype(BF16), dcm[ts])
                dkv[0] += nn(dscore, qm[ts])
                parts.append(nn(kT[hh * 64:(hh + 1) * 64, :], dscore))
            tops.append(jnp.concatenate(parts, axis=1))
        dq[:, cols] = (jnp.concatenate(tops, axis=0).T * 0.125).astype(BF16)
        dk[:, cols] = dkv[0].astype(BF16)
        dv[:, cols] = dkv[1].astype(BF16)
        return carry

    lax.fori_loop(0, 2 * NP, attend_back, 0)
    gv[R_BQ:R_BQ + 1, :] = colsum(dq[...].astype(F32))
    gv[R_BV:R_BV + 1, :] = colsum(dv[...].astype(F32))

    swapped = vecf[R_LANE:R_LANE + 1, :] > 0.5
    none = jnp.zeros((L, D), BF16)
    dc[...] = jnp.where(swapped, dk[...], none)
    flow[...] = jnp.where(swapped, dv[...], none)
    dk[...] = jnp.where(swapped, none, dk[...])
    dv[...] = jnp.where(swapped, none, dv[...])
    backs[...] = (nt(dc[...], gwk[...]) + nt(flow[...], gwv[...])).astype(BF16)
    back_c = rc(backs, backr, core)
    for h in range(2):
        hs = slice(h * DH, (h + 1) * DH)
        for n, (a, x) in enumerate(((dq, None), (dk, dc), (dv, flow))):
            at = slice(2 * FH + DH + n * DH, 2 * FH + 2 * DH + n * DH)
            for dst, rows in ((gs, send_rows), (gk, keep_rows)):
                val = nn(tA[rows, :], a[:, hs])
                if x is not None:
                    val = val + nn(tB[rows, :], x[:, hs])
                dst[h, :, at] = val.astype(BF16)
    acc[...] += nt(dq[...], gwq[...]) + nt(dk[...], gwk[...]) + nt(dv[...], gwv[...])
    lo_local.wait()
    lo_y.wait_send()
    back_c.wait_recv()
    lob[...] = (acc[...] + backr[...].astype(F32)).astype(BF16)
    gt_local = lc(lob, grad_tokens.at[p])
    gt_y = rc(lob, grad_tokens.at[p], ypeer)
    gt_local.wait()
    gt_y.wait_recv()
    lo_y.wait_recv()
    for cp in sent:
        if cp is not lo_y:
            cp.wait_send()


def per_device(
    tokens, lengths, head_route, w_query, b_query, w_key, w_value, b_value, w_out, b_out,
    first_gain, first_shift, w_inner, b_inner, w_outer, b_outer, second_gain, second_shift, cotangent,
):
    p, b = lax.axis_index("perm"), lax.axis_index("blk")
    L, D = tokens.shape[1:]
    FF = w_inner.shape[1] * 2
    heads = head_route.shape[0] * 2
    hd = D // heads
    quarter = p * 2 + b

    def put(vector, offset, keep=None):
        vector = vector.astype(F32)
        if keep is not None:
            vector = jnp.where(keep, vector, 0.0)
        return lax.dynamic_update_slice(jnp.zeros((D,), F32), vector, (offset,))

    first_p, first_b = p == 0, b == 0
    by_blk = b * (D // 2)
    route = head_route.astype(F32)
    rows = [put(b_query, quarter * (D // 4)), put(b_value, quarter * (D // 4))]
    rows += [put(a, by_blk, first_p) for a in (b_out, first_gain, first_shift, b_outer, second_gain, second_shift)]
    hidden = lax.dynamic_update_slice(jnp.zeros((FF,), F32), b_inner.astype(F32), (quarter * (FF // 4),)).reshape(FF // D, D)
    lane_route = put(jnp.repeat(route, hd), p * (D // 2), first_b)
    head_rows = lax.dynamic_update_slice(
        jnp.zeros((16, D), F32),
        jnp.broadcast_to(jnp.where(first_b, route, 0.0)[:, None], (heads // 2, D)),
        (p * (heads // 2), 0))
    vec = jnp.concatenate([jnp.stack(rows), hidden, lane_route[None], jnp.zeros((3, D), F32), head_rows], axis=0)

    half = FF + 4 * (D // 2)
    any_ = pl.BlockSpec(memory_space=pl.ANY)
    vm = pl.BlockSpec(memory_space=pltpu.VMEM)
    V = pltpu.VMEM
    layer_out, grad_tokens, gk, gs, gv = pl.pallas_call(
        functools.partial(layer_kernel, heads),
        out_shape=(
            jax.ShapeDtypeStruct(tokens.shape, BF16),
            jax.ShapeDtypeStruct(tokens.shape, BF16),
            jax.ShapeDtypeStruct((2, D // 2, half), BF16),
            jax.ShapeDtypeStruct((2, D // 2, half), BF16),
            jax.ShapeDtypeStruct((16, D), F32),
        ),
        in_specs=[any_, any_, pl.BlockSpec(memory_space=pltpu.SMEM), vm] + [any_] * 6,
        out_specs=(any_, any_, vm, vm, vm),
        scratch_shapes=[
            V((L, D), BF16), V((L, D), BF16), V((L, D), BF16),
            V((D, D), BF16), V((D, D), BF16), V((D, D), BF16), V((D, D), BF16), V((D, FF), BF16), V((FF, D), BF16),
            V((4, 32, D), F32), V((32, D), F32), V((2, L, 128), F32),
            V((L, D), BF16), V((L, D), BF16), V((L, D), BF16), V((L, D), BF16),
            V((L, D), BF16), V((L, D), F32), V((L, 128), F32), V((16, 1, L), F32),
            V((L, FF), BF16), V((L, FF), BF16), V((L, D), F32), V((L, D), BF16),
            V((D, L), BF16), V((D, L), BF16), V((L, D), BF16),
            V((L, D), BF16), V((L, D), BF16), V((L, D), BF16), V((L, D), BF16),
            V((L, D), F32), V((L, D), BF16), V((L, D), BF16),
            V((16, 1, 128), F32), V((FF // D, 1, D), F32), V((FF // D, 1, D), F32),
            pltpu.SemaphoreType.DMA((16,)),
            pltpu.SemaphoreType.DMA((48,)),
            pltpu.SemaphoreType.DMA((48,)),
        ],
        compiler_params=pltpu.CompilerParams(collective_id=0, has_side_effects=True, vmem_limit_bytes=62 * 2**20),
        name="layer",
    )(tokens, cotangent, lengths, vec, w_query, w_key, w_value, w_out, w_inner, w_outer)

    share = gk.astype(F32) + lax.ppermute(gs, "blk", [(0, 1), (1, 0)]).astype(F32)
    other = lax.dynamic_index_in_dim(share, 1 - p, 0, keepdims=False).astype(BF16)
    mine = lax.dynamic_index_in_dim(share, p, 0, keepdims=False)
    mine = mine + lax.ppermute(other, "perm", [(0, 1), (1, 0)]).astype(F32)
    mine = lax.psum(mine.astype(BF16), "dp").astype(F32)
    vectors = lax.psum(gv, ("dp", "perm", "blk"))

    DH, FH = D // 2, FF // 2
    at = 2 * FH

    def of_blk(row):
        return lax.dynamic_slice(vectors[row], (b * DH,), (DH,))

    def of_quarter(row):
        return lax.dynamic_slice(vectors[row], (quarter * (D // 4),), (D // 4,))

    hidden_grad = lax.dynamic_slice(vectors[R_B1:R_B1 + FF // D].reshape(FF), (quarter * (FF // 4),), (FF // 4,))
    return (
        layer_out,
        grad_tokens,
        mine[:, at + DH:at + 2 * DH],
        of_quarter(R_BQ),
        mine[:, at + 2 * DH:at + 3 * DH],
        mine[:, at + 3 * DH:at + 4 * DH],
        of_quarter(R_BV),
        mine[:, at:at + DH].T,
        of_blk(R_BO),
        of_blk(R_G1),
        of_blk(R_S1),
        mine[:, :FH],
        hidden_grad,
        mine[:, FH:at].T,
        of_blk(R_B2),
        of_blk(R_G2),
        of_blk(R_S2),
    )


def solution(mesh):
    placed = (
        P("dp", "blk", None), P("dp"), P("perm"), P("blk", "perm"), P(("perm", "blk")), P("blk", "perm"),
        P("blk", "perm"), P(("perm", "blk")), P("perm", "blk"), P("blk"), P("blk"), P("blk"), P("blk", "perm"),
        P(("perm", "blk")), P("perm", "blk"), P("blk"), P("blk"), P("blk"), P("dp", "blk", None),
    )
    outs = (
        P("dp", "blk", None), P("dp", "blk", None), P("blk", "perm"), P(("perm", "blk")), P("blk", "perm"),
        P("blk", "perm"), P(("perm", "blk")), P("perm", "blk"), P("blk"), P("blk"), P("blk"), P("blk", "perm"),
        P(("perm", "blk")), P("perm", "blk"), P("blk"), P("blk"), P("blk"),
    )
    return jax.shard_map(per_device, mesh=mesh, in_specs=placed, out_specs=outs, check_vma=False)
```

```python
import functools
import math

import jax
import jax.numpy as jnp
from jax import lax
from jax.experimental import pallas as pl
from jax.experimental.pallas import tpu as pltpu
from jax.sharding import PartitionSpec as P

EPSILON = 1e-05
MASKED_SCORE = -1e30
MESH = pl.DeviceIdType.MESH
F32 = jnp.float32
BF16 = jnp.bfloat16
GELU_C = math.sqrt(2.0 / math.pi)


def nn(left, right):
    return lax.dot_general(left, right, (((1,), (0,)), ((), ())), preferred_element_type=F32)


def nt(left, right):
    return lax.dot_general(left, right, (((1,), (1,)), ((), ())), preferred_element_type=F32)


def al(value, multiple):
    return pl.multiple_of(value, multiple)


R_BQ, R_BV, R_BO, R_G1, R_S1, R_B2, R_G2, R_S2, R_B1, R_LANE = 0, 1, 2, 3, 4, 5, 6, 7, 8, 12
BY_BLK = (R_BO, R_G1, R_S1, R_B2, R_G2, R_S2)

ORDER = ("y", 0, 1, 2)


def unit_table(DH, FH, D):
    tail = 2 * FH
    table = []
    for i in range(FH // D):
        table.append((i * D, D, ORDER))
        table.append((FH + i * D, D, ORDER))
    for i in range(4):
        table.append((tail + i * DH, DH, ORDER))
    return table


def stage_shapes(table, DH, bits):
    shapes = []
    for col, width, order in table:
        rows, halves = DH, 2
        for axis in order:
            if axis == "y":
                halves = 1
            elif axis < bits:
                rows //= 2
            else:
                continue
            shapes.append((halves, rows, width))
        for _ in range(bits - 3):
            shapes.append((1, rows, width))
    return shapes


def layer_kernel(
    heads, dp_size,
    tokens, cot, lengths, vec, wq, wk, wv, wo, w1, w2,
    layer_out, grad_tokens, gk_out, gv,
    xo, xx, cotb, gwq, gwk, gwv, gwo, gw1, gw2, vecs, vecf, biasb,
    q, k, v, c, flow, xh1, rs1, lse, act, dact, acc, go, tA, tB, lob, wide, backr, hrow, b1r, gb1,
    gk, gs, rcore, gvr,
    *rest,
):
    sem_l, sem_s, sem_r = rest[-3:]
    landing = list(rest[:-3])
    d, p, b = lax.axis_index("dp"), lax.axis_index("perm"), lax.axis_index("blk")
    D = xo.shape[1]
    L = xo.shape[0]
    FF = gw2.shape[0]
    DH, FH = D // 2, FF // 2
    NP = heads // 4
    xbit = lax.rem(d, 2)
    dq, dk, dv, dc = (act.at[:, i * D:(i + 1) * D] for i in range(4))
    backs = dact.at[:, 0:D]
    core, ypeer, diag = (d, p, 1 - b), (d, 1 - p, b), (d, 1 - p, 1 - b)
    dp_bits = (dp_size - 1).bit_length()

    def bit(t):
        return lax.rem(lax.div(d, 2**t), 2)

    def peer_of(t):
        return (d + 2**t - 2 ** (t + 1) * bit(t), p, b)

    xpeer = peer_of(0)

    bar = pltpu.get_barrier_semaphore()
    peers = (core, ypeer, diag) + tuple(peer_of(t) for t in range(dp_bits))
    for peer in peers:
        pl.semaphore_signal(bar, 1, device_id=peer, device_id_type=MESH)
    pl.semaphore_wait(bar, len(peers))

    count = [0]
    sent = []
    waited = []

    def rc(src, dst, peer):
        i = count[0]
        count[0] += 1
        cp = pltpu.make_async_remote_copy(
            src_ref=src, dst_ref=dst, send_sem=sem_s.at[i], recv_sem=sem_r.at[i],
            device_id=peer, device_id_type=MESH)
        cp.start()
        sent.append(cp)
        return cp

    nl = [0]

    def lc(src, dst):
        i = nl[0]
        nl[0] += 1
        cp = pltpu.make_async_copy(src, dst, sem_l.at[i])
        cp.start()
        return cp

    shards = (wq, wk, wv, wo, w1, w2)
    full = (gwq, gwk, gwv, gwo, gw1, gw2)
    rows_by_blk = (True, True, True, False, True, False)

    def place(n, pp, bb):
        sr, sc = shards[n].shape
        if rows_by_blk[n]:
            return bb * sr, pp * sc, sr, sc
        return pp * sr, bb * sc, sr, sc

    def region(n, pp, bb):
        r0, c0, sr, sc = place(n, pp, bb)
        return full[n].at[pl.ds(al(r0, 128), sr), pl.ds(al(c0, 128), sc)]

    def region_half(n, pp, bb, xh):
        r0, c0, sr, sc = place(n, pp, bb)
        return full[n].at[pl.ds(al(r0 + xh * (sr // 2), 64), sr // 2), pl.ds(al(c0, 128), sc)]

    quarter = p * 2 + b
    vecs[quarter] = vec[...]
    cp_x = lc(tokens.at[p], xo)
    own = [lc(shards[n], region(n, p, b)) for n in range(6)]
    cp_cot = lc(cot.at[p], cotb)
    v_c = rc(vec, vecs.at[quarter], core)
    v_y = rc(vec, vecs.at[quarter], ypeer)
    v_d = rc(vec, vecs.at[quarter], diag)
    x_c = rc(tokens.at[p], xx, core)
    to_core = []
    to_y = []
    for n in range(6):
        sr = shards[n].shape[0]
        to_core.append(rc(shards[n], region(n, p, b), core))
        to_y.append(rc(shards[n].at[pl.ds(al(xbit * (sr // 2), 64), sr // 2)], region_half(n, p, b, xbit), ypeer))
    to_x = [None] * 6
    to_c1 = [None] * 6
    to_c2 = [None] * 6

    def svc1(n):
        to_y[n].wait_recv()
        src = region_half(n, 1 - p, b, xbit)
        to_x[n] = rc(src, src, xpeer)
        to_c1[n] = rc(src, src, core)

    def svc2(n):
        to_x[n].wait_recv()
        src = region_half(n, 1 - p, b, 1 - xbit)
        to_c2[n] = rc(src, src, core)

    def need(n):
        to_c1[n].wait_recv()
        to_c2[n].wait_recv()

    cp_x.wait()
    for cp in (v_c, v_y, v_d):
        cp.wait_recv()
    DQ = D // 4
    for row in (R_BQ, R_BV):
        vecf[row:row + 1, :] = jnp.concatenate([vecs[i, row:row + 1, 0:DQ] for i in range(4)], axis=1)
    for row in BY_BLK:
        vecf[row:row + 1, :] = jnp.concatenate([vecs[i, row:row + 1, 0:DH] for i in range(2)], axis=1)
    vecf[R_LANE:R_LANE + 1, :] = jnp.concatenate([vecs[2 * i, R_LANE:R_LANE + 1, 0:DH] for i in range(2)], axis=1)
    for t in range(FF // D):
        per = D * 4 // FF
        b1r[t] = jnp.concatenate([vecs[i, R_B1:R_B1 + 1, 0:FF // 4] for i in range(t * per, t * per + per)], axis=1)
    for pair in range(heads // 2):
        two = vecf[R_LANE:R_LANE + 1, pair * 128:pair * 128 + 128]
        hrow[2 * pair] = jnp.broadcast_to(two[:, 0:1], (1, 128))
        hrow[2 * pair + 1] = jnp.broadcast_to(two[:, 64:65], (1, 128))
    length = lengths[p]
    pos = lax.broadcasted_iota(jnp.int32, (L, 128), 0)
    for which in range(2):
        start = (b if which == 0 else 1 - b) * L
        biasb[which] = jnp.where(pos + start < length, 0.0, MASKED_SCORE)
    x_c.wait_recv()

    lane = lax.broadcasted_iota(jnp.int32, (1, 128), 1)

    def head_lanes(hh):
        return (lane < 64) if hh == 0 else (lane >= 64)

    def head_bias(head):
        return jnp.where(hrow[head] > 0.5, biasb[1], biasb[0])

    def project(h):
        cols = pl.ds(al(h * DH, 128), DH)
        swapped = vecf[R_LANE:R_LANE + 1, cols] > 0.5
        q[:, cols] = (nn(xo[...], gwq[:, cols]) + vecf[R_BQ:R_BQ + 1, cols]).astype(BF16) * jnp.asarray(0.125, BF16)
        k[:, cols] = jnp.where(swapped, nn(xx[...], gwk[:, cols]), nn(xo[...], gwk[:, cols])).astype(BF16)
        v[:, cols] = (jnp.where(swapped, nn(xx[...], gwv[:, cols]), nn(xo[...], gwv[:, cols]))
                      + vecf[R_BV:R_BV + 1, cols]).astype(BF16)

    def attend(h, j):
        cols = pl.ds(al(h * DH + j * 128, 128), 128)
        kp, vp = k[:, cols], v[:, cols]
        vT = vp.T
        tops = []
        for hh in range(2):
            head = h * (heads // 2) + 2 * j + hh
            km = jnp.where(head_lanes(hh), kp, jnp.zeros_like(kp))
            bias = head_bias(head)
            bias = jnp.concatenate([bias, bias], axis=1)
            parts = []
            for t in range(L // 256):
                s = nt(km, q[t * 256:(t + 1) * 256, cols]) + bias
                peak = jnp.max(s, axis=0, keepdims=True)
                e = jnp.exp(s - peak)
                total = jnp.sum(e, axis=0, keepdims=True)
                lse[head, :, t * 256:(t + 1) * 256] = peak + jnp.log(total)
                parts.append(nn(vT[hh * 64:(hh + 1) * 64, :], e.astype(BF16)) * (1.0 / total))
            tops.append(jnp.concatenate(parts, axis=1))
        c[:, cols] = jnp.concatenate(tops, axis=0).T.astype(BF16)

    for n in range(4):
        own[n].wait()
        to_core[n].wait_recv()
    project(p)
    svc1(0)
    svc1(1)

    def own_pair(j, carry):
        attend(p, j)
        return carry

    lax.fori_loop(0, NP, own_pair, 0)
    svc1(2)
    svc1(3)
    for n in range(4):
        svc2(n)
    for n in range(4):
        need(n)
    project(1 - p)

    def other_pair(j, carry):
        attend(1 - p, j)
        return carry

    lax.fori_loop(0, NP, other_pair, 0)
    svc1(4)
    svc1(5)

    acc[...] = nn(c[...], gwo[...])
    TR = 128

    def rows_of(i):
        return pl.ds(al(i * TR, TR), TR)

    def norm1(i, carry):
        r = rows_of(i)
        val = xo[r, :].astype(F32) + (acc[r, :] + vecf[R_BO:R_BO + 1, :])
        centre = val - jnp.mean(val, axis=1, keepdims=True)
        spread = jnp.mean(centre * centre, axis=1, keepdims=True)
        rs = lax.rsqrt(spread + EPSILON)
        xh = centre * rs
        xh1[r, :] = xh
        rs1[r, :] = jnp.broadcast_to(rs, (TR, 128))
        flow[r, :] = (xh * vecf[R_G1:R_G1 + 1, :] + vecf[R_S1:R_S1 + 1, :]).astype(BF16)
        return carry

    lax.fori_loop(0, L // TR, norm1, 0)
    tA[...] = flow[...].T

    NT = FH // D

    def ff_tile(h, i, first):
        hid = pl.ds(al(h * FH + i * D, 128), D)
        wide[...] = nn(flow[...], gw1[:, hid])

        def gelu_rows(j, carry):
            r = pl.ds(al(j * 32, 32), 32)
            u = wide[r, :] + b1r[h * NT + i]
            uu = u * u
            th = jnp.tanh(GELU_C * u * (1.0 + 0.044715 * uu))
            half = 0.5 * (1.0 + th)
            act[r, hid] = (u * half).astype(BF16)
            slope = half + 0.5 * u * (1.0 - th * th) * (GELU_C * (1.0 + 3 * 0.044715 * uu))
            dact[r, hid] = slope.astype(BF16)
            return carry

        lax.fori_loop(0, L // 32, gelu_rows, 0)
        out = nn(act[:, hid], gw2[hid, :])
        if first:
            acc[...] = out
        else:
            acc[...] += out

    for n in (4, 5):
        own[n].wait()
        to_core[n].wait_recv()
    ff_tile(p, 0, True)
    for i in range(1, NT):
        ff_tile(p, i, False)
    svc2(4)
    svc2(5)
    need(4)
    need(5)

    def ff_other(i, carry):
        ff_tile(1 - p, i, False)
        return carry

    lax.fori_loop(0, NT, ff_other, 0)

    cp_cot.wait()
    zero = jnp.zeros((1, D), F32)
    for r0 in range(gv.shape[0]):
        gv[r0:r0 + 1, :] = zero

    def colsum(x):
        return jnp.sum(x, axis=0, keepdims=True)

    def norm2(i, carry):
        dg, ds, db = carry
        r = rows_of(i)
        fo = xh1[r, :] * vecf[R_G1:R_G1 + 1, :] + vecf[R_S1:R_S1 + 1, :]
        val = fo + (acc[r, :] + vecf[R_B2:R_B2 + 1, :])
        centre = val - jnp.mean(val, axis=1, keepdims=True)
        spread = jnp.mean(centre * centre, axis=1, keepdims=True)
        rs = lax.rsqrt(spread + EPSILON)
        xh = centre * rs
        g2 = vecf[R_G2:R_G2 + 1, :]
        lob[r, :] = (xh * g2 + vecf[R_S2:R_S2 + 1, :]).astype(BF16)
        up = cotb[r, :].astype(F32)
        dxh = up * g2
        gin = rs * (dxh - jnp.mean(dxh, axis=1, keepdims=True) - xh * jnp.mean(dxh * xh, axis=1, keepdims=True))
        acc[r, :] = gin
        low = gin.astype(BF16)
        go[r, :] = low
        return dg + colsum(up * xh), ds + colsum(up), db + colsum(low.astype(F32))

    dg, ds, db = lax.fori_loop(0, L // TR, norm2, (zero, zero, zero))
    gv[R_G2:R_G2 + 1, :] = dg
    gv[R_S2:R_S2 + 1, :] = ds
    gv[R_B2:R_B2 + 1, :] = db
    lo_local = lc(lob, layer_out.at[p])
    lo_y = rc(lob, layer_out.at[p], ypeer)

    tB[...] = go[...].T
    keep_rows = pl.ds(al(b * DH, 128), DH)
    send_rows = pl.ds(al((1 - b) * DH, 128), DH)

    table = unit_table(DH, FH, D)
    units = []
    for col, width, order in table:
        order = [axis for axis in order if axis == "y" or axis < dp_bits]
        bufs = [landing.pop(0) for _ in range(len(order) + max(dp_bits - 3, 0))]
        units.append({"at": slice(col, col + width), "order": order, "bufs": bufs, "next": 0, "r0": 0, "rows": DH,
                      "both": True, "core": [None, None], "copy": None, "path": []})

    def core_send(u, src, h_is_own):
        h = p if h_is_own else 1 - p
        units[u]["core"][h_is_own] = rc(src, rcore.at[h, :, units[u]["at"]], core)

    def add_block(h, r0, rows, at, src):
        step = 48 if rows % 48 == 0 else rows

        def one(i, carry):
            here = pl.ds(al(r0 + i * step, 16), step)
            gk[h, here, at] = (gk[h, here, at].astype(F32) + src(pl.ds(al(i * step, 16), step)).astype(F32)).astype(BF16)
            return carry

        lax.fori_loop(0, rows // step, one, 0)

    def start_stage(u, s):
        un = units[u]
        axis, buf, at = un["order"][s], un["bufs"][s], un["at"]
        if axis == "y":
            here = pl.ds(al(un["r0"], 16), un["rows"])
            un["copy"] = rc(gk.at[1 - p, here, at], buf.at[0], ypeer)
            un["both"] = False
            return
        rows = un["rows"] // 2
        away = pl.ds(al(un["r0"] + (1 - bit(axis)) * rows, 16), rows)
        src = gk.at[:, away, at] if un["both"] else gk.at[pl.ds(p, 1), away, at]
        un["copy"] = rc(src, buf, peer_of(axis))
        un["path"].append((axis, un["r0"], un["rows"]))
        un["r0"] = un["r0"] + bit(axis) * rows
        un["rows"] = rows

    def step(u):
        un = units[u]
        ev, n, at = un["next"], len(un["order"]), un["at"]
        un["next"] += 1
        if ev == 0:
            for own in (0, 1):
                un["core"][own].wait_recv()
                h = p if own else 1 - p
                add_block(h, 0, DH, at, lambda r, h=h: rcore[h, r, at])
            start_stage(u, 0)
            return
        un["copy"].wait_recv()
        if ev <= n:
            buf = un["bufs"][ev - 1]
            if un["both"]:
                for h in range(2):
                    add_block(h, un["r0"], un["rows"], at, lambda r, h=h: buf[h, r, :])
            else:
                add_block(p, un["r0"], un["rows"], at, lambda r: buf[0, r, :])
            if ev < n:
                start_stage(u, ev)
                return
            for t in range(3, dp_bits):
                buf = un["bufs"][n + t - 3]
                mine = gk.at[pl.ds(p, 1), pl.ds(al(un["r0"], 16), un["rows"]), at]
                cp = rc(mine, buf, peer_of(t))
                cp.wait_recv()
                cp.wait_send()
                waited.append(id(cp))
                add_block(p, un["r0"], un["rows"], at, lambda r: buf[0, r, :])
            here = pl.ds(al(un["r0"], 16), un["rows"])
            un["bufs"][0][0, here, :] = gk[p, here, at]
        if un["path"]:
            axis, r0, rows = un["path"].pop()
            mine = un["bufs"][0].at[0, pl.ds(al(un["r0"], 16), un["rows"])]
            un["copy"] = rc(mine, mine, peer_of(axis))
            un["r0"], un["rows"] = r0, rows
            return
        un["out"] = lc(un["bufs"][0].at[0], gk_out.at[:, at])

    def total_events(u):
        un = units[u]
        return 2 * len(un["order"])

    def weight_grad(leftT, right, send, own, col, width):
        h = p if own else 1 - p
        send[...] = nn(leftT[send_rows, :], right).astype(BF16)
        gk[h, :, col:col + width] = nn(leftT[keep_rows, :], right).astype(BF16)

    def ff_back(own, i):
        h = p if own else 1 - p
        hid = pl.ds(al(h * FH + i * D, 128), D)
        du = (nt(go[...], gw2[hid, :]) * dact[:, hid].astype(F32)).astype(BF16)
        gb1[h * NT + i] = colsum(du.astype(F32))
        dact[:, hid] = du
        acc[...] += nt(dact[:, hid], gw1[:, hid])
        for u, leftT, side in ((2 * i, tA, dact), (2 * i + 1, tB, act)):
            send = side.at[0:DH, hid]
            weight_grad(leftT, side[:, hid], send, own, table[u][0], D)
            core_send(u, send, own)

    for i in range(NT):
        ff_back(0, i)
        ff_back(1, i)
        if i > 0:
            step(2 * i - 2)
            step(2 * i - 1)
    for t in range(FF // D):
        gv[R_B1 + t:R_B1 + t + 1, :] = gb1[t]

    def norm1_back(i, carry):
        dg, ds, db = carry
        r = rows_of(i)
        up = acc[r, :]
        xh = xh1[r, :]
        dxh = up * vecf[R_G1:R_G1 + 1, :]
        gin = rs1[r, 0:1] * (dxh - jnp.mean(dxh, axis=1, keepdims=True) - xh * jnp.mean(dxh * xh, axis=1, keepdims=True))
        acc[r, :] = gin
        low = gin.astype(BF16)
        go[r, :] = low
        return dg + colsum(up * xh), ds + colsum(up), db + colsum(low.astype(F32))

    dg, ds, db = lax.fori_loop(0, L // TR, norm1_back, (zero, zero, zero))
    gv[R_G1:R_G1 + 1, :] = dg
    gv[R_S1:R_S1 + 1, :] = ds
    gv[R_BO:R_BO + 1, :] = db
    tB[...] = go[...].T
    UO = 2 * NT
    step(UO - 2)
    step(UO - 1)
    for u in range(UO):
        for cp in units[u]["core"]:
            cp.wait_send()
            waited.append(id(cp))
    dc[...] = nt(go[...], gwo[...]).astype(BF16)
    tail = 2 * FH

    def part(n, h):
        return gs.at[h, :, n * DH:(n + 1) * DH]

    for own in (0, 1):
        h = p if own else 1 - p
        weight_grad(tB, c[:, pl.ds(al(h * DH, 128), DH)], part(0, h), own, tail, DH)
        core_send(UO, part(0, h), own)
    tA[...] = xo[...].T
    tB[...] = xx[...].T

    def attend_back(j, carry):
        cols = pl.ds(al(j * 128, 128), 128)
        kp, vp, qp, dcp = k[:, cols], v[:, cols], q[:, cols], dc[:, cols]
        kT = kp.T
        dkv = [jnp.zeros((L, 128), F32), jnp.zeros((L, 128), F32)]
        tops = []
        for hh in range(2):
            head = 2 * j + hh
            mine = head_lanes(hh)
            none = jnp.zeros_like(kp)
            km, vm = jnp.where(mine, kp, none), jnp.where(mine, vp, none)
            qm, dcm = jnp.where(mine, qp, none), jnp.where(mine, dcp, none)
            bias = head_bias(head)
            bias = jnp.concatenate([bias, bias], axis=1)
            parts = []
            for t in range(L // 256):
                ts = slice(t * 256, (t + 1) * 256)
                prob = jnp.exp(nt(km, qp[ts]) + bias - lse[head, :, ts])
                dprob = nt(vm, dcp[ts])
                delta = jnp.sum(prob * dprob, axis=0, keepdims=True)
                dscore = (prob * (dprob - delta)).astype(BF16)
                dkv[1] += nn(prob.astype(BF16), dcm[ts])
                dkv[0] += nn(dscore, qm[ts])
                parts.append(nn(kT[hh * 64:(hh + 1) * 64, :], dscore))
            tops.append(jnp.concatenate(parts, axis=1))
        dq[:, cols] = (jnp.concatenate(tops, axis=0).T * 0.125).astype(BF16)
        dk[:, cols] = dkv[0].astype(BF16)
        dv[:, cols] = dkv[1].astype(BF16)
        return carry

    lax.fori_loop(0, NP, attend_back, 0)
    step(UO)
    lax.fori_loop(NP, 2 * NP, attend_back, 0)
    gv[R_BQ:R_BQ + 1, :] = colsum(dq[...].astype(F32))
    gv[R_BV:R_BV + 1, :] = colsum(dv[...].astype(F32))

    swapped = vecf[R_LANE:R_LANE + 1, :] > 0.5
    none = jnp.zeros((L, D), BF16)
    dc[...] = jnp.where(swapped, dk[...], none)
    flow[...] = jnp.where(swapped, dv[...], none)
    dk[...] = jnp.where(swapped, none, dk[...])
    dv[...] = jnp.where(swapped, none, dv[...])
    backs[...] = (nt(dc[...], gwk[...]) + nt(flow[...], gwv[...])).astype(BF16)
    back_c = rc(backs, backr, core)
    for own in (0, 1):
        h = p if own else 1 - p
        hs = pl.ds(al(h * DH, 128), DH)
        for n, (a, x) in enumerate(((dq, None), (dk, dc), (dv, flow))):
            u = UO + 1 + n
            send = part(1 + n, h)
            for dst, rows in ((send, send_rows), (gk.at[h, :, table[u][0]:table[u][0] + DH], keep_rows)):
                val = nn(tA[rows, :], a[:, hs])
                if x is not None:
                    val = val + nn(tB[rows, :], x[:, hs])
                dst[...] = val.astype(BF16)
            core_send(u, send, own)
    vec_peers = [core, ypeer] + [peer_of(t) for t in range(dp_bits)]
    vstate = {"s": 0, "cp": None}
    gvr[0, 0] = gv[...]

    def vec_step():
        s = vstate["s"]
        if s > 0:
            vstate["cp"].wait_recv()
            total = gvr[s - 1, 0] + gvr[s - 1, 1]
            if s == len(vec_peers):
                gv[...] = total
                return
            gvr[s, 0] = total
        vstate["cp"] = rc(gvr.at[s, 0], gvr.at[s, 1], vec_peers[s])
        vstate["s"] = s + 1

    vec_step()
    acc[...] += nt(dq[...], gwq[...]) + nt(dk[...], gwk[...]) + nt(dv[...], gwv[...])
    step(0)
    step(1)
    for n in range(3):
        step(UO + 1 + n)
    lo_local.wait()
    back_c.wait_recv()
    for r0 in range(0, L, TR):
        acc[r0:r0 + TR, :] += backr[r0:r0 + TR, :].astype(F32)
    lo_y.wait_send()
    waited.append(id(lo_y))
    lob[...] = acc[...].astype(BF16)
    gt_local = lc(lob, grad_tokens.at[p])
    gt_y = rc(lob, grad_tokens.at[p], ypeer)
    order = []
    for u in range(len(units)):
        for ev in range(units[u]["next"], total_events(u)):
            order.append((ev * 1.0 + u * 1.0 + 0.01 * u, u))
    order.sort()
    for i, (_, u) in enumerate(order):
        step(u)
        if i % 4 == 3 and vstate["s"] <= len(vec_peers) and i // 4 < len(vec_peers):
            vec_step()
    for _ in range(len(vec_peers) - len(order) // 4):
        vec_step()
    for un in units:
        un["out"].wait()
    gt_local.wait()
    gt_y.wait_recv()
    lo_y.wait_recv()
    for cp in sent:
        if id(cp) not in waited:
            cp.wait_send()


def finish_kernel(
    gk, gv, g_wq, g_bq, g_wk, g_wv, g_bv, g_wo, g_bo, g_g1, g_s1, g_w1, g_b1, g_w2, g_b2, g_g2, g_s2
):
    p, b = lax.axis_index("perm"), lax.axis_index("blk")
    D = gv.shape[1]
    DH, FH = D // 2, g_w1.shape[1]
    tail = 2 * FH
    g_w1[...] = gk[:, 0:FH].astype(F32)
    for i in range(FH // DH):
        g_w2[i * DH:(i + 1) * DH, :] = gk[:, FH + i * DH:FH + (i + 1) * DH].astype(F32).T
    g_wo[...] = gk[:, tail:tail + DH].astype(F32).T
    for n, ref in enumerate((g_wq, g_wk, g_wv)):
        ref[...] = gk[:, tail + (n + 1) * DH:tail + (n + 2) * DH].astype(F32)
    for row, ref in ((R_BO, g_bo), (R_G1, g_g1), (R_S1, g_s1), (R_B2, g_b2), (R_G2, g_g2), (R_S2, g_s2)):
        ref[...] = jnp.where(b == 0, gv[row:row + 1, 0:DH], gv[row:row + 1, DH:D])
    for row, ref in ((R_BQ, g_bq), (R_BV, g_bv)):
        n = D // 4
        left = jnp.where(b == 0, gv[row:row + 1, 0:n], gv[row:row + 1, n:2 * n])
        right = jnp.where(b == 0, gv[row:row + 1, 2 * n:3 * n], gv[row:row + 1, 3 * n:D])
        ref[...] = jnp.where(p == 0, left, right)
    left = jnp.where(b == 0, gv[R_B1:R_B1 + 1, :], gv[R_B1 + 1:R_B1 + 2, :])
    right = jnp.where(b == 0, gv[R_B1 + 2:R_B1 + 3, :], gv[R_B1 + 3:R_B1 + 4, :])
    g_b1[...] = jnp.where(p == 0, left, right)


def per_device(
    tokens, lengths, head_route, w_query, b_query, w_key, w_value, b_value, w_out, b_out,
    first_gain, first_shift, w_inner, b_inner, w_outer, b_outer, second_gain, second_shift, cotangent,
):
    L, D = tokens.shape[1:]
    FF = w_inner.shape[1] * 2
    heads = head_route.shape[0] * 2
    hd = D // heads

    def padded(vector):
        return jnp.pad(vector.astype(F32), (0, D - vector.shape[0]))

    none = jnp.zeros((D,), F32)
    rows = [b_query, b_value, b_out, first_gain, first_shift, b_outer, second_gain, second_shift, b_inner]
    rows = [padded(row) for row in rows] + [none] * 3
    rows += [padded(jnp.repeat(head_route, hd))] + [none] * 3
    vec = jnp.concatenate(rows).reshape(16, D)
    bits = (lax.axis_size("dp") - 1).bit_length()

    half = FF + 4 * (D // 2)
    any_ = pl.BlockSpec(memory_space=pl.ANY)
    vm = pl.BlockSpec(memory_space=pltpu.VMEM)
    V = pltpu.VMEM
    layer_out, grad_tokens, reduced, vectors = pl.pallas_call(
        functools.partial(layer_kernel, heads, lax.axis_size("dp")),
        out_shape=(
            jax.ShapeDtypeStruct(tokens.shape, BF16),
            jax.ShapeDtypeStruct(tokens.shape, BF16),
            jax.ShapeDtypeStruct((D // 2, half), BF16),
            jax.ShapeDtypeStruct((16, D), F32),
        ),
        in_specs=[any_, any_, pl.BlockSpec(memory_space=pltpu.SMEM), vm] + [any_] * 6,
        out_specs=(any_, any_, any_, vm),
        scratch_shapes=[
            V((L, D), BF16), V((L, D), BF16), V((L, D), BF16),
            V((D, D), BF16), V((D, D), BF16), V((D, D), BF16), V((D, D), BF16), V((D, FF), BF16), V((FF, D), BF16),
            V((4, 16, D), F32), V((16, D), F32), V((2, L, 128), F32),
            V((L, D), BF16), V((L, D), BF16), V((L, D), BF16), V((L, D), BF16),
            V((L, D), BF16), V((L, D), F32), V((L, 128), F32), V((16, 1, L), F32),
            V((L, FF), BF16), V((L, FF), BF16), V((L, D), F32), V((L, D), BF16),
            V((D, L), BF16), V((D, L), BF16), V((L, D), BF16),
            V((L, D), F32), V((L, D), BF16),
            V((16, 1, 128), F32), V((FF // D, 1, D), F32), V((FF // D, 1, D), F32),
            V((2, D // 2, half), BF16), V((2, D // 2, 4 * (D // 2)), BF16), V((2, D // 2, half), BF16),
            V((2 + bits, 2, 16, D), F32),
        ] + [V(shape, BF16) for shape in stage_shapes(unit_table(D // 2, FF // 2, D), D // 2, bits)] + [
            pltpu.SemaphoreType.DMA((24,)),
            pltpu.SemaphoreType.DMA((192,)),
            pltpu.SemaphoreType.DMA((192,)),
        ],
        compiler_params=pltpu.CompilerParams(collective_id=0, has_side_effects=True, vmem_limit_bytes=62 * 2**20),
        name="layer",
    )(tokens, cotangent, lengths, vec, w_query, w_key, w_value, w_out, w_inner, w_outer)

    DH, FH = D // 2, FF // 2
    shapes = [(DH, DH), (1, D // 4), (DH, DH), (DH, DH), (1, D // 4), (DH, DH), (1, DH), (1, DH), (1, DH), (DH, FH),
              (1, FF // 4), (FH, DH), (1, DH), (1, DH), (1, DH)]
    grads = pl.pallas_call(
        finish_kernel,
        out_shape=[jax.ShapeDtypeStruct(shape, F32) for shape in shapes],
        in_specs=[vm, vm],
        out_specs=[vm] * len(shapes),
        compiler_params=pltpu.CompilerParams(vmem_limit_bytes=48 * 2**20),
        name="finish",
    )(reduced, vectors)
    grads = [g.reshape(-1) if g.shape[0] == 1 else g for g in grads]
    return (layer_out, grad_tokens, *grads)


def solution(mesh):
    placed = (
        P("dp", "blk", None), P("dp"), P("perm"), P("blk", "perm"), P(("perm", "blk")), P("blk", "perm"),
        P("blk", "perm"), P(("perm", "blk")), P("perm", "blk"), P("blk"), P("blk"), P("blk"), P("blk", "perm"),
        P(("perm", "blk")), P("perm", "blk"), P("blk"), P("blk"), P("blk"), P("dp", "blk", None),
    )
    outs = (
        P("dp", "blk", None), P("dp", "blk", None), P("blk", "perm"), P(("perm", "blk")), P("blk", "perm"),
        P("blk", "perm"), P(("perm", "blk")), P("perm", "blk"), P("blk"), P("blk"), P("blk"), P("blk", "perm"),
        P(("perm", "blk")), P("perm", "blk"), P("blk"), P("blk"), P("blk"),
    )
    return jax.shard_map(per_device, mesh=mesh, in_specs=placed, out_specs=outs, check_vma=False)
```

```python
import functools
import math

import jax
import jax.numpy as jnp
from jax import lax
from jax.experimental import pallas as pl
from jax.experimental.pallas import tpu as pltpu
from jax.sharding import PartitionSpec as P

EPSILON = 1e-05
MASKED_SCORE = -1e30
MESH = pl.DeviceIdType.MESH
F32 = jnp.float32
BF16 = jnp.bfloat16
GELU_C = math.sqrt(2.0 / math.pi)


def nn(left, right):
    return lax.dot_general(left, right, (((1,), (0,)), ((), ())), preferred_element_type=F32)


def nt(left, right):
    return lax.dot_general(left, right, (((1,), (1,)), ((), ())), preferred_element_type=F32)


def al(value, multiple):
    return pl.multiple_of(value, multiple)


R_BQ, R_BV, R_BO, R_G1, R_S1, R_B2, R_G2, R_S2, R_B1, R_LANE = 0, 1, 2, 3, 4, 5, 6, 7, 8, 12
BY_BLK = (R_BO, R_G1, R_S1, R_B2, R_G2, R_S2)

ORDERS = (
    (0, 1, "y", 2),
    ("y", 0, 1, 2),
    (1, 0, "y", 2),
    ("y", 1, 0, 2),
    (0, 1, "y", 2),
    (0, "y", 1, 2),
    ("y", 0, 1, 2),
    ("y", 0, 1, 2),
)
EVENTS = {
        "ff00": (),
        "ff01": (),
        "ff10": (0, 1),
        "ff11": (),
        "n1": (),
        "wo": (2, 3, 4),
        "ab0": (0, 1),
        "ab1": (4,),
        "ab2": (2,),
        "q5": (1, 0, 3),
        "q6": (4, 5),
        "q7": (1, 2, 6, 4, 0),
        "acc": (7, 2, 3, 5, 1),
        "drain": (4, 0, 6, 3, 2, 1, 6, 4, 7, 0, 1, 5, 6, 7, 3, 4, 2, 0, 5, 6, 1, 7, 3, 4, 5, 6, 2, 7, 5, 6, 0, 2, 7,
        3, 5, 6, 7, 5, 7, 3),
}
LO_FIRST, LO_PLACE = 2, "end"


def unit_table(DH, FH, D):
    tail = 2 * FH
    table = []
    for i in range(FH // D):
        table += [(i * D, D), (FH + i * D, D)]
    table += [(tail + i * DH, DH) for i in range(4)]
    return [(col, width, order) for (col, width), order in zip(table, ORDERS)]


def stage_shapes(table, DH, bits):
    shapes = []
    for col, width, order in table:
        rows, halves = DH, 2
        for axis in order:
            if axis == "y":
                halves = 1
            elif axis < bits:
                rows //= 2
            else:
                continue
            shapes.append((halves, rows, width))
        for _ in range(bits - 3):
            shapes.append((1, rows, width))
    shapes += [(1, DH, width) for _, width, order in table if order[0] != "y"]
    return shapes


def layer_kernel(
    heads, dp_size,
    tokens, cot, lengths, vec, wq, wk, wv, wo, w1, w2,
    layer_out, grad_tokens, gk_out, gv,
    xo, xx, cotb, gwq, gwk, gwv, gwo, gw1, gw2, vecs, vecf, biasb,
    q, k, v, c, flow, xh1, rs1, lse, act, dact, acc, go, tA, tB, lob, wide, backr, hrow, b1r, gb1,
    gk, rcore, gvr,
    *rest,
):
    sem_l, sem_s, sem_r = rest[-3:]
    landing, landing_res = list(rest[:-3]), []
    d, p, b = lax.axis_index("dp"), lax.axis_index("perm"), lax.axis_index("blk")
    D = xo.shape[1]
    L = xo.shape[0]
    FF = gw2.shape[0]
    DH, FH = D // 2, FF // 2
    NP = heads // 4
    xbit = lax.rem(d, 2)
    dq, dk, dv, dc = (act.at[:, i * D:(i + 1) * D] for i in range(4))
    backs = dact.at[:, 0:D]
    core, ypeer, diag = (d, p, 1 - b), (d, 1 - p, b), (d, 1 - p, 1 - b)
    dp_bits = (dp_size - 1).bit_length()

    def bit(t):
        return lax.rem(lax.div(d, 2**t), 2)

    def peer_of(t):
        return (d + 2**t - 2 ** (t + 1) * bit(t), p, b)

    xpeer = peer_of(0)

    bar = pltpu.get_barrier_semaphore()
    peers = (core, ypeer, diag) + tuple(peer_of(t) for t in range(dp_bits))
    for peer in peers:
        pl.semaphore_signal(bar, 1, device_id=peer, device_id_type=MESH)
    pl.semaphore_wait(bar, len(peers))

    count = [0]
    sent = []
    waited = []

    def rc(src, dst, peer):
        i = count[0]
        count[0] += 1
        cp = pltpu.make_async_remote_copy(
            src_ref=src, dst_ref=dst, send_sem=sem_s.at[i], recv_sem=sem_r.at[i],
            device_id=peer, device_id_type=MESH)
        cp.start()
        sent.append(cp)
        return cp

    nl = [0]

    def lc(src, dst):
        i = nl[0]
        nl[0] += 1
        cp = pltpu.make_async_copy(src, dst, sem_l.at[i])
        cp.start()
        return cp

    pieces = [(wq, gwq, True, 0, wq.shape[1]), (wk, gwk, True, 0, wk.shape[1]), (wv, gwv, True, 0, wv.shape[1]),
              (wo, gwo, False, 0, wo.shape[0])]
    for i in range(FH // D):
        pieces += [(w1, gw1, True, i * D, D), (w2, gw2, False, i * D, D)]
    NW = len(pieces)

    def extent(n):
        shard, _, by_blk, _, size = pieces[n]
        return (shard.shape[0], size) if by_blk else (size, shard.shape[1])

    def span(n, pp, bb, r0, rows):
        shard, full, by_blk, first, size = pieces[n]
        sr, sc = shard.shape
        if by_blk:
            return full.at[pl.ds(al(bb * sr + r0, 16), rows), pl.ds(al(pp * sc + first, 128), size)]
        return full.at[pl.ds(al(pp * sr + first + r0, 16), rows), pl.ds(al(bb * sc, 128), sc)]

    def shard_rows(n, r0, rows):
        shard, _, by_blk, first, size = pieces[n]
        if by_blk:
            return shard.at[pl.ds(al(r0, 16), rows), first:first + size]
        return shard.at[pl.ds(al(first + r0, 16), rows), :]

    zbit = bit(1)
    zpeer = peer_of(1)

    def fourth(n, xb, zb):
        rows = extent(n)[0] // 4
        return (2 * xb + zb) * rows, rows

    def third(n, xb, zb, i):
        r0, rows = fourth(n, xb, zb)
        return r0 + i * (rows // 3), rows // 3

    quarter = p * 2 + b
    vecs[quarter] = vec[...]
    cp_x = lc(tokens.at[p], xo)
    own = [lc(shard_rows(n, 0, extent(n)[0]), span(n, p, b, 0, extent(n)[0])) for n in range(NW)]
    cp_cot = lc(cot.at[p], cotb)
    v_c = rc(vec, vecs.at[quarter], core)
    v_y = rc(vec, vecs.at[quarter], ypeer)
    v_d = rc(vec, vecs.at[quarter], diag)
    to_core, to_y, to_y3 = [], [], []
    for n in range(NW):
        to_core.append(rc(shard_rows(n, 0, extent(n)[0]), span(n, p, b, 0, extent(n)[0]), core))
        if n == 2:
            x_c = rc(tokens.at[p], xx, core)
        r = fourth(n, xbit, zbit)
        to_y.append(rc(shard_rows(n, *r), span(n, p, b, *r), ypeer))
        r = third(n, 1 - xbit, 1 - zbit, 0)
        to_y3.append(rc(shard_rows(n, *r), span(n, p, b, *r), ypeer))
    to_x, to_z, to_x3, to_z3 = ([None] * NW for _ in range(4))
    fwd = [[] for _ in range(NW)]

    def svc_a(n):
        to_y[n].wait_recv()
        src = span(n, 1 - p, b, *fourth(n, xbit, zbit))
        to_x[n] = rc(src, src, xpeer)
        to_z[n] = rc(src, src, zpeer)
        fwd[n].append(rc(src, src, core))

    def svc_b(n):
        to_x[n].wait_recv()
        src = span(n, 1 - p, b, *third(n, 1 - xbit, zbit, 2))
        to_z3[n] = rc(src, src, zpeer)
        to_z[n].wait_recv()
        src = span(n, 1 - p, b, *third(n, xbit, 1 - zbit, 1))
        to_x3[n] = rc(src, src, xpeer)
        for r in (fourth(n, 1 - xbit, zbit), fourth(n, xbit, 1 - zbit)):
            src = span(n, 1 - p, b, *r)
            fwd[n].append(rc(src, src, core))

    def svc_c(n):
        for cp in (to_y3[n], to_x3[n], to_z3[n]):
            cp.wait_recv()
        src = span(n, 1 - p, b, *fourth(n, 1 - xbit, 1 - zbit))
        fwd[n].append(rc(src, src, core))

    def need(n):
        for cp in fwd[n]:
            cp.wait_recv()

    cp_x.wait()
    for cp in (v_c, v_y, v_d):
        cp.wait_recv()
    DQ = D // 4
    for row in (R_BQ, R_BV):
        vecf[row:row + 1, :] = jnp.concatenate([vecs[i, row:row + 1, 0:DQ] for i in range(4)], axis=1)
    for row in BY_BLK:
        vecf[row:row + 1, :] = jnp.concatenate([vecs[i, row:row + 1, 0:DH] for i in range(2)], axis=1)
    vecf[R_LANE:R_LANE + 1, :] = jnp.concatenate([vecs[2 * i, R_LANE:R_LANE + 1, 0:DH] for i in range(2)], axis=1)
    for t in range(FF // D):
        per = D * 4 // FF
        b1r[t] = jnp.concatenate([vecs[i, R_B1:R_B1 + 1, 0:FF // 4] for i in range(t * per, t * per + per)], axis=1)
    for pair in range(heads // 2):
        two = vecf[R_LANE:R_LANE + 1, pair * 128:pair * 128 + 128]
        hrow[2 * pair] = jnp.broadcast_to(two[:, 0:1], (1, 128))
        hrow[2 * pair + 1] = jnp.broadcast_to(two[:, 64:65], (1, 128))
    length = lengths[p]
    pos = lax.broadcasted_iota(jnp.int32, (L, 128), 0)
    for which in range(2):
        start = (b if which == 0 else 1 - b) * L
        biasb[which] = jnp.where(pos + start < length, 0.0, MASKED_SCORE)

    lane = lax.broadcasted_iota(jnp.int32, (1, 128), 1)

    def head_lanes(hh):
        return (lane < 64) if hh == 0 else (lane >= 64)

    def head_bias(head):
        return jnp.where(hrow[head] > 0.5, biasb[1], biasb[0])

    def project(h):
        cols = pl.ds(al(h * DH, 128), DH)
        swapped = vecf[R_LANE:R_LANE + 1, cols] > 0.5
        q[:, cols] = (nn(xo[...], gwq[:, cols]) + vecf[R_BQ:R_BQ + 1, cols]).astype(BF16) * jnp.asarray(0.125, BF16)
        k[:, cols] = jnp.where(swapped, nn(xx[...], gwk[:, cols]), nn(xo[...], gwk[:, cols])).astype(BF16)
        v[:, cols] = (jnp.where(swapped, nn(xx[...], gwv[:, cols]), nn(xo[...], gwv[:, cols]))
                      + vecf[R_BV:R_BV + 1, cols]).astype(BF16)

    def attend(h, j):
        cols = pl.ds(al(h * DH + j * 128, 128), 128)
        kp, vp = k[:, cols], v[:, cols]
        vT = vp.T
        tops = []
        for hh in range(2):
            head = h * (heads // 2) + 2 * j + hh
            km = jnp.where(head_lanes(hh), kp, jnp.zeros_like(kp))
            bias = head_bias(head)
            bias = jnp.concatenate([bias, bias], axis=1)
            parts = []
            for t in range(L // 256):
                s = nt(km, q[t * 256:(t + 1) * 256, cols]) + bias
                peak = jnp.max(s, axis=0, keepdims=True)
                e = jnp.exp(s - peak)
                total = jnp.sum(e, axis=0, keepdims=True)
                lse[head, :, t * 256:(t + 1) * 256] = peak + jnp.log(total)
                parts.append(nn(vT[hh * 64:(hh + 1) * 64, :], e.astype(BF16)) * (1.0 / total))
            tops.append(jnp.concatenate(parts, axis=1))
        c[:, cols] = jnp.concatenate(tops, axis=0).T.astype(BF16)

    for n in range(4):
        own[n].wait()
        to_core[n].wait_recv()
    x_c.wait_recv()
    project(p)
    svc_a(0)
    svc_a(1)

    def pair(h, j):
        def one(i, carry):
            attend(h, j)
            return carry

        lax.fori_loop(0, 1, one, 0)

    pair(p, 0)
    svc_a(2)
    svc_b(0)
    svc_b(1)
    pair(p, 1)
    svc_a(3)
    svc_b(2)
    svc_c(0)
    pair(p, 2)
    svc_c(1)
    svc_b(3)
    svc_a(4)
    svc_c(2)
    svc_c(3)
    for n in range(4):
        need(n)
    project(1 - p)
    pair(1 - p, 0)
    svc_a(5)
    svc_b(4)
    pair(1 - p, 1)
    svc_a(6)
    svc_b(5)
    svc_c(4)
    pair(1 - p, 2)

    acc[...] = nn(c[...], gwo[...])
    TR = 128

    def rows_of(i):
        return pl.ds(al(i * TR, TR), TR)

    def norm1(i, carry):
        r = rows_of(i)
        val = xo[r, :].astype(F32) + (acc[r, :] + vecf[R_BO:R_BO + 1, :])
        centre = val - jnp.mean(val, axis=1, keepdims=True)
        spread = jnp.mean(centre * centre, axis=1, keepdims=True)
        rs = lax.rsqrt(spread + EPSILON)
        xh = centre * rs
        xh1[r, :] = xh
        rs1[r, :] = jnp.broadcast_to(rs, (TR, 128))
        flow[r, :] = (xh * vecf[R_G1:R_G1 + 1, :] + vecf[R_S1:R_S1 + 1, :]).astype(BF16)
        return carry

    lax.fori_loop(0, L // TR, norm1, 0)
    svc_a(7)
    svc_b(6)
    svc_c(5)
    tA[...] = flow[...].T

    NT = FH // D

    def ff_tile(h, i, first):
        hid = pl.ds(al(h * FH + i * D, 128), D)
        wide[...] = nn(flow[...], gw1[:, hid])

        def gelu_rows(j, carry):
            r = pl.ds(al(j * 32, 32), 32)
            u = wide[r, :] + b1r[h * NT + i]
            uu = u * u
            th = jnp.tanh(GELU_C * u * (1.0 + 0.044715 * uu))
            half = 0.5 * (1.0 + th)
            act[r, hid] = (u * half).astype(BF16)
            slope = half + 0.5 * u * (1.0 - th * th) * (GELU_C * (1.0 + 3 * 0.044715 * uu))
            dact[r, hid] = slope.astype(BF16)
            return carry

        lax.fori_loop(0, L // 32, gelu_rows, 0)
        out = nn(act[:, hid], gw2[hid, :])
        if first:
            acc[...] = out
        else:
            acc[...] += out

    for n in range(4, NW):
        own[n].wait()
        to_core[n].wait_recv()
    ff_tile(p, 0, True)
    svc_b(7)
    svc_c(6)
    ff_tile(p, 1, False)
    svc_c(7)
    for i in range(NT):
        need(4 + 2 * i)
        need(5 + 2 * i)
        ff_tile(1 - p, i, False)

    cp_cot.wait()
    zero = jnp.zeros((1, D), F32)
    for r0 in range(gv.shape[0]):
        gv[r0:r0 + 1, :] = zero

    def colsum(x):
        return jnp.sum(x, axis=0, keepdims=True)

    def norm2(i, carry):
        dg, ds, db = carry
        r = rows_of(i)
        fo = xh1[r, :] * vecf[R_G1:R_G1 + 1, :] + vecf[R_S1:R_S1 + 1, :]
        val = fo + (acc[r, :] + vecf[R_B2:R_B2 + 1, :])
        centre = val - jnp.mean(val, axis=1, keepdims=True)
        spread = jnp.mean(centre * centre, axis=1, keepdims=True)
        rs = lax.rsqrt(spread + EPSILON)
        xh = centre * rs
        g2 = vecf[R_G2:R_G2 + 1, :]
        lob[r, :] = (xh * g2 + vecf[R_S2:R_S2 + 1, :]).astype(BF16)
        up = cotb[r, :].astype(F32)
        dxh = up * g2
        gin = rs * (dxh - jnp.mean(dxh, axis=1, keepdims=True) - xh * jnp.mean(dxh * xh, axis=1, keepdims=True))
        acc[r, :] = gin
        low = gin.astype(BF16)
        go[r, :] = low
        return dg + colsum(up * xh), ds + colsum(up), db + colsum(low.astype(F32))

    dg, ds, db = lax.fori_loop(0, L // TR, norm2, (zero, zero, zero))
    gv[R_G2:R_G2 + 1, :] = dg
    gv[R_S2:R_S2 + 1, :] = ds
    gv[R_B2:R_B2 + 1, :] = db
    lo_local = lc(lob, layer_out.at[p])
    lo_y = []

    def lo_send(parts):
        for i in parts:
            part = pl.ds(i * (L // 4), L // 4)
            lo_y.append(rc(lob.at[part], layer_out.at[p, part], ypeer))

    lo_send(range(LO_FIRST))

    tB[...] = go[...].T
    keep_rows = pl.ds(al(b * DH, 128), DH)
    send_rows = pl.ds(al((1 - b) * DH, 128), DH)

    table = unit_table(DH, FH, D)
    units = []
    n_res = sum(order[0] != "y" for _, _, order in table)
    landing, landing_res = landing[:len(landing) - n_res], landing[len(landing) - n_res:]
    for col, width, order in table:
        order = [axis for axis in order if axis == "y" or axis < dp_bits]
        bufs = [landing.pop(0) for _ in range(len(order) + max(dp_bits - 3, 0))]
        units.append({"at": slice(col, col + width), "order": order, "bufs": bufs, "next": 0, "r0": 0, "rows": DH,
                      "both": True, "core": [None, None], "copy": None, "path": []})
        units[-1]["res"] = bufs[0] if order[0] == "y" else landing_res.pop(0)

    def core_send(u, src, h_is_own):
        h = p if h_is_own else 1 - p
        units[u]["core"][h_is_own] = rc(src, rcore.at[h, :, units[u]["at"]], core)

    def add_block(h, r0, rows, at, src):
        step = 48 if rows % 48 == 0 else rows

        def one(i, carry):
            here = pl.ds(al(r0 + i * step, 16), step)
            gk[h, here, at] = (gk[h, here, at].astype(F32) + src(pl.ds(al(i * step, 16), step)).astype(F32)).astype(BF16)
            return carry

        lax.fori_loop(0, rows // step, one, 0)

    def start_stage(u, s):
        un = units[u]
        axis, buf, at = un["order"][s], un["bufs"][s], un["at"]
        if axis == "y":
            here = pl.ds(al(un["r0"], 16), un["rows"])
            un["copy"] = rc(gk.at[1 - p, here, at], buf.at[0], ypeer)
            un["both"] = False
            return
        rows = un["rows"] // 2
        away = pl.ds(al(un["r0"] + (1 - bit(axis)) * rows, 16), rows)
        src = gk.at[:, away, at] if un["both"] else gk.at[pl.ds(p, 1), away, at]
        un["copy"] = rc(src, buf, peer_of(axis))
        un["path"].append((axis, un["r0"], un["rows"]))
        un["r0"] = un["r0"] + bit(axis) * rows
        un["rows"] = rows

    def step(u):
        un = units[u]
        ev, n, at = un["next"], len(un["order"]), un["at"]
        un["next"] += 1
        if ev == 0:
            for own in (0, 1):
                un["core"][own].wait_recv()
                h = p if own else 1 - p
                add_block(h, 0, DH, at, lambda r, h=h: rcore[h, r, at])
            start_stage(u, 0)
            return
        un["copy"].wait_recv()
        if ev <= n:
            buf = un["bufs"][ev - 1]
            if un["both"]:
                for h in range(2):
                    add_block(h, un["r0"], un["rows"], at, lambda r, h=h: buf[h, r, :])
            else:
                add_block(p, un["r0"], un["rows"], at, lambda r: buf[0, r, :])
            if ev < n:
                start_stage(u, ev)
                return
            for t in range(3, dp_bits):
                buf = un["bufs"][n + t - 3]
                mine = gk.at[pl.ds(p, 1), pl.ds(al(un["r0"], 16), un["rows"]), at]
                cp = rc(mine, buf, peer_of(t))
                cp.wait_recv()
                cp.wait_send()
                waited.append(id(cp))
                add_block(p, un["r0"], un["rows"], at, lambda r: buf[0, r, :])
            here = pl.ds(al(un["r0"], 16), un["rows"])
            un["res"][0, here, :] = gk[p, here, at]
        if un["path"]:
            axis, r0, rows = un["path"].pop()
            mine = un["res"].at[0, pl.ds(al(un["r0"], 16), un["rows"])]
            un["copy"] = rc(mine, mine, peer_of(axis))
            un["r0"], un["rows"] = r0, rows
            return
        un["out"] = lc(un["res"].at[0], gk_out.at[:, at])

    def events(place):
        for u in EVENTS[place]:
            step(u)

    def weight_grad(leftT, right, send, own, col, width):
        h = p if own else 1 - p
        send[...] = nn(leftT[send_rows, :], right).astype(BF16)
        gk[h, :, col:col + width] = nn(leftT[keep_rows, :], right).astype(BF16)

    def ff_back(own, i):
        h = p if own else 1 - p
        hid = pl.ds(al(h * FH + i * D, 128), D)
        du = (nt(go[...], gw2[hid, :]) * dact[:, hid].astype(F32)).astype(BF16)
        gb1[h * NT + i] = colsum(du.astype(F32))
        dact[:, hid] = du
        acc[...] += nt(dact[:, hid], gw1[:, hid])
        for u, leftT, side in ((2 * i, tA, dact), (2 * i + 1, tB, act)):
            send = side.at[0:DH, hid]
            weight_grad(leftT, side[:, hid], send, own, table[u][0], D)
            core_send(u, send, own)

    for i in range(NT):
        for own in (0, 1):
            ff_back(own, i)
            events("ff%d%d" % (i, own))
    if LO_PLACE == "ff":
        lo_send(range(LO_FIRST, 4))
    for t in range(FF // D):
        gv[R_B1 + t:R_B1 + t + 1, :] = gb1[t]

    def norm1_back(i, carry):
        dg, ds, db = carry
        r = rows_of(i)
        up = acc[r, :]
        xh = xh1[r, :]
        dxh = up * vecf[R_G1:R_G1 + 1, :]
        gin = rs1[r, 0:1] * (dxh - jnp.mean(dxh, axis=1, keepdims=True) - xh * jnp.mean(dxh * xh, axis=1, keepdims=True))
        acc[r, :] = gin
        low = gin.astype(BF16)
        go[r, :] = low
        return dg + colsum(up * xh), ds + colsum(up), db + colsum(low.astype(F32))

    dg, ds, db = lax.fori_loop(0, L // TR, norm1_back, (zero, zero, zero))
    gv[R_G1:R_G1 + 1, :] = dg
    gv[R_S1:R_S1 + 1, :] = ds
    gv[R_BO:R_BO + 1, :] = db
    tB[...] = go[...].T
    UO = 2 * NT
    events("n1")
    if LO_PLACE == "n1":
        lo_send(range(LO_FIRST, 4))
    for u in range(UO):
        for cp in units[u]["core"]:
            cp.wait_send()
            waited.append(id(cp))
    dc[...] = nt(go[...], gwo[...]).astype(BF16)
    tail = 2 * FH

    def part(n, h):
        return dact.at[0:DH, pl.ds(al(D + (n % 3 * 2 + h) * DH, 128), DH)]

    for own in (0, 1):
        h = p if own else 1 - p
        weight_grad(tB, c[:, pl.ds(al(h * DH, 128), DH)], part(0, h), own, tail, DH)
        core_send(UO, part(0, h), own)
    events("wo")
    tA[...] = xo[...].T
    tB[...] = xx[...].T

    def attend_back(j, carry):
        cols = pl.ds(al(j * 128, 128), 128)
        kp, vp, qp, dcp = k[:, cols], v[:, cols], q[:, cols], dc[:, cols]
        kT = kp.T
        dkv = [jnp.zeros((L, 128), F32), jnp.zeros((L, 128), F32)]
        tops = []
        for hh in range(2):
            head = 2 * j + hh
            mine = head_lanes(hh)
            none = jnp.zeros_like(kp)
            km, vm = jnp.where(mine, kp, none), jnp.where(mine, vp, none)
            qm, dcm = jnp.where(mine, qp, none), jnp.where(mine, dcp, none)
            bias = head_bias(head)
            bias = jnp.concatenate([bias, bias], axis=1)
            parts = []
            for t in range(L // 256):
                ts = slice(t * 256, (t + 1) * 256)
                prob = jnp.exp(nt(km, qp[ts]) + bias - lse[head, :, ts])
                dprob = nt(vm, dcp[ts])
                delta = jnp.sum(prob * dprob, axis=0, keepdims=True)
                dscore = (prob * (dprob - delta)).astype(BF16)
                dkv[1] += nn(prob.astype(BF16), dcm[ts])
                dkv[0] += nn(dscore, qm[ts])
                parts.append(nn(kT[hh * 64:(hh + 1) * 64, :], dscore))
            tops.append(jnp.concatenate(parts, axis=1))
        dq[:, cols] = (jnp.concatenate(tops, axis=0).T * 0.125).astype(BF16)
        dk[:, cols] = dkv[0].astype(BF16)
        dv[:, cols] = dkv[1].astype(BF16)
        return carry

    for i in range(3):
        lax.fori_loop(i * NP * 2 // 3, (i + 1) * NP * 2 // 3, attend_back, 0)
        events("ab%d" % i)
    if LO_PLACE == "ab":
        lo_send(range(LO_FIRST, 4))
    gv[R_BQ:R_BQ + 1, :] = colsum(dq[...].astype(F32))
    gv[R_BV:R_BV + 1, :] = colsum(dv[...].astype(F32))

    swapped = vecf[R_LANE:R_LANE + 1, :] > 0.5
    none = jnp.zeros((L, D), BF16)
    dc[...] = jnp.where(swapped, dk[...], none)
    flow[...] = jnp.where(swapped, dv[...], none)
    dk[...] = jnp.where(swapped, none, dk[...])
    dv[...] = jnp.where(swapped, none, dv[...])
    backs[...] = (nt(dc[...], gwk[...]) + nt(flow[...], gwv[...])).astype(BF16)
    back_c = rc(backs, backr, core)
    for n, (a, x) in enumerate(((dq, None), (dk, dc), (dv, flow))):
        u = UO + 1 + n
        for own in (0, 1):
            h = p if own else 1 - p
            hs = pl.ds(al(h * DH, 128), DH)
            if n == 2:
                units[UO]["core"][own].wait_send()
                waited.append(id(units[UO]["core"][own]))
            send = part(1 + n, h)
            for dst, rows in ((send, send_rows), (gk.at[h, :, table[u][0]:table[u][0] + DH], keep_rows)):
                val = nn(tA[rows, :], a[:, hs])
                if x is not None:
                    val = val + nn(tB[rows, :], x[:, hs])
                dst[...] = val.astype(BF16)
            core_send(u, send, own)
        events("q%d" % (5 + n))
    vec_peers = [core, ypeer] + [peer_of(t) for t in range(dp_bits)]
    vstate = {"s": 0, "cp": None}
    gvr[0, 0] = gv[...]

    def vec_step():
        s = vstate["s"]
        if s > 0:
            vstate["cp"].wait_recv()
            total = gvr[s - 1, 0] + gvr[s - 1, 1]
            if s == len(vec_peers):
                gv[...] = total
                return
            gvr[s, 0] = total
        vstate["cp"] = rc(gvr.at[s, 0], gvr.at[s, 1], vec_peers[s])
        vstate["s"] = s + 1

    vec_step()
    acc[...] += nt(dq[...], gwq[...]) + nt(dk[...], gwk[...]) + nt(dv[...], gwv[...])
    events("acc")
    lo_local.wait()
    back_c.wait_recv()
    for r0 in range(0, L, TR):
        acc[r0:r0 + TR, :] += backr[r0:r0 + TR, :].astype(F32)
    xo[...] = acc[...].astype(BF16)
    gt_local = lc(xo, grad_tokens.at[p])
    gt_y = rc(xo, grad_tokens.at[p], ypeer)
    if LO_PLACE == "end":
        lo_send(range(LO_FIRST, 4))
    for i, u in enumerate(EVENTS["drain"]):
        step(u)
        if i % 4 == 3 and i // 4 < len(vec_peers):
            vec_step()
    for _ in range(len(vec_peers) - len(EVENTS["drain"]) // 4):
        vec_step()
    for un in units:
        un["out"].wait()
    gt_local.wait()
    gt_y.wait_recv()
    for cp in lo_y:
        cp.wait_recv()
    for cp in sent:
        if id(cp) not in waited:
            cp.wait_send()


def finish_kernel(
    gk, gv, g_wq, g_bq, g_wk, g_wv, g_bv, g_wo, g_bo, g_g1, g_s1, g_w1, g_b1, g_w2, g_b2, g_g2, g_s2
):
    p, b = lax.axis_index("perm"), lax.axis_index("blk")
    D = gv.shape[1]
    DH, FH = D // 2, g_w1.shape[1]
    tail = 2 * FH
    g_w1[...] = gk[:, 0:FH].astype(F32)
    for i in range(FH // DH):
        g_w2[i * DH:(i + 1) * DH, :] = gk[:, FH + i * DH:FH + (i + 1) * DH].astype(F32).T
    g_wo[...] = gk[:, tail:tail + DH].astype(F32).T
    for n, ref in enumerate((g_wq, g_wk, g_wv)):
        ref[...] = gk[:, tail + (n + 1) * DH:tail + (n + 2) * DH].astype(F32)
    for row, ref in ((R_BO, g_bo), (R_G1, g_g1), (R_S1, g_s1), (R_B2, g_b2), (R_G2, g_g2), (R_S2, g_s2)):
        ref[...] = jnp.where(b == 0, gv[row:row + 1, 0:DH], gv[row:row + 1, DH:D])
    for row, ref in ((R_BQ, g_bq), (R_BV, g_bv)):
        n = D // 4
        left = jnp.where(b == 0, gv[row:row + 1, 0:n], gv[row:row + 1, n:2 * n])
        right = jnp.where(b == 0, gv[row:row + 1, 2 * n:3 * n], gv[row:row + 1, 3 * n:D])
        ref[...] = jnp.where(p == 0, left, right)
    left = jnp.where(b == 0, gv[R_B1:R_B1 + 1, :], gv[R_B1 + 1:R_B1 + 2, :])
    right = jnp.where(b == 0, gv[R_B1 + 2:R_B1 + 3, :], gv[R_B1 + 3:R_B1 + 4, :])
    g_b1[...] = jnp.where(p == 0, left, right)


def per_device(
    tokens, lengths, head_route, w_query, b_query, w_key, w_value, b_value, w_out, b_out,
    first_gain, first_shift, w_inner, b_inner, w_outer, b_outer, second_gain, second_shift, cotangent,
):
    L, D = tokens.shape[1:]
    FF = w_inner.shape[1] * 2
    heads = head_route.shape[0] * 2
    hd = D // heads

    def padded(vector):
        return jnp.pad(vector.astype(F32), (0, D - vector.shape[0]))

    none = jnp.zeros((D,), F32)
    rows = [b_query, b_value, b_out, first_gain, first_shift, b_outer, second_gain, second_shift, b_inner]
    rows = [padded(row) for row in rows] + [none] * 3
    rows += [padded(jnp.repeat(head_route, hd))] + [none] * 3
    vec = jnp.concatenate(rows).reshape(16, D)
    bits = (lax.axis_size("dp") - 1).bit_length()

    half = FF + 4 * (D // 2)
    any_ = pl.BlockSpec(memory_space=pl.ANY)
    vm = pl.BlockSpec(memory_space=pltpu.VMEM)
    V = pltpu.VMEM
    layer_out, grad_tokens, reduced, vectors = pl.pallas_call(
        functools.partial(layer_kernel, heads, lax.axis_size("dp")),
        out_shape=(
            jax.ShapeDtypeStruct(tokens.shape, BF16),
            jax.ShapeDtypeStruct(tokens.shape, BF16),
            jax.ShapeDtypeStruct((D // 2, half), BF16),
            jax.ShapeDtypeStruct((16, D), F32),
        ),
        in_specs=[any_, any_, pl.BlockSpec(memory_space=pltpu.SMEM), vm] + [any_] * 6,
        out_specs=(any_, any_, any_, vm),
        scratch_shapes=[
            V((L, D), BF16), V((L, D), BF16), V((L, D), BF16),
            V((D, D), BF16), V((D, D), BF16), V((D, D), BF16), V((D, D), BF16), V((D, FF), BF16), V((FF, D), BF16),
            V((4, 16, D), F32), V((16, D), F32), V((2, L, 128), F32),
            V((L, D), BF16), V((L, D), BF16), V((L, D), BF16), V((L, D), BF16),
            V((L, D), BF16), V((L, D), F32), V((L, 128), F32), V((16, 1, L), F32),
            V((L, FF), BF16), V((L, FF), BF16), V((L, D), F32), V((L, D), BF16),
            V((D, L), BF16), V((D, L), BF16), V((L, D), BF16),
            V((L, D), F32), V((L, D), BF16),
            V((16, 1, 128), F32), V((FF // D, 1, D), F32), V((FF // D, 1, D), F32),
            V((2, D // 2, half), BF16), V((2, D // 2, half), BF16),
            V((2 + bits, 2, 16, D), F32),
        ] + [V(shape, BF16) for shape in stage_shapes(unit_table(D // 2, FF // 2, D), D // 2, bits)] + [
            pltpu.SemaphoreType.DMA((32,)),
            pltpu.SemaphoreType.DMA((256,)),
            pltpu.SemaphoreType.DMA((256,)),
        ],
        compiler_params=pltpu.CompilerParams(collective_id=0, has_side_effects=True, vmem_limit_bytes=62 * 2**20),
        name="layer",
    )(tokens, cotangent, lengths, vec, w_query, w_key, w_value, w_out, w_inner, w_outer)

    DH, FH = D // 2, FF // 2
    shapes = [(DH, DH), (1, D // 4), (DH, DH), (DH, DH), (1, D // 4), (DH, DH), (1, DH), (1, DH), (1, DH), (DH, FH),
              (1, FF // 4), (FH, DH), (1, DH), (1, DH), (1, DH)]
    grads = pl.pallas_call(
        finish_kernel,
        out_shape=[jax.ShapeDtypeStruct(shape, F32) for shape in shapes],
        in_specs=[vm, vm],
        out_specs=[vm] * len(shapes),
        compiler_params=pltpu.CompilerParams(vmem_limit_bytes=48 * 2**20),
        name="finish",
    )(reduced, vectors)
    grads = [g.reshape(-1) if g.shape[0] == 1 else g for g in grads]
    return (layer_out, grad_tokens, *grads)


def solution(mesh):
    placed = (
        P("dp", "blk", None), P("dp"), P("perm"), P("blk", "perm"), P(("perm", "blk")), P("blk", "perm"),
        P("blk", "perm"), P(("perm", "blk")), P("perm", "blk"), P("blk"), P("blk"), P("blk"), P("blk", "perm"),
        P(("perm", "blk")), P("perm", "blk"), P("blk"), P("blk"), P("blk"), P("dp", "blk", None),
    )
    outs = (
        P("dp", "blk", None), P("dp", "blk", None), P("blk", "perm"), P(("perm", "blk")), P("blk", "perm"),
        P("blk", "perm"), P(("perm", "blk")), P("perm", "blk"), P("blk"), P("blk"), P("blk"), P("blk", "perm"),
        P(("perm", "blk")), P("perm", "blk"), P("blk"), P("blk"), P("blk"),
    )
    return jax.shard_map(per_device, mesh=mesh, in_specs=placed, out_specs=outs, check_vma=False)
```

```python
import functools
import math

import jax
import jax.numpy as jnp
from jax import lax
from jax.experimental import pallas as pl
from jax.experimental.pallas import tpu as pltpu
from jax.sharding import PartitionSpec as P

EPSILON = 1e-05
MASKED_SCORE = -1e30
MESH = pl.DeviceIdType.MESH
F32 = jnp.float32
BF16 = jnp.bfloat16
GELU_C = math.sqrt(2.0 / math.pi)


def nn(left, right):
    return lax.dot_general(left, right, (((1,), (0,)), ((), ())), preferred_element_type=F32)


def nt(left, right):
    return lax.dot_general(left, right, (((1,), (1,)), ((), ())), preferred_element_type=F32)


def al(value, multiple):
    return pl.multiple_of(value, multiple)


R_BQ, R_BV, R_BO, R_G1, R_S1, R_B2, R_G2, R_S2, R_B1, R_LANE = 0, 1, 2, 3, 4, 5, 6, 7, 8, 12
BY_BLK = (R_BO, R_G1, R_S1, R_B2, R_G2, R_S2)

ORDERS = (
    (0, 1, "y", 2),
    ("y", 0, 1, 2),
    (1, 0, "y", 2),
    ("y", 1, 0, 2),
    (0, 1, "y", 2),
    (0, "y", 1, 2),
    ("y", 0, 1, 2),
    ("y", 0, 1, 2),
)
EVENTS = {
        "ff00": (),
        "ff01": (),
        "ff10": (0, 1),
        "ff11": (),
        "n1": (),
        "wo": (2, 3, 4),
        "ab0": (0, 1),
        "ab1": (4,),
        "ab2": (2,),
        "q5": (1, 0, 3),
        "q6": (4, 5),
        "q7": (1, 2, 6, 4, 0),
        "acc": (7, 2, 3, 5, 1),
        "drain": (4, 0, 6, 3, 2, 1, 6, 4, 7, 0, 1, 5, 6, 7, 3, 4, 2, 0, 5, 6, 1, 7, 3, 4, 5, 6, 2, 7, 5, 6, 0, 2, 7,
        3, 5, 6, 7, 5, 7, 3),
}
GATHER = {
    "project0": (("a", 0), ("a", 1),),
    "own0": (("a", 2),),
    "own1": (("a", 3), ("b", 0),),
    "own2": (("b", 1),),
    "wait": (("b", 2), ("a", 4), ("b", 3), ("c", 0), ("c", 1), ("c", 2), ("a", 5),),
    "project1": (),
    "other0": (("b", 4), ("c", 3),),
    "other1": (("a", 6), ("b", 5),),
    "other2": (("c", 4),),
    "norm": (("a", 7),),
    "ff_own0": (("b", 6), ("c", 5),),
    "ff_own1": (("b", 7),),
    "ff_other0": (),
    "ff_other1": (("c", 6), ("c", 7),),
}
LO_FIRST, LO_PLACE = 2, "end"


def unit_table(DH, FH, D):
    tail = 2 * FH
    table = []
    for i in range(FH // D):
        table += [(i * D, D), (FH + i * D, D)]
    table += [(tail + i * DH, DH) for i in range(4)]
    return [(col, width, order) for (col, width), order in zip(table, ORDERS)]


def stage_shapes(table, DH, bits):
    shapes = []
    for col, width, order in table:
        rows, halves = DH, 2
        for axis in order:
            if axis == "y":
                halves = 1
            elif axis < bits:
                rows //= 2
            else:
                continue
            shapes.append((halves, rows, width))
        for _ in range(bits - 3):
            shapes.append((1, rows, width))
    shapes += [(1, DH, width) for _, width, order in table if order[0] != "y"]
    return shapes


def layer_kernel(
    heads, dp_size,
    tokens, cot, lengths, route, wq, wk, wv, wo, w1, w2, *rest,
):
    vectors, (layer_out, grad_tokens, gk_out, gv), rest = rest[:9], rest[9:13], rest[13:]
    (xo, xx, cotb, gwq, gwk, gwv, gwo, gw1, gw2, vecs, vecf, biasb,
     q, k, v, c, flow, xh1, rs1, lse, act, dact, acc, go, tA, tB, lob, wide, backr, hrow, b1r, gb1,
     gk, rcore, gvr), rest = rest[:35], rest[35:]
    sem_l, sem_s, sem_r = rest[-3:]
    landing, landing_res = list(rest[:-3]), []
    d, p, b = lax.axis_index("dp"), lax.axis_index("perm"), lax.axis_index("blk")
    D = xo.shape[1]
    L = xo.shape[0]
    FF = gw2.shape[0]
    DH, FH = D // 2, FF // 2
    NP = heads // 4
    xbit = lax.rem(d, 2)
    dq, dk, dv, dc = (act.at[:, i * D:(i + 1) * D] for i in range(4))
    backs = dact.at[:, 0:D]
    core, ypeer, diag = (d, p, 1 - b), (d, 1 - p, b), (d, 1 - p, 1 - b)
    dp_bits = (dp_size - 1).bit_length()

    def bit(t):
        return lax.rem(lax.div(d, 2**t), 2)

    def peer_of(t):
        return (d + 2**t - 2 ** (t + 1) * bit(t), p, b)

    xpeer = peer_of(0)

    bar = pltpu.get_barrier_semaphore()
    peers = (core, ypeer, diag) + tuple(peer_of(t) for t in range(dp_bits))
    for peer in peers:
        pl.semaphore_signal(bar, 1, device_id=peer, device_id_type=MESH)
    pl.semaphore_wait(bar, len(peers))

    count = [0]
    sent = []
    waited = []

    class Copy:
        def __init__(self, src, dst, peer):
            self.index, self.src, self.dst, self.peer = count[0], src, dst, peer
            count[0] += 1
            self.make().start()
            sent.append(self)

        def make(self):
            src = self.src() if callable(self.src) else self.src
            dst = self.dst() if callable(self.dst) else self.dst
            return pltpu.make_async_remote_copy(
                src_ref=src, dst_ref=dst, send_sem=sem_s.at[self.index], recv_sem=sem_r.at[self.index],
                device_id=self.peer, device_id_type=MESH)

        def wait_recv(self):
            self.make().wait_recv()

        def wait_send(self):
            self.make().wait_send()

    rc = Copy

    def same(ref, peer):
        return rc(ref, ref, peer)

    nl = [0]

    def lc(src, dst):
        i = nl[0]
        nl[0] += 1
        cp = pltpu.make_async_copy(src, dst, sem_l.at[i])
        cp.start()
        return cp

    pieces = [(wq, gwq, True, 0, wq.shape[1]), (wk, gwk, True, 0, wk.shape[1]), (wv, gwv, True, 0, wv.shape[1]),
              (wo, gwo, False, 0, wo.shape[0])]
    for i in range(FH // D):
        pieces += [(w1, gw1, True, i * D, D), (w2, gw2, False, i * D, D)]
    NW = len(pieces)

    def extent(n):
        shard, _, by_blk, _, size = pieces[n]
        return (shard.shape[0], size) if by_blk else (size, shard.shape[1])

    def span(n, pp, bb, r0, rows):
        shard, full, by_blk, first, size = pieces[n]
        sr, sc = shard.shape
        if by_blk:
            return full.at[pl.ds(al(bb * sr + r0, 16), rows), pl.ds(al(pp * sc + first, 128), size)]
        return full.at[pl.ds(al(pp * sr + first + r0, 16), rows), pl.ds(al(bb * sc, 128), sc)]

    def shard_rows(n, r0, rows):
        shard, _, by_blk, first, size = pieces[n]
        if by_blk:
            return shard.at[pl.ds(al(r0, 16), rows), first:first + size]
        return shard.at[pl.ds(al(first + r0, 16), rows), :]

    zbit = bit(1)
    nxbit, nzbit = 1 - xbit, 1 - zbit
    zpeer = peer_of(1)

    def fourth(n, xb, zb):
        rows = extent(n)[0] // 4
        return (2 * xb + zb) * rows, rows

    def third(n, xb, zb, i):
        r0, rows = fourth(n, xb, zb)
        return r0 + i * (rows // 3), rows // 3

    quarter = p * 2 + b
    for row, ref in enumerate(vectors):
        vecs[quarter, row:row + 1, 0:ref.shape[0]] = ref[...].astype(F32).reshape(1, ref.shape[0])
    at_lane = lax.broadcasted_iota(jnp.int32, (1, DH), 1)
    routes = jnp.zeros((1, DH), F32)
    for i in range(heads // 2):
        here = (at_lane >= i * 64) & (at_lane < (i + 1) * 64)
        routes = jnp.where(here, route[i].astype(F32), routes)
    vecs[quarter, R_LANE:R_LANE + 1, 0:DH] = routes
    cp_x = lc(tokens.at[p], xo)
    own = [lc(shard_rows(n, 0, extent(n)[0]), span(n, p, b, 0, extent(n)[0])) for n in range(NW)]
    cp_cot = lc(cot.at[p], cotb)
    v_c = same(vecs.at[quarter], core)
    v_y = same(vecs.at[quarter], ypeer)
    v_d = same(vecs.at[quarter], diag)
    to_core, to_y, to_y3 = [], [], []
    for n in range(NW):
        to_core.append(rc(shard_rows(n, 0, extent(n)[0]), span(n, p, b, 0, extent(n)[0]), core))
        if n == 2:
            x_c = rc(tokens.at[p], xx, core)
        r = fourth(n, xbit, zbit)
        to_y.append(rc(shard_rows(n, *r), span(n, p, b, *r), ypeer))
        r = third(n, 1 - xbit, 1 - zbit, 0)
        to_y3.append(rc(shard_rows(n, *r), span(n, p, b, *r), ypeer))
    to_x, to_z, to_x3, to_z3 = ([None] * NW for _ in range(4))
    fwd = [[] for _ in range(NW)]

    def passed(n, part, *args):
        return lambda: span(n, 1 - p, b, *part(n, *args))

    def svc_a(n):
        to_y[n].wait_recv()
        src = passed(n, fourth, xbit, zbit)
        to_x[n] = same(src, xpeer)
        to_z[n] = same(src, zpeer)
        fwd[n].append(same(src, core))

    def svc_b(n):
        to_x[n].wait_recv()
        to_z3[n] = same(passed(n, third, nxbit, zbit, 2), zpeer)
        to_z[n].wait_recv()
        to_x3[n] = same(passed(n, third, xbit, nzbit, 1), xpeer)
        fwd[n].append(same(passed(n, fourth, nxbit, zbit), core))
        fwd[n].append(same(passed(n, fourth, xbit, nzbit), core))

    def svc_c(n):
        for cp in (to_y3[n], to_x3[n], to_z3[n]):
            cp.wait_recv()
        fwd[n].append(same(passed(n, fourth, nxbit, nzbit), core))

    def need(n):
        for cp in fwd[n]:
            cp.wait_recv()

    cp_x.wait()
    for cp in (v_c, v_y, v_d):
        cp.wait_recv()
    DQ = D // 4
    for row in (R_BQ, R_BV):
        vecf[row:row + 1, :] = jnp.concatenate([vecs[i, row:row + 1, 0:DQ] for i in range(4)], axis=1)
    for row in BY_BLK:
        vecf[row:row + 1, :] = jnp.concatenate([vecs[i, row:row + 1, 0:DH] for i in range(2)], axis=1)
    vecf[R_LANE:R_LANE + 1, :] = jnp.concatenate([vecs[2 * i, R_LANE:R_LANE + 1, 0:DH] for i in range(2)], axis=1)
    for t in range(FF // D):
        per = D * 4 // FF
        b1r[t] = jnp.concatenate([vecs[i, R_B1:R_B1 + 1, 0:FF // 4] for i in range(t * per, t * per + per)], axis=1)
    for pair in range(heads // 2):
        two = vecf[R_LANE:R_LANE + 1, pair * 128:pair * 128 + 128]
        hrow[2 * pair] = jnp.broadcast_to(two[:, 0:1], (1, 128))
        hrow[2 * pair + 1] = jnp.broadcast_to(two[:, 64:65], (1, 128))
    length = lengths[p]
    pos = lax.broadcasted_iota(jnp.int32, (L, 128), 0)
    for which in range(2):
        start = (b if which == 0 else 1 - b) * L
        biasb[which] = jnp.where(pos + start < length, 0.0, MASKED_SCORE)

    lane = lax.broadcasted_iota(jnp.int32, (1, 128), 1)

    def head_lanes(hh):
        return (lane < 64) if hh == 0 else (lane >= 64)

    def head_bias(head):
        return jnp.where(hrow[head] > 0.5, biasb[1], biasb[0])

    def project(h):
        cols = pl.ds(al(h * DH, 128), DH)
        swapped = vecf[R_LANE:R_LANE + 1, cols] > 0.5
        q[:, cols] = (nn(xo[...], gwq[:, cols]) + vecf[R_BQ:R_BQ + 1, cols]).astype(BF16) * jnp.asarray(0.125, BF16)
        k[:, cols] = jnp.where(swapped, nn(xx[...], gwk[:, cols]), nn(xo[...], gwk[:, cols])).astype(BF16)
        v[:, cols] = (jnp.where(swapped, nn(xx[...], gwv[:, cols]), nn(xo[...], gwv[:, cols]))
                      + vecf[R_BV:R_BV + 1, cols]).astype(BF16)

    def attend(h, j):
        cols = pl.ds(al(h * DH + j * 128, 128), 128)
        kp, vp = k[:, cols], v[:, cols]
        vT = vp.T
        tops = []
        for hh in range(2):
            head = h * (heads // 2) + 2 * j + hh
            km = jnp.where(head_lanes(hh), kp, jnp.zeros_like(kp))
            bias = head_bias(head)
            bias = jnp.concatenate([bias, bias], axis=1)
            parts = []
            for t in range(L // 256):
                s = nt(km, q[t * 256:(t + 1) * 256, cols]) + bias
                peak = jnp.max(s, axis=0, keepdims=True)
                e = jnp.exp(s - peak)
                total = jnp.sum(e, axis=0, keepdims=True)
                lse[head, :, t * 256:(t + 1) * 256] = peak + jnp.log(total)
                parts.append(nn(vT[hh * 64:(hh + 1) * 64, :], e.astype(BF16)) * (1.0 / total))
            tops.append(jnp.concatenate(parts, axis=1))
        c[:, cols] = jnp.concatenate(tops, axis=0).T.astype(BF16)

    def gather(place):
        for kind, n in GATHER[place]:
            {"a": svc_a, "b": svc_b, "c": svc_c}[kind](n)

    def pairs(h, name):
        def one(j, carry):
            attend(h, j)
            for i in range(NP):
                pl.when(j == i)(functools.partial(gather, "%s%d" % (name, i)))
            return carry

        lax.fori_loop(0, NP, one, 0)

    for n in range(3):
        own[n].wait()
        to_core[n].wait_recv()
    x_c.wait_recv()
    project(p)
    gather("project0")
    pairs(p, "own")
    gather("wait")
    own[3].wait()
    to_core[3].wait_recv()
    for n in range(3):
        need(n)
    project(1 - p)
    gather("project1")
    pairs(1 - p, "other")
    need(3)

    acc[...] = nn(c[...], gwo[...])
    TR = 128

    def rows_of(i):
        return pl.ds(al(i * TR, TR), TR)

    def norm1(i, carry):
        r = rows_of(i)
        val = xo[r, :].astype(F32) + (acc[r, :] + vecf[R_BO:R_BO + 1, :])
        centre = val - jnp.mean(val, axis=1, keepdims=True)
        spread = jnp.mean(centre * centre, axis=1, keepdims=True)
        rs = lax.rsqrt(spread + EPSILON)
        xh = centre * rs
        xh1[r, :] = xh
        rs1[r, :] = jnp.broadcast_to(rs, (TR, 128))
        flow[r, :] = (xh * vecf[R_G1:R_G1 + 1, :] + vecf[R_S1:R_S1 + 1, :]).astype(BF16)
        return carry

    lax.fori_loop(0, L // TR, norm1, 0)
    gather("norm")
    tA[...] = flow[...].T

    NT = FH // D

    def ff_tile(h, i, first):
        hid = pl.ds(al(h * FH + i * D, 128), D)
        wide[...] = nn(flow[...], gw1[:, hid])

        def gelu_rows(j, carry):
            r = pl.ds(al(j * 32, 32), 32)
            u = wide[r, :] + b1r[h * NT + i]
            uu = u * u
            th = jnp.tanh(GELU_C * u * (1.0 + 0.044715 * uu))
            half = 0.5 * (1.0 + th)
            act[r, hid] = (u * half).astype(BF16)
            slope = half + 0.5 * u * (1.0 - th * th) * (GELU_C * (1.0 + 3 * 0.044715 * uu))
            dact[r, hid] = slope.astype(BF16)
            return carry

        lax.fori_loop(0, L // 32, gelu_rows, 0)
        out = nn(act[:, hid], gw2[hid, :])
        if first:
            acc[...] = out
        else:
            acc[...] += out

    for n in range(4, NW):
        own[n].wait()
        to_core[n].wait_recv()
    for i in range(NT):
        ff_tile(p, i, i == 0)
        gather("ff_own%d" % i)
    for i in range(NT):
        gather("ff_other%d" % i)
        need(4 + 2 * i)
        need(5 + 2 * i)
        ff_tile(1 - p, i, False)

    cp_cot.wait()
    zero = jnp.zeros((1, D), F32)
    for r0 in range(gv.shape[0]):
        gv[r0:r0 + 1, :] = zero

    def colsum(x):
        return jnp.sum(x, axis=0, keepdims=True)

    def norm2(i, carry):
        dg, ds, db = carry
        r = rows_of(i)
        fo = xh1[r, :] * vecf[R_G1:R_G1 + 1, :] + vecf[R_S1:R_S1 + 1, :]
        val = fo + (acc[r, :] + vecf[R_B2:R_B2 + 1, :])
        centre = val - jnp.mean(val, axis=1, keepdims=True)
        spread = jnp.mean(centre * centre, axis=1, keepdims=True)
        rs = lax.rsqrt(spread + EPSILON)
        xh = centre * rs
        g2 = vecf[R_G2:R_G2 + 1, :]
        lob[r, :] = (xh * g2 + vecf[R_S2:R_S2 + 1, :]).astype(BF16)
        up = cotb[r, :].astype(F32)
        dxh = up * g2
        gin = rs * (dxh - jnp.mean(dxh, axis=1, keepdims=True) - xh * jnp.mean(dxh * xh, axis=1, keepdims=True))
        acc[r, :] = gin
        low = gin.astype(BF16)
        go[r, :] = low
        return dg + colsum(up * xh), ds + colsum(up), db + colsum(low.astype(F32))

    dg, ds, db = lax.fori_loop(0, L // TR, norm2, (zero, zero, zero))
    gv[R_G2:R_G2 + 1, :] = dg
    gv[R_S2:R_S2 + 1, :] = ds
    gv[R_B2:R_B2 + 1, :] = db
    lo_local = lc(lob, layer_out.at[p])
    lo_y = []

    def lo_send(parts):
        for i in parts:
            part = pl.ds(i * (L // 4), L // 4)
            lo_y.append(rc(lob.at[part], layer_out.at[p, part], ypeer))

    lo_send(range(LO_FIRST))

    tB[...] = go[...].T
    keep_rows = pl.ds(al(b * DH, 128), DH)
    send_rows = pl.ds(al((1 - b) * DH, 128), DH)

    table = unit_table(DH, FH, D)
    units = []
    n_res = sum(order[0] != "y" for _, _, order in table)
    landing, landing_res = landing[:len(landing) - n_res], landing[len(landing) - n_res:]
    for col, width, order in table:
        order = [axis for axis in order if axis == "y" or axis < dp_bits]
        bufs = [landing.pop(0) for _ in range(len(order) + max(dp_bits - 3, 0))]
        units.append({"at": slice(col, col + width), "order": order, "bufs": bufs, "next": 0, "r0": 0, "rows": DH,
                      "both": True, "core": [None, None], "copy": None, "path": []})
        units[-1]["res"] = bufs[0] if order[0] == "y" else landing_res.pop(0)

    def core_send(u, src, h_is_own):
        h = p if h_is_own else 1 - p
        units[u]["core"][h_is_own] = rc(src, rcore.at[h, :, units[u]["at"]], core)

    def add_block(h, r0, rows, at, src):
        step = 48 if rows % 48 == 0 else rows

        def one(i, carry):
            here = pl.ds(al(r0 + i * step, 16), step)
            gk[h, here, at] = (gk[h, here, at].astype(F32) + src(pl.ds(al(i * step, 16), step)).astype(F32)).astype(BF16)
            return carry

        lax.fori_loop(0, rows // step, one, 0)

    def start_stage(u, s):
        un = units[u]
        axis, buf, at = un["order"][s], un["bufs"][s], un["at"]
        if axis == "y":
            here = pl.ds(al(un["r0"], 16), un["rows"])
            un["copy"] = rc(gk.at[1 - p, here, at], buf.at[0], ypeer)
            un["both"] = False
            return
        rows = un["rows"] // 2
        away = pl.ds(al(un["r0"] + (1 - bit(axis)) * rows, 16), rows)
        src = gk.at[:, away, at] if un["both"] else gk.at[pl.ds(p, 1), away, at]
        un["copy"] = rc(src, buf, peer_of(axis))
        un["path"].append((axis, un["r0"], un["rows"]))
        un["r0"] = un["r0"] + bit(axis) * rows
        un["rows"] = rows

    def step(u):
        un = units[u]
        ev, n, at = un["next"], len(un["order"]), un["at"]
        un["next"] += 1
        if ev == 0:
            for own in (0, 1):
                un["core"][own].wait_recv()
                h = p if own else 1 - p
                add_block(h, 0, DH, at, lambda r, h=h: rcore[h, r, at])
            start_stage(u, 0)
            return
        un["copy"].wait_recv()
        if ev <= n:
            buf = un["bufs"][ev - 1]
            if un["both"]:
                for h in range(2):
                    add_block(h, un["r0"], un["rows"], at, lambda r, h=h: buf[h, r, :])
            else:
                add_block(p, un["r0"], un["rows"], at, lambda r: buf[0, r, :])
            if ev < n:
                start_stage(u, ev)
                return
            for t in range(3, dp_bits):
                buf = un["bufs"][n + t - 3]
                mine = gk.at[pl.ds(p, 1), pl.ds(al(un["r0"], 16), un["rows"]), at]
                cp = rc(mine, buf, peer_of(t))
                cp.wait_recv()
                cp.wait_send()
                waited.append(id(cp))
                add_block(p, un["r0"], un["rows"], at, lambda r: buf[0, r, :])
            here = pl.ds(al(un["r0"], 16), un["rows"])
            un["res"][0, here, :] = gk[p, here, at]
        if un["path"]:
            axis, r0, rows = un["path"].pop()
            mine = un["res"].at[0, pl.ds(al(un["r0"], 16), un["rows"])]
            un["copy"] = rc(mine, mine, peer_of(axis))
            un["r0"], un["rows"] = r0, rows
            return
        un["out"] = lc(un["res"].at[0], gk_out.at[:, at])

    def events(place):
        for u in EVENTS[place]:
            step(u)

    def weight_grad(leftT, right, send, own, col, width):
        h = p if own else 1 - p
        send[...] = nn(leftT[send_rows, :], right).astype(BF16)
        gk[h, :, col:col + width] = nn(leftT[keep_rows, :], right).astype(BF16)

    def ff_back(own, i):
        h = p if own else 1 - p
        hid = pl.ds(al(h * FH + i * D, 128), D)
        du = (nt(go[...], gw2[hid, :]) * dact[:, hid].astype(F32)).astype(BF16)
        gb1[h * NT + i] = colsum(du.astype(F32))
        dact[:, hid] = du
        acc[...] += nt(dact[:, hid], gw1[:, hid])
        for u, leftT, side in ((2 * i, tA, dact), (2 * i + 1, tB, act)):
            send = side.at[0:DH, hid]
            weight_grad(leftT, side[:, hid], send, own, table[u][0], D)
            core_send(u, send, own)

    for i in range(NT):
        for own in (0, 1):
            ff_back(own, i)
            events("ff%d%d" % (i, own))
    if LO_PLACE == "ff":
        lo_send(range(LO_FIRST, 4))
    for t in range(FF // D):
        gv[R_B1 + t:R_B1 + t + 1, :] = gb1[t]

    def norm1_back(i, carry):
        dg, ds, db = carry
        r = rows_of(i)
        up = acc[r, :]
        xh = xh1[r, :]
        dxh = up * vecf[R_G1:R_G1 + 1, :]
        gin = rs1[r, 0:1] * (dxh - jnp.mean(dxh, axis=1, keepdims=True) - xh * jnp.mean(dxh * xh, axis=1, keepdims=True))
        acc[r, :] = gin
        low = gin.astype(BF16)
        go[r, :] = low
        return dg + colsum(up * xh), ds + colsum(up), db + colsum(low.astype(F32))

    dg, ds, db = lax.fori_loop(0, L // TR, norm1_back, (zero, zero, zero))
    gv[R_G1:R_G1 + 1, :] = dg
    gv[R_S1:R_S1 + 1, :] = ds
    gv[R_BO:R_BO + 1, :] = db
    tB[...] = go[...].T
    UO = 2 * NT
    events("n1")
    if LO_PLACE == "n1":
        lo_send(range(LO_FIRST, 4))
    for u in range(UO):
        for cp in units[u]["core"]:
            cp.wait_send()
            waited.append(id(cp))
    dc[...] = nt(go[...], gwo[...]).astype(BF16)
    tail = 2 * FH

    def part(n, h):
        return dact.at[0:DH, pl.ds(al(D + (n % 3 * 2 + h) * DH, 128), DH)]

    for own in (0, 1):
        h = p if own else 1 - p
        weight_grad(tB, c[:, pl.ds(al(h * DH, 128), DH)], part(0, h), own, tail, DH)
        core_send(UO, part(0, h), own)
    events("wo")
    tA[...] = xo[...].T
    tB[...] = xx[...].T

    def attend_back(j, carry):
        cols = pl.ds(al(j * 128, 128), 128)
        kp, vp, qp, dcp = k[:, cols], v[:, cols], q[:, cols], dc[:, cols]
        kT = kp.T
        dkv = [jnp.zeros((L, 128), F32), jnp.zeros((L, 128), F32)]
        tops = []
        for hh in range(2):
            head = 2 * j + hh
            mine = head_lanes(hh)
            none = jnp.zeros_like(kp)
            km, vm = jnp.where(mine, kp, none), jnp.where(mine, vp, none)
            qm, dcm = jnp.where(mine, qp, none), jnp.where(mine, dcp, none)
            bias = head_bias(head)
            bias = jnp.concatenate([bias, bias], axis=1)
            parts = []
            for t in range(L // 256):
                ts = slice(t * 256, (t + 1) * 256)
                prob = jnp.exp(nt(km, qp[ts]) + bias - lse[head, :, ts])
                dprob = nt(vm, dcp[ts])
                delta = jnp.sum(prob * dprob, axis=0, keepdims=True)
                dscore = (prob * (dprob - delta)).astype(BF16)
                dkv[1] += nn(prob.astype(BF16), dcm[ts])
                dkv[0] += nn(dscore, qm[ts])
                parts.append(nn(kT[hh * 64:(hh + 1) * 64, :], dscore))
            tops.append(jnp.concatenate(parts, axis=1))
        dq[:, cols] = (jnp.concatenate(tops, axis=0).T * 0.125).astype(BF16)
        dk[:, cols] = dkv[0].astype(BF16)
        dv[:, cols] = dkv[1].astype(BF16)
        return carry

    for i in range(3):
        lax.fori_loop(i * NP * 2 // 3, (i + 1) * NP * 2 // 3, attend_back, 0)
        events("ab%d" % i)
    if LO_PLACE == "ab":
        lo_send(range(LO_FIRST, 4))
    gv[R_BQ:R_BQ + 1, :] = colsum(dq[...].astype(F32))
    gv[R_BV:R_BV + 1, :] = colsum(dv[...].astype(F32))

    swapped = vecf[R_LANE:R_LANE + 1, :] > 0.5
    none = jnp.zeros((L, D), BF16)
    dc[...] = jnp.where(swapped, dk[...], none)
    flow[...] = jnp.where(swapped, dv[...], none)
    dk[...] = jnp.where(swapped, none, dk[...])
    dv[...] = jnp.where(swapped, none, dv[...])
    backs[...] = (nt(dc[...], gwk[...]) + nt(flow[...], gwv[...])).astype(BF16)
    back_c = rc(backs, backr, core)
    for n, (a, x) in enumerate(((dq, None), (dk, dc), (dv, flow))):
        u = UO + 1 + n
        for own in (0, 1):
            h = p if own else 1 - p
            hs = pl.ds(al(h * DH, 128), DH)
            if n == 2:
                units[UO]["core"][own].wait_send()
                waited.append(id(units[UO]["core"][own]))
            send = part(1 + n, h)
            for dst, rows in ((send, send_rows), (gk.at[h, :, table[u][0]:table[u][0] + DH], keep_rows)):
                val = nn(tA[rows, :], a[:, hs])
                if x is not None:
                    val = val + nn(tB[rows, :], x[:, hs])
                dst[...] = val.astype(BF16)
            core_send(u, send, own)
        events("q%d" % (5 + n))
    vec_peers = [core, ypeer] + [peer_of(t) for t in range(dp_bits)]
    vstate = {"s": 0, "cp": None}
    gvr[0, 0] = gv[...]

    def vec_step():
        s = vstate["s"]
        if s > 0:
            vstate["cp"].wait_recv()
            total = gvr[s - 1, 0] + gvr[s - 1, 1]
            if s == len(vec_peers):
                gv[...] = total
                return
            gvr[s, 0] = total
        vstate["cp"] = rc(gvr.at[s, 0], gvr.at[s, 1], vec_peers[s])
        vstate["s"] = s + 1

    vec_step()
    acc[...] += nt(dq[...], gwq[...]) + nt(dk[...], gwk[...]) + nt(dv[...], gwv[...])
    events("acc")
    lo_local.wait()
    back_c.wait_recv()
    for r0 in range(0, L, TR):
        acc[r0:r0 + TR, :] += backr[r0:r0 + TR, :].astype(F32)
    xo[...] = acc[...].astype(BF16)
    gt_local = lc(xo, grad_tokens.at[p])
    gt_y = rc(xo, grad_tokens.at[p], ypeer)
    if LO_PLACE == "end":
        lo_send(range(LO_FIRST, 4))
    for i, u in enumerate(EVENTS["drain"]):
        step(u)
        if i % 4 == 3 and i // 4 < len(vec_peers):
            vec_step()
    for _ in range(len(vec_peers) - len(EVENTS["drain"]) // 4):
        vec_step()
    for un in units:
        un["out"].wait()
    gt_local.wait()
    gt_y.wait_recv()
    for cp in lo_y:
        cp.wait_recv()
    for cp in sent:
        if id(cp) not in waited:
            cp.wait_send()


def finish_kernel(
    lo, gt, gk, gv,
    lo_out, gt_out, g_wq, g_bq, g_wk, g_wv, g_bv, g_wo, g_bo, g_g1, g_s1, g_w1, g_b1, g_w2, g_b2, g_g2, g_s2,
    low, wide, held, sem_in, sem_out,
):
    p, b = lax.axis_index("perm"), lax.axis_index("blk")
    D = gv.shape[1]
    DH, FH = D // 2, g_w1.shape[1]
    n_cols = gk.shape[1] // DH
    loads = [pltpu.make_async_copy(gk.at[:, i * DH:(i + 1) * DH], low.at[i], sem_in.at[i]) for i in range(n_cols)]
    for load in loads:
        load.start()
    through = [pltpu.make_async_copy(src, held.at[i], sem_in.at[n_cols + i]) for i, src in enumerate((lo, gt))]
    for move in through:
        move.start()
    stores = []
    per = FH // DH
    for i in range(n_cols):
        loads[i].wait()
        value = low[i].astype(F32)
        if per <= i <= 2 * per:
            value = value.T
        wide[i] = value
        if i < per:
            dst = g_w1.at[:, i * DH:(i + 1) * DH]
        elif i < 2 * per:
            dst = g_w2.at[(i - per) * DH:(i - per + 1) * DH, :]
        else:
            dst = (g_wo, g_wq, g_wk, g_wv)[i - 2 * per]
        stores.append(pltpu.make_async_copy(wide.at[i], dst, sem_out.at[i]))
        stores[-1].start()

    def put(ref, row):
        ref[...] = row.reshape(ref.shape)

    for row, ref in ((R_BO, g_bo), (R_G1, g_g1), (R_S1, g_s1), (R_B2, g_b2), (R_G2, g_g2), (R_S2, g_s2)):
        put(ref, jnp.where(b == 0, gv[row:row + 1, 0:DH], gv[row:row + 1, DH:D]))
    for row, ref in ((R_BQ, g_bq), (R_BV, g_bv)):
        n = D // 4
        left = jnp.where(b == 0, gv[row:row + 1, 0:n], gv[row:row + 1, n:2 * n])
        right = jnp.where(b == 0, gv[row:row + 1, 2 * n:3 * n], gv[row:row + 1, 3 * n:D])
        put(ref, jnp.where(p == 0, left, right))
    left = jnp.where(b == 0, gv[R_B1:R_B1 + 1, :], gv[R_B1 + 1:R_B1 + 2, :])
    right = jnp.where(b == 0, gv[R_B1 + 2:R_B1 + 3, :], gv[R_B1 + 3:R_B1 + 4, :])
    put(g_b1, jnp.where(p == 0, left, right))
    for i, dst in enumerate((lo_out, gt_out)):
        through[i].wait()
        stores.append(pltpu.make_async_copy(held.at[i], dst, sem_out.at[n_cols + i]))
        stores[-1].start()
    for store in stores:
        store.wait()


def per_device(
    tokens, lengths, head_route, w_query, b_query, w_key, w_value, b_value, w_out, b_out,
    first_gain, first_shift, w_inner, b_inner, w_outer, b_outer, second_gain, second_shift, cotangent,
):
    L, D = tokens.shape[1:]
    FF = w_inner.shape[1] * 2
    heads = head_route.shape[0] * 2

    bits = (lax.axis_size("dp") - 1).bit_length()

    half = FF + 4 * (D // 2)
    any_ = pl.BlockSpec(memory_space=pl.ANY)
    vm = pl.BlockSpec(memory_space=pltpu.VMEM)
    smem = pl.BlockSpec(memory_space=pltpu.SMEM)
    V = pltpu.VMEM
    layer_out, grad_tokens, reduced, vectors = pl.pallas_call(
        functools.partial(layer_kernel, heads, lax.axis_size("dp")),
        out_shape=(
            jax.ShapeDtypeStruct(tokens.shape, BF16),
            jax.ShapeDtypeStruct(tokens.shape, BF16),
            jax.ShapeDtypeStruct((D // 2, half), BF16),
            jax.ShapeDtypeStruct((16, D), F32),
        ),
        in_specs=[any_, any_, smem, smem] + [any_] * 6 + [vm] * 9,
        out_specs=(any_, any_, any_, vm),
        scratch_shapes=[
            V((L, D), BF16), V((L, D), BF16), V((L, D), BF16),
            V((D, D), BF16), V((D, D), BF16), V((D, D), BF16), V((D, D), BF16), V((D, FF), BF16), V((FF, D), BF16),
            V((4, 16, D), F32), V((16, D), F32), V((2, L, 128), F32),
            V((L, D), BF16), V((L, D), BF16), V((L, D), BF16), V((L, D), BF16),
            V((L, D), BF16), V((L, D), F32), V((L, 128), F32), V((16, 1, L), F32),
            V((L, FF), BF16), V((L, FF), BF16), V((L, D), F32), V((L, D), BF16),
            V((D, L), BF16), V((D, L), BF16), V((L, D), BF16),
            V((L, D), F32), V((L, D), BF16),
            V((16, 1, 128), F32), V((FF // D, 1, D), F32), V((FF // D, 1, D), F32),
            V((2, D // 2, half), BF16), V((2, D // 2, half), BF16),
            V((2 + bits, 2, 16, D), F32),
        ] + [V(shape, BF16) for shape in stage_shapes(unit_table(D // 2, FF // 2, D), D // 2, bits)] + [
            pltpu.SemaphoreType.DMA((32,)),
            pltpu.SemaphoreType.DMA((256,)),
            pltpu.SemaphoreType.DMA((256,)),
        ],
        compiler_params=pltpu.CompilerParams(collective_id=0, has_side_effects=True, vmem_limit_bytes=62 * 2**20),
        name="layer",
    )(tokens, cotangent, lengths, head_route, w_query, w_key, w_value, w_out, w_inner, w_outer,
      b_query, b_value, b_out, first_gain, first_shift, b_outer, second_gain, second_shift, b_inner)

    DH, FH = D // 2, FF // 2
    shapes = [(DH, DH), (D // 4,), (DH, DH), (DH, DH), (D // 4,), (DH, DH), (DH,), (DH,), (DH,), (DH, FH),
              (FF // 4,), (FH, DH), (DH,), (DH,), (DH,)]
    moved = [jax.ShapeDtypeStruct(tokens.shape, BF16)] * 2
    n_cols = half // DH
    return tuple(pl.pallas_call(
        finish_kernel,
        out_shape=moved + [jax.ShapeDtypeStruct(shape, F32) for shape in shapes],
        in_specs=[any_, any_, any_, vm],
        out_specs=[any_, any_] + [any_ if len(shape) == 2 else vm for shape in shapes],
        scratch_shapes=[V((n_cols, DH, DH), BF16), V((n_cols, DH, DH), F32), V((2,) + tokens.shape, BF16),
                        pltpu.SemaphoreType.DMA((n_cols + 2,)), pltpu.SemaphoreType.DMA((n_cols + 2,))],
        compiler_params=pltpu.CompilerParams(vmem_limit_bytes=62 * 2**20),
        name="finish",
    )(layer_out, grad_tokens, reduced, vectors))


def solution(mesh):
    placed = (
        P("dp", "blk", None), P("dp"), P("perm"), P("blk", "perm"), P(("perm", "blk")), P("blk", "perm"),
        P("blk", "perm"), P(("perm", "blk")), P("perm", "blk"), P("blk"), P("blk"), P("blk"), P("blk", "perm"),
        P(("perm", "blk")), P("perm", "blk"), P("blk"), P("blk"), P("blk"), P("dp", "blk", None),
    )
    outs = (
        P("dp", "blk", None), P("dp", "blk", None), P("blk", "perm"), P(("perm", "blk")), P("blk", "perm"),
        P("blk", "perm"), P(("perm", "blk")), P("perm", "blk"), P("blk"), P("blk"), P("blk"), P("blk", "perm"),
        P(("perm", "blk")), P("perm", "blk"), P("blk"), P("blk"), P("blk"),
    )
    return jax.shard_map(per_device, mesh=mesh, in_specs=placed, out_specs=outs, check_vma=False)
```

```python
import functools
import math

import jax
import jax.numpy as jnp
from jax import lax
from jax.experimental import pallas as pl
from jax.experimental.pallas import tpu as pltpu
from jax.sharding import PartitionSpec as P

EPSILON = 1e-05
MASKED_SCORE = -1e30
MESH = pl.DeviceIdType.MESH
F32 = jnp.float32
BF16 = jnp.bfloat16
GELU_C = math.sqrt(2.0 / math.pi)


def nn(left, right):
    return lax.dot_general(left, right, (((1,), (0,)), ((), ())), preferred_element_type=F32)


def nt(left, right):
    return lax.dot_general(left, right, (((1,), (1,)), ((), ())), preferred_element_type=F32)


def al(value, multiple):
    return pl.multiple_of(value, multiple)


R_BQ, R_BV, R_BO, R_G1, R_S1, R_B2, R_G2, R_S2, R_B1, R_LANE = 0, 1, 2, 3, 4, 5, 6, 7, 8, 12
BY_BLK = (R_BO, R_G1, R_S1, R_B2, R_G2, R_S2)

ORDERS = (
    (0, "y", 1, 2),
    (1, 0, "y", 2),
    ("y", 0, 1, 2),
    (1, 0, "y", 2),
    (0, "y", 1, 2),
    ("y", 0, 1, 2),
    ("y", 0, 1, 2),
    ("y", 0, 1, 2),
)
EVENTS = {
    "ff00": (),
    "ff01": (),
    "ff10": (0, 1),
    "ff11": (),
    "n1": (),
    "wo": (2, 3, 4),
    "ab0": (0, 1),
    "ab1": (4,),
    "ab2": (2,),
    "q5": (8, 0, 1, 3),
    "q6": (8, 4, 5, 2),
    "q7": (0, 6, 4, 1),
    "acc": (8, 7, 0, 2, 3, 5, 4),
        "drain": (8, 1, 6, 5, 0, 2, 5, 6, 4, 7, 0, 8, 3, 1, 6, 7, 4, 2, 5, 7, 0, 3, 2, 6, 1, 5, 7, 4, 3, 6, 1, 2, 5,
        7, 3, 6, 7, 5, 6, 3, 7),
}
GATHER = {
    "project0": (("a", 0), ("a", 1),),
    "own0": (("a", 2),),
    "own1": (("a", 3), ("b", 0),),
    "own2": (("b", 1),),
    "wait": (("b", 2), ("a", 4), ("b", 3), ("c", 0), ("c", 1), ("c", 2), ("a", 5),),
    "project1": (),
    "other0": (("b", 4), ("c", 3),),
    "other1": (("a", 6), ("b", 5),),
    "other2": (("c", 4),),
    "norm": (("a", 7),),
    "ff_own0": (("b", 6), ("c", 5),),
    "ff_own1": (("b", 7),),
    "ff_other0": (),
    "ff_other1": (("c", 6), ("c", 7),),
}
LO_FIRST, LO_PLACE = 1, "end"


def unit_table(DH, FH, D):
    tail = 2 * FH
    table = []
    for i in range(FH // D):
        table += [(i * D, D), (FH + i * D, D)]
    table += [(tail + i * DH, DH) for i in range(4)]
    return [(col, width, order) for (col, width), order in zip(table, ORDERS)]


def stage_shapes(table, DH, bits):
    shapes = []
    for col, width, order in table:
        rows, halves = DH, 2
        for axis in order:
            if axis == "y":
                halves = 1
            elif axis < bits:
                rows //= 2
            else:
                continue
            shapes.append((halves, rows, width))
        for _ in range(bits - 3):
            shapes.append((1, rows, width))
    shapes += [(1, DH, width) for _, width, order in table if order[0] != "y"]
    return shapes


def layer_kernel(
    heads, dp_size,
    tokens, cot, lengths, route, wq, wk, wv, wo, w1, w2, *rest,
):
    vectors, (layer_out, grad_tokens, gk_out, gv), rest = rest[:9], rest[9:13], rest[13:]
    (xo, xx, cotb, gwq, gwk, gwv, gwo, gw1, gw2, vecs, vecf, biasb,
     q, k, v, c, flow, xh1, rs1, lse, act, dact, acc, go, tA, tB, lob, wide, backr, hrow, b1r, gb1,
     gk, rcore, gvr), rest = rest[:35], rest[35:]
    sem_l, sem_s, sem_r = rest[-3:]
    landing, landing_res = list(rest[:-3]), []
    d, p, b = lax.axis_index("dp"), lax.axis_index("perm"), lax.axis_index("blk")
    D = xo.shape[1]
    L = xo.shape[0]
    FF = gw2.shape[0]
    DH, FH = D // 2, FF // 2
    NP = heads // 4
    xbit = lax.rem(d, 2)
    dq, dk, dv, dc = (act.at[:, i * D:(i + 1) * D] for i in range(4))
    backs = dact.at[:, 0:D]
    core, ypeer, diag = (d, p, 1 - b), (d, 1 - p, b), (d, 1 - p, 1 - b)
    dp_bits = (dp_size - 1).bit_length()

    def bit(t):
        return lax.rem(lax.div(d, 2**t), 2)

    def peer_of(t):
        return (d + 2**t - 2 ** (t + 1) * bit(t), p, b)

    xpeer = peer_of(0)

    bar = pltpu.get_barrier_semaphore()
    peers = (core, ypeer, diag) + tuple(peer_of(t) for t in range(dp_bits))
    for peer in peers:
        pl.semaphore_signal(bar, 1, device_id=peer, device_id_type=MESH)
    pl.semaphore_wait(bar, len(peers))

    count = [0]
    sent = []
    waited = []

    class Copy:
        def __init__(self, src, dst, peer):
            self.index, self.src, self.dst, self.peer = count[0], src, dst, peer
            count[0] += 1
            self.make().start()
            sent.append(self)

        def make(self):
            src = self.src() if callable(self.src) else self.src
            dst = self.dst() if callable(self.dst) else self.dst
            return pltpu.make_async_remote_copy(
                src_ref=src, dst_ref=dst, send_sem=sem_s.at[self.index], recv_sem=sem_r.at[self.index],
                device_id=self.peer, device_id_type=MESH)

        def wait_recv(self):
            self.make().wait_recv()

        def wait_send(self):
            self.make().wait_send()

    rc = Copy

    def same(ref, peer):
        return rc(ref, ref, peer)

    nl = [0]

    def lc(src, dst):
        i = nl[0]
        nl[0] += 1
        cp = pltpu.make_async_copy(src, dst, sem_l.at[i])
        cp.start()
        return cp

    pieces = [(wq, gwq, True, 0, wq.shape[1]), (wk, gwk, True, 0, wk.shape[1]), (wv, gwv, True, 0, wv.shape[1]),
              (wo, gwo, False, 0, wo.shape[0])]
    for i in range(FH // D):
        pieces += [(w1, gw1, True, i * D, D), (w2, gw2, False, i * D, D)]
    NW = len(pieces)

    def extent(n):
        shard, _, by_blk, _, size = pieces[n]
        return (shard.shape[0], size) if by_blk else (size, shard.shape[1])

    def span(n, pp, bb, r0, rows):
        shard, full, by_blk, first, size = pieces[n]
        sr, sc = shard.shape
        if by_blk:
            return full.at[pl.ds(al(bb * sr + r0, 16), rows), pl.ds(al(pp * sc + first, 128), size)]
        return full.at[pl.ds(al(pp * sr + first + r0, 16), rows), pl.ds(al(bb * sc, 128), sc)]

    def shard_rows(n, r0, rows):
        shard, _, by_blk, first, size = pieces[n]
        if by_blk:
            return shard.at[pl.ds(al(r0, 16), rows), first:first + size]
        return shard.at[pl.ds(al(first + r0, 16), rows), :]

    zbit = bit(1)
    nxbit, nzbit = 1 - xbit, 1 - zbit
    zpeer = peer_of(1)

    def fourth(n, xb, zb):
        rows = extent(n)[0] // 4
        return (2 * xb + zb) * rows, rows

    def third(n, xb, zb, i):
        r0, rows = fourth(n, xb, zb)
        return r0 + i * (rows // 3), rows // 3

    quarter = p * 2 + b
    for row, ref in enumerate(vectors):
        vecs[quarter, row:row + 1, 0:ref.shape[0]] = ref[...].astype(F32).reshape(1, ref.shape[0])
    at_lane = lax.broadcasted_iota(jnp.int32, (1, DH), 1)
    routes = jnp.zeros((1, DH), F32)
    for i in range(heads // 2):
        here = (at_lane >= i * 64) & (at_lane < (i + 1) * 64)
        routes = jnp.where(here, route[i].astype(F32), routes)
    vecs[quarter, R_LANE:R_LANE + 1, 0:DH] = routes
    cp_x = lc(tokens.at[p], xo)
    own = [lc(shard_rows(n, 0, extent(n)[0]), span(n, p, b, 0, extent(n)[0])) for n in range(NW)]
    cp_cot = lc(cot.at[p], cotb)
    v_c = same(vecs.at[quarter], core)
    v_y = same(vecs.at[quarter], ypeer)
    v_d = same(vecs.at[quarter], diag)
    to_core, to_y, to_y3 = [], [], []
    for n in range(NW):
        to_core.append(rc(shard_rows(n, 0, extent(n)[0]), span(n, p, b, 0, extent(n)[0]), core))
        if n == 2:
            x_c = rc(tokens.at[p], xx, core)
        r = fourth(n, xbit, zbit)
        to_y.append(rc(shard_rows(n, *r), span(n, p, b, *r), ypeer))
        r = third(n, 1 - xbit, 1 - zbit, 0)
        to_y3.append(rc(shard_rows(n, *r), span(n, p, b, *r), ypeer))
    to_x, to_z, to_x3, to_z3 = ([None] * NW for _ in range(4))
    fwd = [[] for _ in range(NW)]

    def passed(n, part, *args):
        return lambda: span(n, 1 - p, b, *part(n, *args))

    def svc_a(n):
        to_y[n].wait_recv()
        src = passed(n, fourth, xbit, zbit)
        to_x[n] = same(src, xpeer)
        to_z[n] = same(src, zpeer)
        fwd[n].append(same(src, core))

    def svc_b(n):
        to_x[n].wait_recv()
        to_z3[n] = same(passed(n, third, nxbit, zbit, 2), zpeer)
        to_z[n].wait_recv()
        to_x3[n] = same(passed(n, third, xbit, nzbit, 1), xpeer)
        fwd[n].append(same(passed(n, fourth, nxbit, zbit), core))
        fwd[n].append(same(passed(n, fourth, xbit, nzbit), core))

    def svc_c(n):
        for cp in (to_y3[n], to_x3[n], to_z3[n]):
            cp.wait_recv()
        fwd[n].append(same(passed(n, fourth, nxbit, nzbit), core))

    def need(n):
        for cp in fwd[n]:
            cp.wait_recv()

    cp_x.wait()
    for cp in (v_c, v_y, v_d):
        cp.wait_recv()
    DQ = D // 4
    for row in (R_BQ, R_BV):
        vecf[row:row + 1, :] = jnp.concatenate([vecs[i, row:row + 1, 0:DQ] for i in range(4)], axis=1)
    for row in BY_BLK:
        vecf[row:row + 1, :] = jnp.concatenate([vecs[i, row:row + 1, 0:DH] for i in range(2)], axis=1)
    vecf[R_LANE:R_LANE + 1, :] = jnp.concatenate([vecs[2 * i, R_LANE:R_LANE + 1, 0:DH] for i in range(2)], axis=1)
    for t in range(FF // D):
        per = D * 4 // FF
        b1r[t] = jnp.concatenate([vecs[i, R_B1:R_B1 + 1, 0:FF // 4] for i in range(t * per, t * per + per)], axis=1)
    for pair in range(heads // 2):
        two = vecf[R_LANE:R_LANE + 1, pair * 128:pair * 128 + 128]
        hrow[2 * pair] = jnp.broadcast_to(two[:, 0:1], (1, 128))
        hrow[2 * pair + 1] = jnp.broadcast_to(two[:, 64:65], (1, 128))
    length = lengths[p]
    pos = lax.broadcasted_iota(jnp.int32, (L, 128), 0)
    for which in range(2):
        start = (b if which == 0 else 1 - b) * L
        biasb[which] = jnp.where(pos + start < length, 0.0, MASKED_SCORE)

    lane = lax.broadcasted_iota(jnp.int32, (1, 128), 1)

    def head_lanes(hh):
        return (lane < 64) if hh == 0 else (lane >= 64)

    def head_bias(head):
        return jnp.where(hrow[head] > 0.5, biasb[1], biasb[0])

    def project(h):
        cols = pl.ds(al(h * DH, 128), DH)
        swapped = vecf[R_LANE:R_LANE + 1, cols] > 0.5
        q[:, cols] = (nn(xo[...], gwq[:, cols]) + vecf[R_BQ:R_BQ + 1, cols]).astype(BF16) * jnp.asarray(0.125, BF16)
        k[:, cols] = jnp.where(swapped, nn(xx[...], gwk[:, cols]), nn(xo[...], gwk[:, cols])).astype(BF16)
        v[:, cols] = (jnp.where(swapped, nn(xx[...], gwv[:, cols]), nn(xo[...], gwv[:, cols]))
                      + vecf[R_BV:R_BV + 1, cols]).astype(BF16)

    def attend(h, j):
        cols = pl.ds(al(h * DH + j * 128, 128), 128)
        kp, vp = k[:, cols], v[:, cols]
        vT = vp.T
        tops = []
        for hh in range(2):
            head = h * (heads // 2) + 2 * j + hh
            km = jnp.where(head_lanes(hh), kp, jnp.zeros_like(kp))
            bias = head_bias(head)
            bias = jnp.concatenate([bias, bias], axis=1)
            parts = []
            for t in range(L // 256):
                s = nt(km, q[t * 256:(t + 1) * 256, cols]) + bias
                peak = jnp.max(s, axis=0, keepdims=True)
                e = jnp.exp(s - peak)
                total = jnp.sum(e, axis=0, keepdims=True)
                lse[head, :, t * 256:(t + 1) * 256] = peak + jnp.log(total)
                parts.append(nn(vT[hh * 64:(hh + 1) * 64, :], e.astype(BF16)) * (1.0 / total))
            tops.append(jnp.concatenate(parts, axis=1))
        c[:, cols] = jnp.concatenate(tops, axis=0).T.astype(BF16)

    def gather(place):
        for kind, n in GATHER[place]:
            {"a": svc_a, "b": svc_b, "c": svc_c}[kind](n)

    def pairs(h, name):
        def one(j, carry):
            attend(h, j)
            for i in range(NP):
                pl.when(j == i)(functools.partial(gather, "%s%d" % (name, i)))
            return carry

        lax.fori_loop(0, NP, one, 0)

    for n in range(3):
        own[n].wait()
        to_core[n].wait_recv()
    x_c.wait_recv()
    project(p)
    gather("project0")
    pairs(p, "own")
    gather("wait")
    own[3].wait()
    to_core[3].wait_recv()
    for n in range(3):
        need(n)
    project(1 - p)
    gather("project1")
    pairs(1 - p, "other")
    need(3)

    acc[...] = nn(c[...], gwo[...])
    TR = 128

    def rows_of(i):
        return pl.ds(al(i * TR, TR), TR)

    def norm1(i, carry):
        r = rows_of(i)
        val = xo[r, :].astype(F32) + (acc[r, :] + vecf[R_BO:R_BO + 1, :])
        centre = val - jnp.mean(val, axis=1, keepdims=True)
        spread = jnp.mean(centre * centre, axis=1, keepdims=True)
        rs = lax.rsqrt(spread + EPSILON)
        xh = centre * rs
        xh1[r, :] = xh
        rs1[r, :] = jnp.broadcast_to(rs, (TR, 128))
        flow[r, :] = (xh * vecf[R_G1:R_G1 + 1, :] + vecf[R_S1:R_S1 + 1, :]).astype(BF16)
        return carry

    lax.fori_loop(0, L // TR, norm1, 0)
    gather("norm")
    tA[...] = flow[...].T

    NT = FH // D

    def ff_tile(h, i, first):
        hid = pl.ds(al(h * FH + i * D, 128), D)
        wide[...] = nn(flow[...], gw1[:, hid])

        def gelu_rows(j, carry):
            r = pl.ds(al(j * 32, 32), 32)
            u = wide[r, :] + b1r[h * NT + i]
            uu = u * u
            th = jnp.tanh(GELU_C * u * (1.0 + 0.044715 * uu))
            half = 0.5 * (1.0 + th)
            act[r, hid] = (u * half).astype(BF16)
            slope = half + 0.5 * u * (1.0 - th * th) * (GELU_C * (1.0 + 3 * 0.044715 * uu))
            dact[r, hid] = slope.astype(BF16)
            return carry

        lax.fori_loop(0, L // 32, gelu_rows, 0)
        out = nn(act[:, hid], gw2[hid, :])
        if first:
            acc[...] = out
        else:
            acc[...] += out

    for n in range(4, NW):
        own[n].wait()
        to_core[n].wait_recv()
    for i in range(NT):
        ff_tile(p, i, i == 0)
        gather("ff_own%d" % i)
    for i in range(NT):
        gather("ff_other%d" % i)
        need(4 + 2 * i)
        need(5 + 2 * i)
        ff_tile(1 - p, i, False)

    cp_cot.wait()
    zero = jnp.zeros((1, D), F32)
    for r0 in range(gv.shape[0]):
        gv[r0:r0 + 1, :] = zero

    def colsum(x):
        return jnp.sum(x, axis=0, keepdims=True)

    def norm2(i, carry):
        dg, ds, db = carry
        r = rows_of(i)
        fo = xh1[r, :] * vecf[R_G1:R_G1 + 1, :] + vecf[R_S1:R_S1 + 1, :]
        val = fo + (acc[r, :] + vecf[R_B2:R_B2 + 1, :])
        centre = val - jnp.mean(val, axis=1, keepdims=True)
        spread = jnp.mean(centre * centre, axis=1, keepdims=True)
        rs = lax.rsqrt(spread + EPSILON)
        xh = centre * rs
        g2 = vecf[R_G2:R_G2 + 1, :]
        lob[r, :] = (xh * g2 + vecf[R_S2:R_S2 + 1, :]).astype(BF16)
        up = cotb[r, :].astype(F32)
        dxh = up * g2
        gin = rs * (dxh - jnp.mean(dxh, axis=1, keepdims=True) - xh * jnp.mean(dxh * xh, axis=1, keepdims=True))
        acc[r, :] = gin
        low = gin.astype(BF16)
        go[r, :] = low
        return dg + colsum(up * xh), ds + colsum(up), db + colsum(low.astype(F32))

    dg, ds, db = lax.fori_loop(0, L // TR, norm2, (zero, zero, zero))
    gv[R_G2:R_G2 + 1, :] = dg
    gv[R_S2:R_S2 + 1, :] = ds
    gv[R_B2:R_B2 + 1, :] = db
    lo_local = lc(lob, layer_out.at[p])
    lo_y = []

    def lo_send(parts):
        for i in parts:
            part = pl.ds(i * (L // 4), L // 4)
            lo_y.append(rc(lob.at[part], layer_out.at[p, part], ypeer))

    lo_send(range(LO_FIRST))

    tB[...] = go[...].T
    keep_rows = pl.ds(al(b * DH, 128), DH)
    send_rows = pl.ds(al((1 - b) * DH, 128), DH)

    table = unit_table(DH, FH, D)
    units = []
    n_res = sum(order[0] != "y" for _, _, order in table)
    landing, landing_res = landing[:len(landing) - n_res], landing[len(landing) - n_res:]
    for col, width, order in table:
        order = [axis for axis in order if axis == "y" or axis < dp_bits]
        bufs = [landing.pop(0) for _ in range(len(order) + max(dp_bits - 3, 0))]
        units.append({"at": slice(col, col + width), "order": order, "bufs": bufs, "next": 0, "r0": 0, "rows": DH,
                      "both": True, "core": [None, None], "copy": None, "path": []})
        units[-1]["res"] = bufs[0] if order[0] == "y" else landing_res.pop(0)

    def core_send(u, src, h_is_own):
        h = p if h_is_own else 1 - p
        units[u]["core"][h_is_own] = rc(src, rcore.at[h, :, units[u]["at"]], core)

    def add_block(h, r0, rows, at, src):
        step = 48 if rows % 48 == 0 else rows

        def one(i, carry):
            here = pl.ds(al(r0 + i * step, 16), step)
            gk[h, here, at] = (gk[h, here, at].astype(F32) + src(pl.ds(al(i * step, 16), step)).astype(F32)).astype(BF16)
            return carry

        lax.fori_loop(0, rows // step, one, 0)

    def start_stage(u, s):
        un = units[u]
        axis, buf, at = un["order"][s], un["bufs"][s], un["at"]
        if axis == "y":
            here = pl.ds(al(un["r0"], 16), un["rows"])
            un["copy"] = rc(gk.at[1 - p, here, at], buf.at[0], ypeer)
            un["both"] = False
            return
        rows = un["rows"] // 2
        away = pl.ds(al(un["r0"] + (1 - bit(axis)) * rows, 16), rows)
        src = gk.at[:, away, at] if un["both"] else gk.at[pl.ds(p, 1), away, at]
        un["copy"] = rc(src, buf, peer_of(axis))
        un["path"].append((axis, un["r0"], un["rows"]))
        un["r0"] = un["r0"] + bit(axis) * rows
        un["rows"] = rows

    def step(u):
        un = units[u]
        ev, n, at = un["next"], len(un["order"]), un["at"]
        un["next"] += 1
        if ev == 0:
            for own in (0, 1):
                un["core"][own].wait_recv()
                h = p if own else 1 - p
                add_block(h, 0, DH, at, lambda r, h=h: rcore[h, r, at])
            start_stage(u, 0)
            return
        un["copy"].wait_recv()
        if ev <= n:
            buf = un["bufs"][ev - 1]
            if un["both"]:
                for h in range(2):
                    add_block(h, un["r0"], un["rows"], at, lambda r, h=h: buf[h, r, :])
            else:
                add_block(p, un["r0"], un["rows"], at, lambda r: buf[0, r, :])
            if ev < n:
                start_stage(u, ev)
                return
            for t in range(3, dp_bits):
                buf = un["bufs"][n + t - 3]
                mine = gk.at[pl.ds(p, 1), pl.ds(al(un["r0"], 16), un["rows"]), at]
                cp = rc(mine, buf, peer_of(t))
                cp.wait_recv()
                cp.wait_send()
                waited.append(id(cp))
                add_block(p, un["r0"], un["rows"], at, lambda r: buf[0, r, :])
            here = pl.ds(al(un["r0"], 16), un["rows"])
            un["res"][0, here, :] = gk[p, here, at]
        if un["path"]:
            axis, r0, rows = un["path"].pop()
            mine = un["res"].at[0, pl.ds(al(un["r0"], 16), un["rows"])]
            un["copy"] = rc(mine, mine, peer_of(axis))
            un["r0"], un["rows"] = r0, rows
            return
        un["out"] = lc(un["res"].at[0], gk_out.at[:, at])

    def events(place):
        for u in EVENTS[place]:
            if u < len(units):
                step(u)
            else:
                vec_step()

    def weight_grad(leftT, right, send, own, col, width):
        h = p if own else 1 - p
        send[...] = nn(leftT[send_rows, :], right).astype(BF16)
        gk[h, :, col:col + width] = nn(leftT[keep_rows, :], right).astype(BF16)

    def ff_back(own, i):
        h = p if own else 1 - p
        hid = pl.ds(al(h * FH + i * D, 128), D)
        du = (nt(go[...], gw2[hid, :]) * dact[:, hid].astype(F32)).astype(BF16)
        gb1[h * NT + i] = colsum(du.astype(F32))
        dact[:, hid] = du
        acc[...] += nt(dact[:, hid], gw1[:, hid])
        for u, leftT, side in ((2 * i, tA, dact), (2 * i + 1, tB, act)):
            send = side.at[0:DH, hid]
            weight_grad(leftT, side[:, hid], send, own, table[u][0], D)
            core_send(u, send, own)

    for i in range(NT):
        for own in (0, 1):
            ff_back(own, i)
            events("ff%d%d" % (i, own))
    if LO_PLACE == "ff":
        lo_send(range(LO_FIRST, 4))
    for t in range(FF // D):
        gv[R_B1 + t:R_B1 + t + 1, :] = gb1[t]

    def norm1_back(i, carry):
        dg, ds, db = carry
        r = rows_of(i)
        up = acc[r, :]
        xh = xh1[r, :]
        dxh = up * vecf[R_G1:R_G1 + 1, :]
        gin = rs1[r, 0:1] * (dxh - jnp.mean(dxh, axis=1, keepdims=True) - xh * jnp.mean(dxh * xh, axis=1, keepdims=True))
        acc[r, :] = gin
        low = gin.astype(BF16)
        go[r, :] = low
        return dg + colsum(up * xh), ds + colsum(up), db + colsum(low.astype(F32))

    dg, ds, db = lax.fori_loop(0, L // TR, norm1_back, (zero, zero, zero))
    gv[R_G1:R_G1 + 1, :] = dg
    gv[R_S1:R_S1 + 1, :] = ds
    gv[R_BO:R_BO + 1, :] = db
    tB[...] = go[...].T
    UO = 2 * NT
    events("n1")
    if LO_PLACE == "n1":
        lo_send(range(LO_FIRST, 4))
    for u in range(UO):
        for cp in units[u]["core"]:
            cp.wait_send()
            waited.append(id(cp))
    dc[...] = nt(go[...], gwo[...]).astype(BF16)
    tail = 2 * FH

    def part(n, h):
        return dact.at[0:DH, pl.ds(al(D + (n % 3 * 2 + h) * DH, 128), DH)]

    for own in (0, 1):
        h = p if own else 1 - p
        weight_grad(tB, c[:, pl.ds(al(h * DH, 128), DH)], part(0, h), own, tail, DH)
        core_send(UO, part(0, h), own)
    events("wo")
    tA[...] = xo[...].T
    tB[...] = xx[...].T

    def attend_back(j, carry):
        cols = pl.ds(al(j * 128, 128), 128)
        kp, vp, qp, dcp = k[:, cols], v[:, cols], q[:, cols], dc[:, cols]
        kT = kp.T
        dkv = [jnp.zeros((L, 128), F32), jnp.zeros((L, 128), F32)]
        tops = []
        for hh in range(2):
            head = 2 * j + hh
            mine = head_lanes(hh)
            none = jnp.zeros_like(kp)
            km, vm = jnp.where(mine, kp, none), jnp.where(mine, vp, none)
            qm, dcm = jnp.where(mine, qp, none), jnp.where(mine, dcp, none)
            bias = head_bias(head)
            bias = jnp.concatenate([bias, bias], axis=1)
            parts = []
            for t in range(L // 256):
                ts = slice(t * 256, (t + 1) * 256)
                prob = jnp.exp(nt(km, qp[ts]) + bias - lse[head, :, ts])
                dprob = nt(vm, dcp[ts])
                delta = jnp.sum(prob * dprob, axis=0, keepdims=True)
                dscore = (prob * (dprob - delta)).astype(BF16)
                dkv[1] += nn(prob.astype(BF16), dcm[ts])
                dkv[0] += nn(dscore, qm[ts])
                parts.append(nn(kT[hh * 64:(hh + 1) * 64, :], dscore))
            tops.append(jnp.concatenate(parts, axis=1))
        dq[:, cols] = (jnp.concatenate(tops, axis=0).T * 0.125).astype(BF16)
        dk[:, cols] = dkv[0].astype(BF16)
        dv[:, cols] = dkv[1].astype(BF16)
        return carry

    for i in range(3):
        lax.fori_loop(i * NP * 2 // 3, (i + 1) * NP * 2 // 3, attend_back, 0)
        events("ab%d" % i)
    if LO_PLACE == "ab":
        lo_send(range(LO_FIRST, 4))
    gv[R_BQ:R_BQ + 1, :] = colsum(dq[...].astype(F32))
    gv[R_BV:R_BV + 1, :] = colsum(dv[...].astype(F32))

    vec_peers = [core, ypeer] + [peer_of(t) for t in range(dp_bits)]
    vstate = {"s": 0, "cp": None, "done": False}
    gvr[0, 0] = gv[...]

    def vec_step():
        s = vstate["s"]
        if s > 0:
            vstate["cp"].wait_recv()
            total = gvr[s - 1, 0] + gvr[s - 1, 1]
            if s == len(vec_peers):
                gv[...] = total
                vstate["done"] = True
                return
            gvr[s, 0] = total
        vstate["cp"] = rc(gvr.at[s, 0], gvr.at[s, 1], vec_peers[s])
        vstate["s"] = s + 1

    vec_step()

    swapped = vecf[R_LANE:R_LANE + 1, :] > 0.5
    none = jnp.zeros((L, D), BF16)
    dc[...] = jnp.where(swapped, dk[...], none)
    flow[...] = jnp.where(swapped, dv[...], none)
    dk[...] = jnp.where(swapped, none, dk[...])
    dv[...] = jnp.where(swapped, none, dv[...])
    backs[...] = (nt(dc[...], gwk[...]) + nt(flow[...], gwv[...])).astype(BF16)
    back_c = rc(backs, backr, core)
    for n, (a, x) in enumerate(((dq, None), (dk, dc), (dv, flow))):
        u = UO + 1 + n
        for own in (0, 1):
            h = p if own else 1 - p
            hs = pl.ds(al(h * DH, 128), DH)
            if n == 2:
                units[UO]["core"][own].wait_send()
                waited.append(id(units[UO]["core"][own]))
            send = part(1 + n, h)
            for dst, rows in ((send, send_rows), (gk.at[h, :, table[u][0]:table[u][0] + DH], keep_rows)):
                val = nn(tA[rows, :], a[:, hs])
                if x is not None:
                    val = val + nn(tB[rows, :], x[:, hs])
                dst[...] = val.astype(BF16)
            core_send(u, send, own)
        events("q%d" % (5 + n))
    acc[...] += nt(dq[...], gwq[...]) + nt(dk[...], gwk[...]) + nt(dv[...], gwv[...])
    events("acc")
    lo_local.wait()
    back_c.wait_recv()
    for r0 in range(0, L, TR):
        acc[r0:r0 + TR, :] += backr[r0:r0 + TR, :].astype(F32)
    xo[...] = acc[...].astype(BF16)
    gt_local = lc(xo, grad_tokens.at[p])
    gt_y = rc(xo, grad_tokens.at[p], ypeer)
    if LO_PLACE == "end":
        lo_send(range(LO_FIRST, 4))
    events("drain")
    while not vstate["done"]:
        vec_step()
    for un in units:
        un["out"].wait()
    gt_local.wait()
    gt_y.wait_recv()
    for cp in lo_y:
        cp.wait_recv()
    for cp in sent:
        if id(cp) not in waited:
            cp.wait_send()


def finish_kernel(
    lo, gt, gk, gv,
    lo_out, gt_out, g_wq, g_bq, g_wk, g_wv, g_bv, g_wo, g_bo, g_g1, g_s1, g_w1, g_b1, g_w2, g_b2, g_g2, g_s2,
    low, wide, held, sem_in, sem_out,
):
    p, b = lax.axis_index("perm"), lax.axis_index("blk")
    D = gv.shape[1]
    DH, FH = D // 2, g_w1.shape[1]
    n_cols = gk.shape[1] // DH
    loads = [pltpu.make_async_copy(gk.at[:, i * DH:(i + 1) * DH], low.at[i], sem_in.at[i]) for i in range(n_cols)]
    for load in loads:
        load.start()
    through = [pltpu.make_async_copy(src, held.at[i], sem_in.at[n_cols + i]) for i, src in enumerate((lo, gt))]
    for move in through:
        move.start()
    stores = []
    per = FH // DH
    for i in range(n_cols):
        loads[i].wait()
        value = low[i].astype(F32)
        if per <= i <= 2 * per:
            value = value.T
        wide[i] = value
        if i < per:
            dst = g_w1.at[:, i * DH:(i + 1) * DH]
        elif i < 2 * per:
            dst = g_w2.at[(i - per) * DH:(i - per + 1) * DH, :]
        else:
            dst = (g_wo, g_wq, g_wk, g_wv)[i - 2 * per]
        stores.append(pltpu.make_async_copy(wide.at[i], dst, sem_out.at[i]))
        stores[-1].start()

    def put(ref, row):
        ref[...] = row.reshape(ref.shape)

    for row, ref in ((R_BO, g_bo), (R_G1, g_g1), (R_S1, g_s1), (R_B2, g_b2), (R_G2, g_g2), (R_S2, g_s2)):
        put(ref, jnp.where(b == 0, gv[row:row + 1, 0:DH], gv[row:row + 1, DH:D]))
    for row, ref in ((R_BQ, g_bq), (R_BV, g_bv)):
        n = D // 4
        left = jnp.where(b == 0, gv[row:row + 1, 0:n], gv[row:row + 1, n:2 * n])
        right = jnp.where(b == 0, gv[row:row + 1, 2 * n:3 * n], gv[row:row + 1, 3 * n:D])
        put(ref, jnp.where(p == 0, left, right))
    left = jnp.where(b == 0, gv[R_B1:R_B1 + 1, :], gv[R_B1 + 1:R_B1 + 2, :])
    right = jnp.where(b == 0, gv[R_B1 + 2:R_B1 + 3, :], gv[R_B1 + 3:R_B1 + 4, :])
    put(g_b1, jnp.where(p == 0, left, right))
    for i, dst in enumerate((lo_out, gt_out)):
        through[i].wait()
        stores.append(pltpu.make_async_copy(held.at[i], dst, sem_out.at[n_cols + i]))
        stores[-1].start()
    for store in stores:
        store.wait()


def per_device(
    tokens, lengths, head_route, w_query, b_query, w_key, w_value, b_value, w_out, b_out,
    first_gain, first_shift, w_inner, b_inner, w_outer, b_outer, second_gain, second_shift, cotangent,
):
    L, D = tokens.shape[1:]
    FF = w_inner.shape[1] * 2
    heads = head_route.shape[0] * 2

    bits = (lax.axis_size("dp") - 1).bit_length()

    half = FF + 4 * (D // 2)
    any_ = pl.BlockSpec(memory_space=pl.ANY)
    vm = pl.BlockSpec(memory_space=pltpu.VMEM)
    smem = pl.BlockSpec(memory_space=pltpu.SMEM)
    V = pltpu.VMEM
    layer_out, grad_tokens, reduced, vectors = pl.pallas_call(
        functools.partial(layer_kernel, heads, lax.axis_size("dp")),
        out_shape=(
            jax.ShapeDtypeStruct(tokens.shape, BF16),
            jax.ShapeDtypeStruct(tokens.shape, BF16),
            jax.ShapeDtypeStruct((D // 2, half), BF16),
            jax.ShapeDtypeStruct((16, D), F32),
        ),
        in_specs=[any_, any_, smem, smem] + [any_] * 6 + [vm] * 9,
        out_specs=(any_, any_, any_, vm),
        scratch_shapes=[
            V((L, D), BF16), V((L, D), BF16), V((L, D), BF16),
            V((D, D), BF16), V((D, D), BF16), V((D, D), BF16), V((D, D), BF16), V((D, FF), BF16), V((FF, D), BF16),
            V((4, 16, D), F32), V((16, D), F32), V((2, L, 128), F32),
            V((L, D), BF16), V((L, D), BF16), V((L, D), BF16), V((L, D), BF16),
            V((L, D), BF16), V((L, D), F32), V((L, 128), F32), V((16, 1, L), F32),
            V((L, FF), BF16), V((L, FF), BF16), V((L, D), F32), V((L, D), BF16),
            V((D, L), BF16), V((D, L), BF16), V((L, D), BF16),
            V((L, D), F32), V((L, D), BF16),
            V((16, 1, 128), F32), V((FF // D, 1, D), F32), V((FF // D, 1, D), F32),
            V((2, D // 2, half), BF16), V((2, D // 2, half), BF16),
            V((2 + bits, 2, 16, D), F32),
        ] + [V(shape, BF16) for shape in stage_shapes(unit_table(D // 2, FF // 2, D), D // 2, bits)] + [
            pltpu.SemaphoreType.DMA((32,)),
            pltpu.SemaphoreType.DMA((256,)),
            pltpu.SemaphoreType.DMA((256,)),
        ],
        compiler_params=pltpu.CompilerParams(collective_id=0, has_side_effects=True, vmem_limit_bytes=62 * 2**20),
        name="layer",
    )(tokens, cotangent, lengths, head_route, w_query, w_key, w_value, w_out, w_inner, w_outer,
      b_query, b_value, b_out, first_gain, first_shift, b_outer, second_gain, second_shift, b_inner)

    DH, FH = D // 2, FF // 2
    shapes = [(DH, DH), (D // 4,), (DH, DH), (DH, DH), (D // 4,), (DH, DH), (DH,), (DH,), (DH,), (DH, FH),
              (FF // 4,), (FH, DH), (DH,), (DH,), (DH,)]
    moved = [jax.ShapeDtypeStruct(tokens.shape, BF16)] * 2
    n_cols = half // DH
    return tuple(pl.pallas_call(
        finish_kernel,
        out_shape=moved + [jax.ShapeDtypeStruct(shape, F32) for shape in shapes],
        in_specs=[any_, any_, any_, vm],
        out_specs=[any_, any_] + [any_ if len(shape) == 2 else vm for shape in shapes],
        scratch_shapes=[V((n_cols, DH, DH), BF16), V((n_cols, DH, DH), F32), V((2,) + tokens.shape, BF16),
                        pltpu.SemaphoreType.DMA((n_cols + 2,)), pltpu.SemaphoreType.DMA((n_cols + 2,))],
        compiler_params=pltpu.CompilerParams(vmem_limit_bytes=62 * 2**20),
        name="finish",
    )(layer_out, grad_tokens, reduced, vectors))


def solution(mesh):
    placed = (
        P("dp", "blk", None), P("dp"), P("perm"), P("blk", "perm"), P(("perm", "blk")), P("blk", "perm"),
        P("blk", "perm"), P(("perm", "blk")), P("perm", "blk"), P("blk"), P("blk"), P("blk"), P("blk", "perm"),
        P(("perm", "blk")), P("perm", "blk"), P("blk"), P("blk"), P("blk"), P("dp", "blk", None),
    )
    outs = (
        P("dp", "blk", None), P("dp", "blk", None), P("blk", "perm"), P(("perm", "blk")), P("blk", "perm"),
        P("blk", "perm"), P(("perm", "blk")), P("perm", "blk"), P("blk"), P("blk"), P("blk"), P("blk", "perm"),
        P(("perm", "blk")), P("perm", "blk"), P("blk"), P("blk"), P("blk"),
    )
    return jax.shard_map(per_device, mesh=mesh, in_specs=placed, out_specs=outs, check_vma=False)
```

```python
import functools
import math

import jax
import jax.numpy as jnp
from jax import lax
from jax.experimental import pallas as pl
from jax.experimental.pallas import tpu as pltpu
from jax.sharding import PartitionSpec as P

EPSILON = 1e-05
MASKED_SCORE = -1e30
MESH = pl.DeviceIdType.MESH
F32 = jnp.float32
BF16 = jnp.bfloat16
GELU_C = math.sqrt(2.0 / math.pi)


def nn(left, right):
    return lax.dot_general(left, right, (((1,), (0,)), ((), ())), preferred_element_type=F32)


def nt(left, right):
    return lax.dot_general(left, right, (((1,), (1,)), ((), ())), preferred_element_type=F32)


def al(value, multiple):
    return pl.multiple_of(value, multiple)


R_BQ, R_BV, R_BO, R_G1, R_S1, R_B2, R_G2, R_S2, R_B1, R_LANE = 0, 1, 2, 3, 4, 5, 6, 7, 8, 12
BY_BLK = (R_BO, R_G1, R_S1, R_B2, R_G2, R_S2)

ORDERS = (
    ("y", 0, 1, 2),
    (0, 1, "y", 2),
    (1, 0, "y", 2),
    ("y", 0, 1, 2),
    ("y", 1, 0, 2),
    ("y", 0, 1, 2),
    ("y", 0, 1, 2),
    ("y", 0, 1, 2),
)
EVENTS = {
    "ff00": (),
    "ff01": (0,),
    "ff10": (1,),
    "ff11": (3,),
    "n1": (2,),
    "wo": (),
    "ab0": (0, 4),
    "ab1": (1,),
    "ab2": (3, 0, 2),
    "q5": (8, 4, 1),
    "q6": (0, 3, 8, 5),
    "q7": (6, 4, 1),
    "acc": (8, 0, 2, 3, 7, 4),
        "drain": (1, 8, 5, 0, 3, 6, 5, 4, 2, 0, 1, 6, 8, 5, 7, 3, 4, 0, 1, 6, 2, 7, 5, 4, 3, 6, 2, 7, 5, 1, 4, 6, 7,
        5, 3, 6, 7, 2, 7, 5, 6, 2, 7),
}
GATHER = {
    "project0": (("a", 0), ("a", 1),),
    "own0": (("a", 2),),
    "own1": (("a", 3), ("b", 0),),
    "own2": (("b", 1),),
    "wait": (("b", 2), ("a", 4), ("b", 3), ("c", 0), ("c", 1), ("c", 2), ("a", 5),),
    "project1": (),
    "other0": (("b", 4), ("c", 3),),
    "other1": (("a", 6), ("b", 5),),
    "other2": (("c", 4),),
    "norm": (("a", 7),),
    "ff_own0": (("b", 6), ("c", 5),),
    "ff_own1": (("b", 7),),
    "ff_other0": (),
    "ff_other1": (("c", 6), ("c", 7),),
}
LO_FIRST, LO_PLACE = 1, "end"


def unit_table(DH, FH, D):
    tail = 2 * FH
    table = []
    for i in range(FH // D):
        table += [(i * D, D), (FH + i * D, D)]
    table += [(tail + i * DH, DH) for i in range(4)]
    return [(col, width, order) for (col, width), order in zip(table, ORDERS)]


def stage_shapes(table, DH, bits):
    shapes = []
    for col, width, order in table:
        rows, halves = DH, 2
        for axis in order:
            if axis == "y":
                halves = 1
            elif axis < bits:
                rows //= 2
            else:
                continue
            shapes.append((halves, rows, width))
        for _ in range(bits - 3):
            shapes.append((1, rows, width))
    shapes += [(1, DH, width) for _, width, order in table if order[0] != "y"]
    return shapes


def layer_kernel(
    heads, dp_size,
    tokens, cot, lengths, route, wq, wk, wv, wo, w1, w2, *rest,
):
    vectors, (layer_out, grad_tokens, gk_out, gv), rest = rest[:9], rest[9:13], rest[13:]
    (xo, xx, cotb, gwq, gwk, gwv, gwo, gw1, gw2, vecs, vecf, biasb,
     q, k, v, c, flow, xh1, rs1, lse, act, dact, acc, go, tA, tB, lob, wide, backr, hrow, b1r, gb1,
     gk, rcore, gvr), rest = rest[:35], rest[35:]
    sem_l, sem_s, sem_r = rest[-3:]
    landing, landing_res = list(rest[:-3]), []
    d, p, b = lax.axis_index("dp"), lax.axis_index("perm"), lax.axis_index("blk")
    D = xo.shape[1]
    L = xo.shape[0]
    FF = gw2.shape[0]
    DH, FH = D // 2, FF // 2
    NP = heads // 4
    xbit = lax.rem(d, 2)
    dq, dk, dv, dc = (act.at[:, i * D:(i + 1) * D] for i in range(4))
    backs = dact.at[:, 0:D]
    core, ypeer, diag = (d, p, 1 - b), (d, 1 - p, b), (d, 1 - p, 1 - b)
    dp_bits = (dp_size - 1).bit_length()

    def bit(t):
        return lax.rem(lax.div(d, 2**t), 2)

    def peer_of(t):
        return (d + 2**t - 2 ** (t + 1) * bit(t), p, b)

    xpeer = peer_of(0)

    bar = pltpu.get_barrier_semaphore()
    peers = (core, ypeer, diag) + tuple(peer_of(t) for t in range(dp_bits))
    for peer in peers:
        pl.semaphore_signal(bar, 1, device_id=peer, device_id_type=MESH)
    pl.semaphore_wait(bar, len(peers))

    count = [0]
    sent = []
    waited = []

    class Copy:
        def __init__(self, src, dst, peer):
            self.index, self.src, self.dst, self.peer = count[0], src, dst, peer
            count[0] += 1
            self.make().start()
            sent.append(self)

        def make(self):
            src = self.src() if callable(self.src) else self.src
            dst = self.dst() if callable(self.dst) else self.dst
            return pltpu.make_async_remote_copy(
                src_ref=src, dst_ref=dst, send_sem=sem_s.at[self.index], recv_sem=sem_r.at[self.index],
                device_id=self.peer, device_id_type=MESH)

        def wait_recv(self):
            self.make().wait_recv()

        def wait_send(self):
            self.make().wait_send()

    rc = Copy

    def same(ref, peer):
        return rc(ref, ref, peer)

    nl = [0]

    def lc(src, dst):
        i = nl[0]
        nl[0] += 1
        cp = pltpu.make_async_copy(src, dst, sem_l.at[i])
        cp.start()
        return cp

    pieces = [(wq, gwq, True, 0, wq.shape[1]), (wk, gwk, True, 0, wk.shape[1]), (wv, gwv, True, 0, wv.shape[1]),
              (wo, gwo, False, 0, wo.shape[0])]
    for i in range(FH // D):
        pieces += [(w1, gw1, True, i * D, D), (w2, gw2, False, i * D, D)]
    NW = len(pieces)

    def extent(n):
        shard, _, by_blk, _, size = pieces[n]
        return (shard.shape[0], size) if by_blk else (size, shard.shape[1])

    def span(n, pp, bb, r0, rows):
        shard, full, by_blk, first, size = pieces[n]
        sr, sc = shard.shape
        if by_blk:
            return full.at[pl.ds(al(bb * sr + r0, 16), rows), pl.ds(al(pp * sc + first, 128), size)]
        return full.at[pl.ds(al(pp * sr + first + r0, 16), rows), pl.ds(al(bb * sc, 128), sc)]

    def shard_rows(n, r0, rows):
        shard, _, by_blk, first, size = pieces[n]
        if by_blk:
            return shard.at[pl.ds(al(r0, 16), rows), first:first + size]
        return shard.at[pl.ds(al(first + r0, 16), rows), :]

    zbit = bit(1)
    nxbit, nzbit = 1 - xbit, 1 - zbit
    zpeer = peer_of(1)

    def fourth(n, xb, zb):
        rows = extent(n)[0] // 4
        return (2 * xb + zb) * rows, rows

    def third(n, xb, zb, i):
        r0, rows = fourth(n, xb, zb)
        return r0 + i * (rows // 3), rows // 3

    quarter = p * 2 + b
    for row, ref in enumerate(vectors):
        vecs[quarter, row:row + 1, 0:ref.shape[0]] = ref[...].astype(F32).reshape(1, ref.shape[0])
    at_lane = lax.broadcasted_iota(jnp.int32, (1, DH), 1)
    routes = jnp.zeros((1, DH), F32)
    for i in range(heads // 2):
        here = (at_lane >= i * 64) & (at_lane < (i + 1) * 64)
        routes = jnp.where(here, route[i].astype(F32), routes)
    vecs[quarter, R_LANE:R_LANE + 1, 0:DH] = routes
    cp_x = lc(tokens.at[p], xo)
    own = [lc(shard_rows(n, 0, extent(n)[0]), span(n, p, b, 0, extent(n)[0])) for n in range(NW)]
    cp_cot = lc(cot.at[p], cotb)
    v_c = same(vecs.at[quarter], core)
    v_y = same(vecs.at[quarter], ypeer)
    v_d = same(vecs.at[quarter], diag)
    to_core, to_y, to_y3 = [], [], []
    for n in range(NW):
        to_core.append(rc(shard_rows(n, 0, extent(n)[0]), span(n, p, b, 0, extent(n)[0]), core))
        if n == 2:
            x_c = rc(tokens.at[p], xx, core)
        r = fourth(n, xbit, zbit)
        to_y.append(rc(shard_rows(n, *r), span(n, p, b, *r), ypeer))
        r = third(n, 1 - xbit, 1 - zbit, 0)
        to_y3.append(rc(shard_rows(n, *r), span(n, p, b, *r), ypeer))
    to_x, to_z, to_x3, to_z3 = ([None] * NW for _ in range(4))
    fwd = [[] for _ in range(NW)]

    def passed(n, part, *args):
        return lambda: span(n, 1 - p, b, *part(n, *args))

    def svc_a(n):
        to_y[n].wait_recv()
        src = passed(n, fourth, xbit, zbit)
        to_x[n] = same(src, xpeer)
        to_z[n] = same(src, zpeer)
        fwd[n].append(same(src, core))

    def svc_b(n):
        to_x[n].wait_recv()
        to_z3[n] = same(passed(n, third, nxbit, zbit, 2), zpeer)
        to_z[n].wait_recv()
        to_x3[n] = same(passed(n, third, xbit, nzbit, 1), xpeer)
        fwd[n].append(same(passed(n, fourth, nxbit, zbit), core))
        fwd[n].append(same(passed(n, fourth, xbit, nzbit), core))

    def svc_c(n):
        for cp in (to_y3[n], to_x3[n], to_z3[n]):
            cp.wait_recv()
        fwd[n].append(same(passed(n, fourth, nxbit, nzbit), core))

    def need(n):
        for cp in fwd[n]:
            cp.wait_recv()

    cp_x.wait()
    for cp in (v_c, v_y, v_d):
        cp.wait_recv()
    DQ = D // 4
    for row in (R_BQ, R_BV):
        vecf[row:row + 1, :] = jnp.concatenate([vecs[i, row:row + 1, 0:DQ] for i in range(4)], axis=1)
    for row in BY_BLK:
        vecf[row:row + 1, :] = jnp.concatenate([vecs[i, row:row + 1, 0:DH] for i in range(2)], axis=1)
    vecf[R_LANE:R_LANE + 1, :] = jnp.concatenate([vecs[2 * i, R_LANE:R_LANE + 1, 0:DH] for i in range(2)], axis=1)
    for t in range(FF // D):
        per = D * 4 // FF
        b1r[t] = jnp.concatenate([vecs[i, R_B1:R_B1 + 1, 0:FF // 4] for i in range(t * per, t * per + per)], axis=1)
    for pair in range(heads // 2):
        two = vecf[R_LANE:R_LANE + 1, pair * 128:pair * 128 + 128]
        hrow[2 * pair] = jnp.broadcast_to(two[:, 0:1], (1, 128))
        hrow[2 * pair + 1] = jnp.broadcast_to(two[:, 64:65], (1, 128))
    length = lengths[p]
    pos = lax.broadcasted_iota(jnp.int32, (L, 128), 0)
    for which in range(2):
        start = (b if which == 0 else 1 - b) * L
        biasb[which] = jnp.where(pos + start < length, 0.0, MASKED_SCORE)

    lane = lax.broadcasted_iota(jnp.int32, (1, 128), 1)

    def head_lanes(hh):
        return (lane < 64) if hh == 0 else (lane >= 64)

    def head_bias(head):
        return jnp.where(hrow[head] > 0.5, biasb[1], biasb[0])

    def project(h):
        cols = pl.ds(al(h * DH, 128), DH)
        swapped = vecf[R_LANE:R_LANE + 1, cols] > 0.5
        q[:, cols] = (nn(xo[...], gwq[:, cols]) + vecf[R_BQ:R_BQ + 1, cols]).astype(BF16) * jnp.asarray(0.125, BF16)
        k[:, cols] = jnp.where(swapped, nn(xx[...], gwk[:, cols]), nn(xo[...], gwk[:, cols])).astype(BF16)
        v[:, cols] = (jnp.where(swapped, nn(xx[...], gwv[:, cols]), nn(xo[...], gwv[:, cols]))
                      + vecf[R_BV:R_BV + 1, cols]).astype(BF16)

    def attend(h, j):
        cols = pl.ds(al(h * DH + j * 128, 128), 128)
        kp, vp = k[:, cols], v[:, cols]
        vT = vp.T
        tops = []
        for hh in range(2):
            head = h * (heads // 2) + 2 * j + hh
            km = jnp.where(head_lanes(hh), kp, jnp.zeros_like(kp))
            bias = head_bias(head)
            bias = jnp.concatenate([bias, bias], axis=1)
            parts = []
            for t in range(L // 256):
                s = nt(km, q[t * 256:(t + 1) * 256, cols]) + bias
                peak = jnp.max(s, axis=0, keepdims=True)
                e = jnp.exp(s - peak)
                total = jnp.sum(e, axis=0, keepdims=True)
                lse[head, :, t * 256:(t + 1) * 256] = peak + jnp.log(total)
                parts.append(nn(vT[hh * 64:(hh + 1) * 64, :], e.astype(BF16)) * (1.0 / total))
            tops.append(jnp.concatenate(parts, axis=1))
        c[:, cols] = jnp.concatenate(tops, axis=0).T.astype(BF16)

    def gather(place):
        for kind, n in GATHER[place]:
            {"a": svc_a, "b": svc_b, "c": svc_c}[kind](n)

    def pairs(h, name):
        def one(j, carry):
            attend(h, j)
            for i in range(NP):
                pl.when(j == i)(functools.partial(gather, "%s%d" % (name, i)))
            return carry

        lax.fori_loop(0, NP, one, 0)

    for n in range(3):
        own[n].wait()
        to_core[n].wait_recv()
    x_c.wait_recv()
    project(p)
    gather("project0")
    pairs(p, "own")
    gather("wait")
    own[3].wait()
    to_core[3].wait_recv()
    for n in range(3):
        need(n)
    project(1 - p)
    gather("project1")
    pairs(1 - p, "other")
    need(3)

    acc[...] = nn(c[...], gwo[...])
    TR = 128

    def rows_of(i):
        return pl.ds(al(i * TR, TR), TR)

    def norm1(i, carry):
        r = rows_of(i)
        val = xo[r, :].astype(F32) + (acc[r, :] + vecf[R_BO:R_BO + 1, :])
        centre = val - jnp.mean(val, axis=1, keepdims=True)
        spread = jnp.mean(centre * centre, axis=1, keepdims=True)
        rs = lax.rsqrt(spread + EPSILON)
        xh = centre * rs
        xh1[r, :] = xh
        rs1[r, :] = jnp.broadcast_to(rs, (TR, 128))
        flow[r, :] = (xh * vecf[R_G1:R_G1 + 1, :] + vecf[R_S1:R_S1 + 1, :]).astype(BF16)
        return carry

    lax.fori_loop(0, L // TR, norm1, 0)
    gather("norm")
    tA[...] = flow[...].T

    NT = FH // D

    def ff_tile(h, i, first):
        hid = pl.ds(al(h * FH + i * D, 128), D)
        wide[...] = nn(flow[...], gw1[:, hid])

        def gelu_rows(j, carry):
            r = pl.ds(al(j * 32, 32), 32)
            u = wide[r, :] + b1r[h * NT + i]
            uu = u * u
            th = jnp.tanh(GELU_C * u * (1.0 + 0.044715 * uu))
            half = 0.5 * (1.0 + th)
            act[r, hid] = (u * half).astype(BF16)
            slope = half + 0.5 * u * (1.0 - th * th) * (GELU_C * (1.0 + 3 * 0.044715 * uu))
            dact[r, hid] = slope.astype(BF16)
            return carry

        lax.fori_loop(0, L // 32, gelu_rows, 0)
        out = nn(act[:, hid], gw2[hid, :])
        if first:
            acc[...] = out
        else:
            acc[...] += out

    for n in range(4, NW):
        own[n].wait()
        to_core[n].wait_recv()
    for i in range(NT):
        ff_tile(p, i, i == 0)
        gather("ff_own%d" % i)
    for i in range(NT):
        gather("ff_other%d" % i)
        need(4 + 2 * i)
        need(5 + 2 * i)
        ff_tile(1 - p, i, False)

    cp_cot.wait()
    zero = jnp.zeros((1, D), F32)
    for r0 in range(gv.shape[0]):
        gv[r0:r0 + 1, :] = zero

    def colsum(x):
        return jnp.sum(x, axis=0, keepdims=True)

    def norm2(i, carry):
        dg, ds, db = carry
        r = rows_of(i)
        fo = xh1[r, :] * vecf[R_G1:R_G1 + 1, :] + vecf[R_S1:R_S1 + 1, :]
        val = fo + (acc[r, :] + vecf[R_B2:R_B2 + 1, :])
        centre = val - jnp.mean(val, axis=1, keepdims=True)
        spread = jnp.mean(centre * centre, axis=1, keepdims=True)
        rs = lax.rsqrt(spread + EPSILON)
        xh = centre * rs
        g2 = vecf[R_G2:R_G2 + 1, :]
        lob[r, :] = (xh * g2 + vecf[R_S2:R_S2 + 1, :]).astype(BF16)
        up = cotb[r, :].astype(F32)
        dxh = up * g2
        gin = rs * (dxh - jnp.mean(dxh, axis=1, keepdims=True) - xh * jnp.mean(dxh * xh, axis=1, keepdims=True))
        acc[r, :] = gin
        low = gin.astype(BF16)
        go[r, :] = low
        return dg + colsum(up * xh), ds + colsum(up), db + colsum(low.astype(F32))

    dg, ds, db = lax.fori_loop(0, L // TR, norm2, (zero, zero, zero))
    gv[R_G2:R_G2 + 1, :] = dg
    gv[R_S2:R_S2 + 1, :] = ds
    gv[R_B2:R_B2 + 1, :] = db
    lo_local = lc(lob, layer_out.at[p])
    lo_y = []

    def lo_send(parts):
        for i in parts:
            part = pl.ds(i * (L // 4), L // 4)
            lo_y.append(rc(lob.at[part], layer_out.at[p, part], ypeer))

    lo_send(range(LO_FIRST))

    tB[...] = go[...].T
    keep_rows = pl.ds(al(b * DH, 128), DH)
    send_rows = pl.ds(al((1 - b) * DH, 128), DH)

    table = unit_table(DH, FH, D)
    units = []
    n_res = sum(order[0] != "y" for _, _, order in table)
    landing, landing_res = landing[:len(landing) - n_res], landing[len(landing) - n_res:]
    for col, width, order in table:
        order = [axis for axis in order if axis == "y" or axis < dp_bits]
        bufs = [landing.pop(0) for _ in range(len(order) + max(dp_bits - 3, 0))]
        units.append({"at": slice(col, col + width), "order": order, "bufs": bufs, "next": 0, "r0": 0, "rows": DH,
                      "both": True, "core": [None, None], "copy": None, "path": []})
        units[-1]["res"] = bufs[0] if order[0] == "y" else landing_res.pop(0)

    def core_send(u, src, h_is_own):
        h = p if h_is_own else 1 - p
        units[u]["core"][h_is_own] = rc(src, rcore.at[h, :, units[u]["at"]], core)

    def add_block(h, r0, rows, at, src):
        step = 48 if rows % 48 == 0 else rows

        def one(i, carry):
            here = pl.ds(al(r0 + i * step, 16), step)
            gk[h, here, at] = (gk[h, here, at].astype(F32) + src(pl.ds(al(i * step, 16), step)).astype(F32)).astype(BF16)
            return carry

        lax.fori_loop(0, rows // step, one, 0)

    def start_stage(u, s):
        un = units[u]
        axis, buf, at = un["order"][s], un["bufs"][s], un["at"]
        if axis == "y":
            here = pl.ds(al(un["r0"], 16), un["rows"])
            un["copy"] = rc(gk.at[1 - p, here, at], buf.at[0], ypeer)
            un["both"] = False
            return
        rows = un["rows"] // 2
        away = pl.ds(al(un["r0"] + (1 - bit(axis)) * rows, 16), rows)
        src = gk.at[:, away, at] if un["both"] else gk.at[pl.ds(p, 1), away, at]
        un["copy"] = rc(src, buf, peer_of(axis))
        un["path"].append((axis, un["r0"], un["rows"]))
        un["r0"] = un["r0"] + bit(axis) * rows
        un["rows"] = rows

    def step(u):
        un = units[u]
        ev, n, at = un["next"], len(un["order"]), un["at"]
        un["next"] += 1
        if ev == 0:
            for own in (0,) if un["order"][0] == "y" else (0, 1):
                un["core"][own].wait_recv()
                h = p if own else 1 - p
                add_block(h, 0, DH, at, lambda r, h=h: rcore[h, r, at])
            start_stage(u, 0)
            return
        un["copy"].wait_recv()
        if ev <= n:
            buf = un["bufs"][ev - 1]
            if ev == 1 and un["order"][0] == "y":
                un["core"][1].wait_recv()
                add_block(p, 0, DH, at, lambda r: rcore[p, r, at].astype(F32) + buf[0, r, :].astype(F32))
            elif un["both"]:
                for h in range(2):
                    add_block(h, un["r0"], un["rows"], at, lambda r, h=h: buf[h, r, :])
            else:
                add_block(p, un["r0"], un["rows"], at, lambda r: buf[0, r, :])
            if ev < n:
                start_stage(u, ev)
                return
            for t in range(3, dp_bits):
                buf = un["bufs"][n + t - 3]
                mine = gk.at[pl.ds(p, 1), pl.ds(al(un["r0"], 16), un["rows"]), at]
                cp = rc(mine, buf, peer_of(t))
                cp.wait_recv()
                cp.wait_send()
                waited.append(id(cp))
                add_block(p, un["r0"], un["rows"], at, lambda r: buf[0, r, :])
            here = pl.ds(al(un["r0"], 16), un["rows"])
            un["res"][0, here, :] = gk[p, here, at]
        if un["path"]:
            axis, r0, rows = un["path"].pop()
            mine = un["res"].at[0, pl.ds(al(un["r0"], 16), un["rows"])]
            un["copy"] = rc(mine, mine, peer_of(axis))
            un["r0"], un["rows"] = r0, rows
            return
        un["out"] = lc(un["res"].at[0], gk_out.at[:, at])

    def events(place):
        for u in EVENTS[place]:
            if u < len(units):
                step(u)
            else:
                vec_step()

    def weight_grad(leftT, right, send, own, col, width):
        h = p if own else 1 - p
        send[...] = nn(leftT[send_rows, :], right).astype(BF16)
        gk[h, :, col:col + width] = nn(leftT[keep_rows, :], right).astype(BF16)

    def ff_back(own, i):
        h = p if own else 1 - p
        hid = pl.ds(al(h * FH + i * D, 128), D)
        du = (nt(go[...], gw2[hid, :]) * dact[:, hid].astype(F32)).astype(BF16)
        gb1[h * NT + i] = colsum(du.astype(F32))
        dact[:, hid] = du
        acc[...] += nt(dact[:, hid], gw1[:, hid])
        for u, leftT, side in ((2 * i, tA, dact), (2 * i + 1, tB, act)):
            send = side.at[0:DH, hid]
            weight_grad(leftT, side[:, hid], send, own, table[u][0], D)
            core_send(u, send, own)

    for i in range(NT):
        for own in (0, 1):
            ff_back(own, i)
            events("ff%d%d" % (i, own))
    if LO_PLACE == "ff":
        lo_send(range(LO_FIRST, 4))
    for t in range(FF // D):
        gv[R_B1 + t:R_B1 + t + 1, :] = gb1[t]

    def norm1_back(i, carry):
        dg, ds, db = carry
        r = rows_of(i)
        up = acc[r, :]
        xh = xh1[r, :]
        dxh = up * vecf[R_G1:R_G1 + 1, :]
        gin = rs1[r, 0:1] * (dxh - jnp.mean(dxh, axis=1, keepdims=True) - xh * jnp.mean(dxh * xh, axis=1, keepdims=True))
        acc[r, :] = gin
        low = gin.astype(BF16)
        go[r, :] = low
        return dg + colsum(up * xh), ds + colsum(up), db + colsum(low.astype(F32))

    dg, ds, db = lax.fori_loop(0, L // TR, norm1_back, (zero, zero, zero))
    gv[R_G1:R_G1 + 1, :] = dg
    gv[R_S1:R_S1 + 1, :] = ds
    gv[R_BO:R_BO + 1, :] = db
    tB[...] = go[...].T
    UO = 2 * NT
    events("n1")
    if LO_PLACE == "n1":
        lo_send(range(LO_FIRST, 4))
    for u in range(UO):
        for cp in units[u]["core"]:
            cp.wait_send()
            waited.append(id(cp))
    dc[...] = nt(go[...], gwo[...]).astype(BF16)
    tail = 2 * FH

    def part(n, h):
        return dact.at[0:DH, pl.ds(al(D + (n % 3 * 2 + h) * DH, 128), DH)]

    for own in (0, 1):
        h = p if own else 1 - p
        weight_grad(tB, c[:, pl.ds(al(h * DH, 128), DH)], part(0, h), own, tail, DH)
        core_send(UO, part(0, h), own)
    events("wo")
    tA[...] = xo[...].T
    tB[...] = xx[...].T

    def attend_back(j, carry):
        cols = pl.ds(al(j * 128, 128), 128)
        kp, vp, qp, dcp = k[:, cols], v[:, cols], q[:, cols], dc[:, cols]
        kT = kp.T
        dkv = [jnp.zeros((L, 128), F32), jnp.zeros((L, 128), F32)]
        tops = []
        for hh in range(2):
            head = 2 * j + hh
            mine = head_lanes(hh)
            none = jnp.zeros_like(kp)
            km, vm = jnp.where(mine, kp, none), jnp.where(mine, vp, none)
            qm, dcm = jnp.where(mine, qp, none), jnp.where(mine, dcp, none)
            bias = head_bias(head)
            bias = jnp.concatenate([bias, bias], axis=1)
            parts = []
            for t in range(L // 256):
                ts = slice(t * 256, (t + 1) * 256)
                prob = jnp.exp(nt(km, qp[ts]) + bias - lse[head, :, ts])
                dprob = nt(vm, dcp[ts])
                delta = jnp.sum(prob * dprob, axis=0, keepdims=True)
                dscore = (prob * (dprob - delta)).astype(BF16)
                dkv[1] += nn(prob.astype(BF16), dcm[ts])
                dkv[0] += nn(dscore, qm[ts])
                parts.append(nn(kT[hh * 64:(hh + 1) * 64, :], dscore))
            tops.append(jnp.concatenate(parts, axis=1))
        dq[:, cols] = (jnp.concatenate(tops, axis=0).T * 0.125).astype(BF16)
        dk[:, cols] = dkv[0].astype(BF16)
        dv[:, cols] = dkv[1].astype(BF16)
        return carry

    for i in range(3):
        lax.fori_loop(i * NP * 2 // 3, (i + 1) * NP * 2 // 3, attend_back, 0)
        events("ab%d" % i)
    if LO_PLACE == "ab":
        lo_send(range(LO_FIRST, 4))
    gv[R_BQ:R_BQ + 1, :] = colsum(dq[...].astype(F32))
    gv[R_BV:R_BV + 1, :] = colsum(dv[...].astype(F32))

    vec_peers = [core, ypeer] + [peer_of(t) for t in range(dp_bits)]
    vstate = {"s": 0, "cp": None, "done": False}
    gvr[0, 0] = gv[...]

    def vec_step():
        s = vstate["s"]
        if s > 0:
            vstate["cp"].wait_recv()
            total = gvr[s - 1, 0] + gvr[s - 1, 1]
            if s == len(vec_peers):
                gv[...] = total
                vstate["done"] = True
                return
            gvr[s, 0] = total
        vstate["cp"] = rc(gvr.at[s, 0], gvr.at[s, 1], vec_peers[s])
        vstate["s"] = s + 1

    vec_step()

    swapped = vecf[R_LANE:R_LANE + 1, :] > 0.5
    none = jnp.zeros((L, D), BF16)
    dc[...] = jnp.where(swapped, dk[...], none)
    flow[...] = jnp.where(swapped, dv[...], none)
    dk[...] = jnp.where(swapped, none, dk[...])
    dv[...] = jnp.where(swapped, none, dv[...])
    backs[...] = (nt(dc[...], gwk[...]) + nt(flow[...], gwv[...])).astype(BF16)
    back_c = rc(backs, backr, core)
    for n, (a, x) in enumerate(((dq, None), (dk, dc), (dv, flow))):
        u = UO + 1 + n
        for own in (0, 1):
            h = p if own else 1 - p
            hs = pl.ds(al(h * DH, 128), DH)
            if n == 2:
                units[UO]["core"][own].wait_send()
                waited.append(id(units[UO]["core"][own]))
            send = part(1 + n, h)
            for dst, rows in ((send, send_rows), (gk.at[h, :, table[u][0]:table[u][0] + DH], keep_rows)):
                val = nn(tA[rows, :], a[:, hs])
                if x is not None:
                    val = val + nn(tB[rows, :], x[:, hs])
                dst[...] = val.astype(BF16)
            core_send(u, send, own)
        events("q%d" % (5 + n))
    acc[...] += nt(dq[...], gwq[...]) + nt(dk[...], gwk[...]) + nt(dv[...], gwv[...])
    events("acc")
    lo_local.wait()
    back_c.wait_recv()
    for r0 in range(0, L, TR):
        acc[r0:r0 + TR, :] += backr[r0:r0 + TR, :].astype(F32)
    xo[...] = acc[...].astype(BF16)
    gt_local = lc(xo, grad_tokens.at[p])
    gt_y = rc(xo, grad_tokens.at[p], ypeer)
    if LO_PLACE == "end":
        lo_send(range(LO_FIRST, 4))
    events("drain")
    while not vstate["done"]:
        vec_step()
    for un in units:
        un["out"].wait()
    gt_local.wait()
    gt_y.wait_recv()
    for cp in lo_y:
        cp.wait_recv()
    for cp in sent:
        if id(cp) not in waited:
            cp.wait_send()


def finish_kernel(
    lo, gt, gk, gv,
    lo_out, gt_out, g_wq, g_bq, g_wk, g_wv, g_bv, g_wo, g_bo, g_g1, g_s1, g_w1, g_b1, g_w2, g_b2, g_g2, g_s2,
    low, wide, held, sem_in, sem_out,
):
    p, b = lax.axis_index("perm"), lax.axis_index("blk")
    D = gv.shape[1]
    DH, FH = D // 2, g_w1.shape[1]
    n_cols = gk.shape[1] // DH
    loads = [pltpu.make_async_copy(gk.at[:, i * DH:(i + 1) * DH], low.at[i], sem_in.at[i]) for i in range(n_cols)]
    for load in loads:
        load.start()
    through = [pltpu.make_async_copy(src, held.at[i], sem_in.at[n_cols + i]) for i, src in enumerate((lo, gt))]
    for move in through:
        move.start()
    stores = []
    per = FH // DH
    for i in range(n_cols):
        loads[i].wait()
        if i == per:
            for j, dst in enumerate((lo_out, gt_out)):
                through[j].wait()
                stores.append(pltpu.make_async_copy(held.at[j], dst, sem_out.at[n_cols + j]))
                stores[-1].start()
        value = low[i].T if per <= i <= 2 * per else low[i]
        wide[i] = value.astype(F32)
        if i < per:
            dst = g_w1.at[:, i * DH:(i + 1) * DH]
        elif i < 2 * per:
            dst = g_w2.at[(i - per) * DH:(i - per + 1) * DH, :]
        else:
            dst = (g_wo, g_wq, g_wk, g_wv)[i - 2 * per]
        stores.append(pltpu.make_async_copy(wide.at[i], dst, sem_out.at[i]))
        stores[-1].start()

    def put(ref, row):
        ref[...] = row.reshape(ref.shape)

    for row, ref in ((R_BO, g_bo), (R_G1, g_g1), (R_S1, g_s1), (R_B2, g_b2), (R_G2, g_g2), (R_S2, g_s2)):
        put(ref, jnp.where(b == 0, gv[row:row + 1, 0:DH], gv[row:row + 1, DH:D]))
    for row, ref in ((R_BQ, g_bq), (R_BV, g_bv)):
        n = D // 4
        left = jnp.where(b == 0, gv[row:row + 1, 0:n], gv[row:row + 1, n:2 * n])
        right = jnp.where(b == 0, gv[row:row + 1, 2 * n:3 * n], gv[row:row + 1, 3 * n:D])
        put(ref, jnp.where(p == 0, left, right))
    left = jnp.where(b == 0, gv[R_B1:R_B1 + 1, :], gv[R_B1 + 1:R_B1 + 2, :])
    right = jnp.where(b == 0, gv[R_B1 + 2:R_B1 + 3, :], gv[R_B1 + 3:R_B1 + 4, :])
    put(g_b1, jnp.where(p == 0, left, right))
    for store in stores:
        store.wait()


def per_device(
    tokens, lengths, head_route, w_query, b_query, w_key, w_value, b_value, w_out, b_out,
    first_gain, first_shift, w_inner, b_inner, w_outer, b_outer, second_gain, second_shift, cotangent,
):
    L, D = tokens.shape[1:]
    FF = w_inner.shape[1] * 2
    heads = head_route.shape[0] * 2

    bits = (lax.axis_size("dp") - 1).bit_length()

    half = FF + 4 * (D // 2)
    any_ = pl.BlockSpec(memory_space=pl.ANY)
    vm = pl.BlockSpec(memory_space=pltpu.VMEM)
    smem = pl.BlockSpec(memory_space=pltpu.SMEM)
    V = pltpu.VMEM
    layer_out, grad_tokens, reduced, vectors = pl.pallas_call(
        functools.partial(layer_kernel, heads, lax.axis_size("dp")),
        out_shape=(
            jax.ShapeDtypeStruct(tokens.shape, BF16),
            jax.ShapeDtypeStruct(tokens.shape, BF16),
            jax.ShapeDtypeStruct((D // 2, half), BF16),
            jax.ShapeDtypeStruct((16, D), F32),
        ),
        in_specs=[any_, any_, smem, smem] + [any_] * 6 + [vm] * 9,
        out_specs=(any_, any_, any_, vm),
        scratch_shapes=[
            V((L, D), BF16), V((L, D), BF16), V((L, D), BF16),
            V((D, D), BF16), V((D, D), BF16), V((D, D), BF16), V((D, D), BF16), V((D, FF), BF16), V((FF, D), BF16),
            V((4, 16, D), F32), V((16, D), F32), V((2, L, 128), F32),
            V((L, D), BF16), V((L, D), BF16), V((L, D), BF16), V((L, D), BF16),
            V((L, D), BF16), V((L, D), F32), V((L, 128), F32), V((16, 1, L), F32),
            V((L, FF), BF16), V((L, FF), BF16), V((L, D), F32), V((L, D), BF16),
            V((D, L), BF16), V((D, L), BF16), V((L, D), BF16),
            V((L, D), F32), V((L, D), BF16),
            V((16, 1, 128), F32), V((FF // D, 1, D), F32), V((FF // D, 1, D), F32),
            V((2, D // 2, half), BF16), V((2, D // 2, half), BF16),
            V((2 + bits, 2, 16, D), F32),
        ] + [V(shape, BF16) for shape in stage_shapes(unit_table(D // 2, FF // 2, D), D // 2, bits)] + [
            pltpu.SemaphoreType.DMA((32,)),
            pltpu.SemaphoreType.DMA((256,)),
            pltpu.SemaphoreType.DMA((256,)),
        ],
        compiler_params=pltpu.CompilerParams(collective_id=0, has_side_effects=True, vmem_limit_bytes=62 * 2**20),
        name="layer",
    )(tokens, cotangent, lengths, head_route, w_query, w_key, w_value, w_out, w_inner, w_outer,
      b_query, b_value, b_out, first_gain, first_shift, b_outer, second_gain, second_shift, b_inner)

    DH, FH = D // 2, FF // 2
    shapes = [(DH, DH), (D // 4,), (DH, DH), (DH, DH), (D // 4,), (DH, DH), (DH,), (DH,), (DH,), (DH, FH),
              (FF // 4,), (FH, DH), (DH,), (DH,), (DH,)]
    moved = [jax.ShapeDtypeStruct(tokens.shape, BF16)] * 2
    n_cols = half // DH
    return tuple(pl.pallas_call(
        finish_kernel,
        out_shape=moved + [jax.ShapeDtypeStruct(shape, F32) for shape in shapes],
        in_specs=[any_, any_, any_, vm],
        out_specs=[any_, any_] + [any_ if len(shape) == 2 else vm for shape in shapes],
        scratch_shapes=[V((n_cols, DH, DH), BF16), V((n_cols, DH, DH), F32), V((2,) + tokens.shape, BF16),
                        pltpu.SemaphoreType.DMA((n_cols + 2,)), pltpu.SemaphoreType.DMA((n_cols + 2,))],
        compiler_params=pltpu.CompilerParams(vmem_limit_bytes=62 * 2**20),
        name="finish",
    )(layer_out, grad_tokens, reduced, vectors))


def solution(mesh):
    placed = (
        P("dp", "blk", None), P("dp"), P("perm"), P("blk", "perm"), P(("perm", "blk")), P("blk", "perm"),
        P("blk", "perm"), P(("perm", "blk")), P("perm", "blk"), P("blk"), P("blk"), P("blk"), P("blk", "perm"),
        P(("perm", "blk")), P("perm", "blk"), P("blk"), P("blk"), P("blk"), P("dp", "blk", None),
    )
    outs = (
        P("dp", "blk", None), P("dp", "blk", None), P("blk", "perm"), P(("perm", "blk")), P("blk", "perm"),
        P("blk", "perm"), P(("perm", "blk")), P("perm", "blk"), P("blk"), P("blk"), P("blk"), P("blk", "perm"),
        P(("perm", "blk")), P("perm", "blk"), P("blk"), P("blk"), P("blk"),
    )
    return jax.shard_map(per_device, mesh=mesh, in_specs=placed, out_specs=outs, check_vma=False)
```

```python
import functools
import math

import jax
import jax.numpy as jnp
from jax import lax
from jax.experimental import pallas as pl
from jax.experimental.pallas import tpu as pltpu
from jax.sharding import PartitionSpec as P

EPSILON = 1e-05
MASKED_SCORE = -1e30
MESH = pl.DeviceIdType.MESH
F32 = jnp.float32
BF16 = jnp.bfloat16
GELU_C = math.sqrt(2.0 / math.pi)


def nn(left, right):
    return lax.dot_general(left, right, (((1,), (0,)), ((), ())), preferred_element_type=F32)


def nt(left, right):
    return lax.dot_general(left, right, (((1,), (1,)), ((), ())), preferred_element_type=F32)


def al(value, multiple):
    return pl.multiple_of(value, multiple)


R_BQ, R_BV, R_BO, R_G1, R_S1, R_B2, R_G2, R_S2, R_B1, R_LANE = 0, 1, 2, 3, 4, 5, 6, 7, 8, 12
BY_BLK = (R_BO, R_G1, R_S1, R_B2, R_G2, R_S2)

ORDERS = (
    ("y", 0, 1, 2),
    (0, 1, "y", 2),
    (1, 0, "y", 2),
    ("y", 0, 1, 2),
    ("y", 1, 0, 2),
    ("y", 0, 1, 2),
    ("y", 0, 1, 2),
    ("y", 0, 1, 2),
)
EVENTS = {
    "ff00": (),
    "ff01": (0,),
    "ff10": (1,),
    "ff11": (3,),
    "n1": (2,),
    "wo": (),
    "ab0": (0, 4),
    "ab1": (1,),
    "ab2": (0, 3, 2),
    "q5": (8,),
    "q6": (4, 1, 5, 8, 6, 0),
    "q7": (3,),
    "acc": (0, 4, 1, 7, 8, 3, 2),
        "drain": (5, 4, 0, 8, 1, 6, 5, 3, 0, 4, 6, 8, 7, 5, 1, 2, 6, 0, 3, 4, 1, 7, 5, 4, 2, 3, 6, 7, 5, 1, 4, 2, 6,
        7, 3, 5, 6, 7, 2, 7, 5, 6, 2, 7),
}
GATHER = {
    "project0": (("a", 0), ("a", 1),),
    "own0": (("a", 2),),
    "own1": (("a", 3), ("b", 0),),
    "own2": (("b", 1),),
    "wait": (("b", 2), ("a", 4), ("b", 3), ("c", 0), ("c", 1), ("c", 2), ("a", 5),),
    "project1": (),
    "other0": (("b", 4), ("c", 3),),
    "other1": (("a", 6), ("b", 5),),
    "other2": (("c", 4),),
    "norm": (("a", 7),),
    "ff_own0": (("b", 6), ("c", 5),),
    "ff_own1": (("b", 7),),
    "ff_other0": (),
    "ff_other1": (("c", 6), ("c", 7),),
}
LO_FIRST, LO_PLACE = 2, "end"


def unit_table(DH, FH, D):
    tail = 2 * FH
    table = []
    for i in range(FH // D):
        table += [(i * D, D), (FH + i * D, D)]
    table += [(tail + i * DH, DH) for i in range(4)]
    return [(col, width, order) for (col, width), order in zip(table, ORDERS)]


def stage_shapes(table, DH, bits):
    shapes = []
    for col, width, order in table:
        rows, halves = DH, 2
        for axis in order:
            if axis == "y":
                halves = 1
            elif axis < bits:
                rows //= 2
            else:
                continue
            shapes.append((halves, rows, width))
        for _ in range(bits - 3):
            shapes.append((1, rows, width))
    shapes += [(1, DH, width) for _, width, order in table if order[0] != "y"]
    return shapes


def layer_kernel(
    heads, dp_size,
    tokens, cot, lengths, route, wq, wk, wv, wo, w1, w2, *rest,
):
    vectors, (layer_out, grad_tokens, gk_out, gv), rest = rest[:9], rest[9:13], rest[13:]
    (xo, xx, cotb, gwq, gwk, gwv, gwo, gw1, gw2, vecs, vecf, biasb,
     q, k, v, c, flow, xh1, rs1, lse, act, dact, acc, go, tA, tB, lob, wide, backr, hrow, b1r, gb1,
     gk, rcore, gvr), rest = rest[:35], rest[35:]
    sem_l, sem_s, sem_r = rest[-3:]
    landing, landing_res = list(rest[:-3]), []
    d, p, b = lax.axis_index("dp"), lax.axis_index("perm"), lax.axis_index("blk")
    D = xo.shape[1]
    L = xo.shape[0]
    FF = gw2.shape[0]
    DH, FH = D // 2, FF // 2
    NP = heads // 4
    xbit = lax.rem(d, 2)
    dq, dk, dv, dc = (act.at[:, i * D:(i + 1) * D] for i in range(4))
    backs = dact.at[:, 0:D]
    core, ypeer, diag = (d, p, 1 - b), (d, 1 - p, b), (d, 1 - p, 1 - b)
    dp_bits = (dp_size - 1).bit_length()

    def bit(t):
        return lax.rem(lax.div(d, 2**t), 2)

    def peer_of(t):
        return (d + 2**t - 2 ** (t + 1) * bit(t), p, b)

    xpeer = peer_of(0)

    bar = pltpu.get_barrier_semaphore()
    peers = (core, ypeer, diag) + tuple(peer_of(t) for t in range(dp_bits))
    for peer in peers:
        pl.semaphore_signal(bar, 1, device_id=peer, device_id_type=MESH)
    pl.semaphore_wait(bar, len(peers))

    count = [0]
    sent = []
    waited = []

    class Copy:
        def __init__(self, src, dst, peer):
            self.index, self.src, self.dst, self.peer = count[0], src, dst, peer
            count[0] += 1
            self.make().start()
            sent.append(self)

        def make(self):
            src = self.src() if callable(self.src) else self.src
            dst = self.dst() if callable(self.dst) else self.dst
            return pltpu.make_async_remote_copy(
                src_ref=src, dst_ref=dst, send_sem=sem_s.at[self.index], recv_sem=sem_r.at[self.index],
                device_id=self.peer, device_id_type=MESH)

        def wait_recv(self):
            self.make().wait_recv()

        def wait_send(self):
            self.make().wait_send()

    rc = Copy

    def same(ref, peer):
        return rc(ref, ref, peer)

    nl = [0]

    def lc(src, dst):
        i = nl[0]
        nl[0] += 1
        cp = pltpu.make_async_copy(src, dst, sem_l.at[i])
        cp.start()
        return cp

    pieces = [(wq, gwq, True, 0, wq.shape[1]), (wk, gwk, True, 0, wk.shape[1]), (wv, gwv, True, 0, wv.shape[1]),
              (wo, gwo, False, 0, wo.shape[0])]
    for i in range(FH // D):
        pieces += [(w1, gw1, True, i * D, D), (w2, gw2, False, i * D, D)]
    NW = len(pieces)

    def extent(n):
        shard, _, by_blk, _, size = pieces[n]
        return (shard.shape[0], size) if by_blk else (size, shard.shape[1])

    def span(n, pp, bb, r0, rows):
        shard, full, by_blk, first, size = pieces[n]
        sr, sc = shard.shape
        if by_blk:
            return full.at[pl.ds(al(bb * sr + r0, 16), rows), pl.ds(al(pp * sc + first, 128), size)]
        return full.at[pl.ds(al(pp * sr + first + r0, 16), rows), pl.ds(al(bb * sc, 128), sc)]

    def shard_rows(n, r0, rows):
        shard, _, by_blk, first, size = pieces[n]
        if by_blk:
            return shard.at[pl.ds(al(r0, 16), rows), first:first + size]
        return shard.at[pl.ds(al(first + r0, 16), rows), :]

    zbit = bit(1)
    nxbit, nzbit = 1 - xbit, 1 - zbit
    zpeer = peer_of(1)

    def fourth(n, xb, zb):
        rows = extent(n)[0] // 4
        return (2 * xb + zb) * rows, rows

    def third(n, xb, zb, i):
        r0, rows = fourth(n, xb, zb)
        return r0 + i * (rows // 3), rows // 3

    quarter = p * 2 + b
    for row, ref in enumerate(vectors):
        vecs[quarter, row:row + 1, 0:ref.shape[0]] = ref[...].astype(F32).reshape(1, ref.shape[0])
    at_lane = lax.broadcasted_iota(jnp.int32, (1, DH), 1)
    routes = jnp.zeros((1, DH), F32)
    for i in range(heads // 2):
        here = (at_lane >= i * 64) & (at_lane < (i + 1) * 64)
        routes = jnp.where(here, route[i].astype(F32), routes)
    vecs[quarter, R_LANE:R_LANE + 1, 0:DH] = routes
    cp_x = lc(tokens.at[p], xo)
    own = [lc(shard_rows(n, 0, extent(n)[0]), span(n, p, b, 0, extent(n)[0])) for n in range(NW)]
    cp_cot = lc(cot.at[p], cotb)
    v_c = same(vecs.at[quarter], core)
    v_y = same(vecs.at[quarter], ypeer)
    v_d = same(vecs.at[quarter], diag)
    to_core, to_y, to_y3 = [], [], []
    for n in range(NW):
        to_core.append(rc(shard_rows(n, 0, extent(n)[0]), span(n, p, b, 0, extent(n)[0]), core))
        if n == 2:
            x_c = rc(tokens.at[p], xx, core)
        r = fourth(n, xbit, zbit)
        to_y.append(rc(shard_rows(n, *r), span(n, p, b, *r), ypeer))
        r = third(n, 1 - xbit, 1 - zbit, 0)
        to_y3.append(rc(shard_rows(n, *r), span(n, p, b, *r), ypeer))
    to_x, to_z, to_x3, to_z3 = ([None] * NW for _ in range(4))
    fwd = [[] for _ in range(NW)]

    def passed(n, part, *args):
        return lambda: span(n, 1 - p, b, *part(n, *args))

    def svc_a(n):
        to_y[n].wait_recv()
        src = passed(n, fourth, xbit, zbit)
        to_x[n] = same(src, xpeer)
        to_z[n] = same(src, zpeer)
        fwd[n].append(same(src, core))

    def svc_b(n):
        to_x[n].wait_recv()
        to_z3[n] = same(passed(n, third, nxbit, zbit, 2), zpeer)
        to_z[n].wait_recv()
        to_x3[n] = same(passed(n, third, xbit, nzbit, 1), xpeer)
        fwd[n].append(same(passed(n, fourth, nxbit, zbit), core))
        fwd[n].append(same(passed(n, fourth, xbit, nzbit), core))

    def svc_c(n):
        for cp in (to_y3[n], to_x3[n], to_z3[n]):
            cp.wait_recv()
        fwd[n].append(same(passed(n, fourth, nxbit, nzbit), core))

    def need(n):
        for cp in fwd[n]:
            cp.wait_recv()

    cp_x.wait()
    for cp in (v_c, v_y, v_d):
        cp.wait_recv()
    DQ = D // 4
    for row in (R_BQ, R_BV):
        vecf[row:row + 1, :] = jnp.concatenate([vecs[i, row:row + 1, 0:DQ] for i in range(4)], axis=1)
    for row in BY_BLK:
        vecf[row:row + 1, :] = jnp.concatenate([vecs[i, row:row + 1, 0:DH] for i in range(2)], axis=1)
    vecf[R_LANE:R_LANE + 1, :] = jnp.concatenate([vecs[2 * i, R_LANE:R_LANE + 1, 0:DH] for i in range(2)], axis=1)
    for t in range(FF // D):
        per = D * 4 // FF
        b1r[t] = jnp.concatenate([vecs[i, R_B1:R_B1 + 1, 0:FF // 4] for i in range(t * per, t * per + per)], axis=1)
    for pair in range(heads // 2):
        two = vecf[R_LANE:R_LANE + 1, pair * 128:pair * 128 + 128]
        hrow[2 * pair] = jnp.broadcast_to(two[:, 0:1], (1, 128))
        hrow[2 * pair + 1] = jnp.broadcast_to(two[:, 64:65], (1, 128))
    length = lengths[p]
    pos = lax.broadcasted_iota(jnp.int32, (L, 128), 0)
    for which in range(2):
        start = (b if which == 0 else 1 - b) * L
        biasb[which] = jnp.where(pos + start < length, 0.0, MASKED_SCORE)

    lane = lax.broadcasted_iota(jnp.int32, (1, 128), 1)

    def head_lanes(hh):
        return (lane < 64) if hh == 0 else (lane >= 64)

    def head_bias(head):
        return jnp.where(hrow[head] > 0.5, biasb[1], biasb[0])

    def project(h):
        cols = pl.ds(al(h * DH, 128), DH)
        swapped = vecf[R_LANE:R_LANE + 1, cols] > 0.5
        q[:, cols] = (nn(xo[...], gwq[:, cols]) + vecf[R_BQ:R_BQ + 1, cols]).astype(BF16) * jnp.asarray(0.125, BF16)
        k[:, cols] = jnp.where(swapped, nn(xx[...], gwk[:, cols]), nn(xo[...], gwk[:, cols])).astype(BF16)
        v[:, cols] = (jnp.where(swapped, nn(xx[...], gwv[:, cols]), nn(xo[...], gwv[:, cols]))
                      + vecf[R_BV:R_BV + 1, cols]).astype(BF16)

    def attend(h, j):
        cols = pl.ds(al(h * DH + j * 128, 128), 128)
        kp, vp = k[:, cols], v[:, cols]
        vT = vp.T
        tops = []
        for hh in range(2):
            head = h * (heads // 2) + 2 * j + hh
            km = jnp.where(head_lanes(hh), kp, jnp.zeros_like(kp))
            bias = head_bias(head)
            bias = jnp.concatenate([bias, bias], axis=1)
            parts = []
            for t in range(L // 256):
                s = nt(km, q[t * 256:(t + 1) * 256, cols]) + bias
                peak = jnp.max(s, axis=0, keepdims=True)
                e = jnp.exp(s - peak)
                total = jnp.sum(e, axis=0, keepdims=True)
                lse[head, :, t * 256:(t + 1) * 256] = peak + jnp.log(total)
                parts.append(nn(vT[hh * 64:(hh + 1) * 64, :], e.astype(BF16)) * (1.0 / total))
            tops.append(jnp.concatenate(parts, axis=1))
        c[:, cols] = jnp.concatenate(tops, axis=0).T.astype(BF16)

    def gather(place):
        for kind, n in GATHER[place]:
            {"a": svc_a, "b": svc_b, "c": svc_c}[kind](n)

    def pairs(h, name):
        def one(j, carry):
            attend(h, j)
            for i in range(NP):
                pl.when(j == i)(functools.partial(gather, "%s%d" % (name, i)))
            return carry

        lax.fori_loop(0, NP, one, 0)

    for n in range(3):
        own[n].wait()
        to_core[n].wait_recv()
    x_c.wait_recv()
    project(p)
    gather("project0")
    pairs(p, "own")
    gather("wait")
    own[3].wait()
    to_core[3].wait_recv()
    for n in range(3):
        need(n)
    project(1 - p)
    gather("project1")
    pairs(1 - p, "other")
    need(3)

    acc[...] = nn(c[...], gwo[...])
    TR = 128

    def rows_of(i):
        return pl.ds(al(i * TR, TR), TR)

    def norm1(i, carry):
        r = rows_of(i)
        val = xo[r, :].astype(F32) + (acc[r, :] + vecf[R_BO:R_BO + 1, :])
        centre = val - jnp.mean(val, axis=1, keepdims=True)
        spread = jnp.mean(centre * centre, axis=1, keepdims=True)
        rs = lax.rsqrt(spread + EPSILON)
        xh = centre * rs
        xh1[r, :] = xh
        rs1[r, :] = jnp.broadcast_to(rs, (TR, 128))
        flow[r, :] = (xh * vecf[R_G1:R_G1 + 1, :] + vecf[R_S1:R_S1 + 1, :]).astype(BF16)
        return carry

    lax.fori_loop(0, L // TR, norm1, 0)
    gather("norm")
    tA[...] = flow[...].T

    NT = FH // D

    def ff_tile(h, i, first):
        hid = pl.ds(al(h * FH + i * D, 128), D)
        wide[...] = nn(flow[...], gw1[:, hid])

        def gelu_rows(j, carry):
            r = pl.ds(al(j * 32, 32), 32)
            u = wide[r, :] + b1r[h * NT + i]
            uu = u * u
            th = jnp.tanh(GELU_C * u * (1.0 + 0.044715 * uu))
            half = 0.5 * (1.0 + th)
            act[r, hid] = (u * half).astype(BF16)
            slope = half + 0.5 * u * (1.0 - th * th) * (GELU_C * (1.0 + 3 * 0.044715 * uu))
            dact[r, hid] = slope.astype(BF16)
            return carry

        lax.fori_loop(0, L // 32, gelu_rows, 0)
        out = nn(act[:, hid], gw2[hid, :])
        if first:
            acc[...] = out
        else:
            acc[...] += out

    for n in range(4, NW):
        own[n].wait()
        to_core[n].wait_recv()
    for i in range(NT):
        ff_tile(p, i, i == 0)
        gather("ff_own%d" % i)
    for i in range(NT):
        gather("ff_other%d" % i)
        need(4 + 2 * i)
        need(5 + 2 * i)
        ff_tile(1 - p, i, False)

    cp_cot.wait()
    zero = jnp.zeros((1, D), F32)
    for r0 in range(gv.shape[0]):
        gv[r0:r0 + 1, :] = zero

    def colsum(x):
        return jnp.sum(x, axis=0, keepdims=True)

    def norm2(i, carry):
        dg, ds, db = carry
        r = rows_of(i)
        fo = xh1[r, :] * vecf[R_G1:R_G1 + 1, :] + vecf[R_S1:R_S1 + 1, :]
        val = fo + (acc[r, :] + vecf[R_B2:R_B2 + 1, :])
        centre = val - jnp.mean(val, axis=1, keepdims=True)
        spread = jnp.mean(centre * centre, axis=1, keepdims=True)
        rs = lax.rsqrt(spread + EPSILON)
        xh = centre * rs
        g2 = vecf[R_G2:R_G2 + 1, :]
        lob[r, :] = (xh * g2 + vecf[R_S2:R_S2 + 1, :]).astype(BF16)
        up = cotb[r, :].astype(F32)
        dxh = up * g2
        gin = rs * (dxh - jnp.mean(dxh, axis=1, keepdims=True) - xh * jnp.mean(dxh * xh, axis=1, keepdims=True))
        acc[r, :] = gin
        low = gin.astype(BF16)
        go[r, :] = low
        return dg + colsum(up * xh), ds + colsum(up), db + colsum(low.astype(F32))

    dg, ds, db = lax.fori_loop(0, L // TR, norm2, (zero, zero, zero))
    gv[R_G2:R_G2 + 1, :] = dg
    gv[R_S2:R_S2 + 1, :] = ds
    gv[R_B2:R_B2 + 1, :] = db
    lo_local = lc(lob, layer_out.at[p])
    lo_y = []

    def lo_send(parts):
        for i in parts:
            part = pl.ds(i * (L // 4), L // 4)
            lo_y.append(rc(lob.at[part], layer_out.at[p, part], ypeer))

    lo_send(range(LO_FIRST))

    tB[...] = go[...].T
    keep_rows = pl.ds(al(b * DH, 128), DH)
    send_rows = pl.ds(al((1 - b) * DH, 128), DH)

    table = unit_table(DH, FH, D)
    units = []
    n_res = sum(order[0] != "y" for _, _, order in table)
    landing, landing_res = landing[:len(landing) - n_res], landing[len(landing) - n_res:]
    for col, width, order in table:
        order = [axis for axis in order if axis == "y" or axis < dp_bits]
        bufs = [landing.pop(0) for _ in range(len(order) + max(dp_bits - 3, 0))]
        units.append({"at": slice(col, col + width), "order": order, "bufs": bufs, "next": 0, "r0": 0, "rows": DH,
                      "both": True, "core": [None, None], "copy": None, "path": []})
        units[-1]["res"] = bufs[0] if order[0] == "y" else landing_res.pop(0)

    def core_send(u, src, h_is_own):
        h = p if h_is_own else 1 - p
        units[u]["core"][h_is_own] = rc(src, rcore.at[h, :, units[u]["at"]], core)

    def add_block(h, r0, rows, at, src):
        step = 48 if rows % 48 == 0 else rows

        def one(i, carry):
            here = pl.ds(al(r0 + i * step, 16), step)
            gk[h, here, at] = (gk[h, here, at].astype(F32) + src(pl.ds(al(i * step, 16), step)).astype(F32)).astype(BF16)
            return carry

        lax.fori_loop(0, rows // step, one, 0)

    def start_stage(u, s):
        un = units[u]
        axis, buf, at = un["order"][s], un["bufs"][s], un["at"]
        if axis == "y":
            here = pl.ds(al(un["r0"], 16), un["rows"])
            un["copy"] = rc(gk.at[1 - p, here, at], buf.at[0], ypeer)
            un["both"] = False
            return
        rows = un["rows"] // 2
        away = pl.ds(al(un["r0"] + (1 - bit(axis)) * rows, 16), rows)
        src = gk.at[:, away, at] if un["both"] else gk.at[pl.ds(p, 1), away, at]
        un["copy"] = rc(src, buf, peer_of(axis))
        un["path"].append((axis, un["r0"], un["rows"]))
        un["r0"] = un["r0"] + bit(axis) * rows
        un["rows"] = rows

    def step(u):
        un = units[u]
        ev, n, at = un["next"], len(un["order"]), un["at"]
        un["next"] += 1
        if ev == 0:
            for own in (0,) if un["order"][0] == "y" else (0, 1):
                un["core"][own].wait_recv()
                h = p if own else 1 - p
                add_block(h, 0, DH, at, lambda r, h=h: rcore[h, r, at])
            start_stage(u, 0)
            return
        un["copy"].wait_recv()
        if ev <= n:
            buf = un["bufs"][ev - 1]
            if ev == 1 and un["order"][0] == "y":
                un["core"][1].wait_recv()
                add_block(p, 0, DH, at, lambda r: rcore[p, r, at].astype(F32) + buf[0, r, :].astype(F32))
            elif un["both"]:
                for h in range(2):
                    add_block(h, un["r0"], un["rows"], at, lambda r, h=h: buf[h, r, :])
            else:
                add_block(p, un["r0"], un["rows"], at, lambda r: buf[0, r, :])
            if ev < n:
                start_stage(u, ev)
                return
            for t in range(3, dp_bits):
                buf = un["bufs"][n + t - 3]
                mine = gk.at[pl.ds(p, 1), pl.ds(al(un["r0"], 16), un["rows"]), at]
                cp = rc(mine, buf, peer_of(t))
                cp.wait_recv()
                cp.wait_send()
                waited.append(id(cp))
                add_block(p, un["r0"], un["rows"], at, lambda r: buf[0, r, :])
            here = pl.ds(al(un["r0"], 16), un["rows"])
            un["res"][0, here, :] = gk[p, here, at]
        if un["path"]:
            axis, r0, rows = un["path"].pop()
            mine = un["res"].at[0, pl.ds(al(un["r0"], 16), un["rows"])]
            un["copy"] = rc(mine, mine, peer_of(axis))
            un["r0"], un["rows"] = r0, rows
            return
        un["out"] = lc(un["res"].at[0], gk_out.at[:, at])

    def events(place):
        for u in EVENTS[place]:
            if u < len(units):
                step(u)
            else:
                vec_step()

    def weight_grad(leftT, right, send, own, col, width):
        h = p if own else 1 - p
        send[...] = nn(leftT[send_rows, :], right).astype(BF16)
        gk[h, :, col:col + width] = nn(leftT[keep_rows, :], right).astype(BF16)

    def ff_back(own, i):
        h = p if own else 1 - p
        hid = pl.ds(al(h * FH + i * D, 128), D)
        du = (nt(go[...], gw2[hid, :]) * dact[:, hid].astype(F32)).astype(BF16)
        gb1[h * NT + i] = colsum(du.astype(F32))
        dact[:, hid] = du
        acc[...] += nt(dact[:, hid], gw1[:, hid])
        for u, leftT, side in ((2 * i, tA, dact), (2 * i + 1, tB, act)):
            send = side.at[0:DH, hid]
            weight_grad(leftT, side[:, hid], send, own, table[u][0], D)
            core_send(u, send, own)

    for i in range(NT):
        for own in (0, 1):
            ff_back(own, i)
            events("ff%d%d" % (i, own))
    if LO_PLACE == "ff":
        lo_send(range(LO_FIRST, 4))
    for t in range(FF // D):
        gv[R_B1 + t:R_B1 + t + 1, :] = gb1[t]

    def norm1_back(i, carry):
        dg, ds, db = carry
        r = rows_of(i)
        up = acc[r, :]
        xh = xh1[r, :]
        dxh = up * vecf[R_G1:R_G1 + 1, :]
        gin = rs1[r, 0:1] * (dxh - jnp.mean(dxh, axis=1, keepdims=True) - xh * jnp.mean(dxh * xh, axis=1, keepdims=True))
        acc[r, :] = gin
        low = gin.astype(BF16)
        go[r, :] = low
        return dg + colsum(up * xh), ds + colsum(up), db + colsum(low.astype(F32))

    dg, ds, db = lax.fori_loop(0, L // TR, norm1_back, (zero, zero, zero))
    gv[R_G1:R_G1 + 1, :] = dg
    gv[R_S1:R_S1 + 1, :] = ds
    gv[R_BO:R_BO + 1, :] = db
    tB[...] = go[...].T
    UO = 2 * NT
    events("n1")
    if LO_PLACE == "n1":
        lo_send(range(LO_FIRST, 4))
    for u in range(UO):
        for cp in units[u]["core"]:
            cp.wait_send()
            waited.append(id(cp))
    dc[...] = nt(go[...], gwo[...]).astype(BF16)
    tail = 2 * FH

    def part(n, h):
        return dact.at[0:DH, pl.ds(al(D + (n % 3 * 2 + h) * DH, 128), DH)]

    for own in (0, 1):
        h = p if own else 1 - p
        weight_grad(tB, c[:, pl.ds(al(h * DH, 128), DH)], part(0, h), own, tail, DH)
        core_send(UO, part(0, h), own)
    events("wo")
    tA[...] = xo[...].T
    tB[...] = xx[...].T

    def attend_back(j, carry):
        cols = pl.ds(al(j * 128, 128), 128)
        kp, vp, qp, dcp = k[:, cols], v[:, cols], q[:, cols], dc[:, cols]
        kT = kp.T
        dkv = [jnp.zeros((L, 128), F32), jnp.zeros((L, 128), F32)]
        tops = []
        for hh in range(2):
            head = 2 * j + hh
            mine = head_lanes(hh)
            none = jnp.zeros_like(kp)
            km, vm = jnp.where(mine, kp, none), jnp.where(mine, vp, none)
            qm, dcm = jnp.where(mine, qp, none), jnp.where(mine, dcp, none)
            bias = head_bias(head)
            bias = jnp.concatenate([bias, bias], axis=1)
            parts = []
            for t in range(L // 256):
                ts = slice(t * 256, (t + 1) * 256)
                prob = jnp.exp(nt(km, qp[ts]) + bias - lse[head, :, ts])
                dprob = nt(vm, dcp[ts])
                delta = jnp.sum(prob * dprob, axis=0, keepdims=True)
                dscore = (prob * (dprob - delta)).astype(BF16)
                dkv[1] += nn(prob.astype(BF16), dcm[ts])
                dkv[0] += nn(dscore, qm[ts])
                parts.append(nn(kT[hh * 64:(hh + 1) * 64, :], dscore))
            tops.append(jnp.concatenate(parts, axis=1))
        dq[:, cols] = (jnp.concatenate(tops, axis=0).T * 0.125).astype(BF16)
        dk[:, cols] = dkv[0].astype(BF16)
        dv[:, cols] = dkv[1].astype(BF16)
        return carry

    for i in range(3):
        lax.fori_loop(i * NP * 2 // 3, (i + 1) * NP * 2 // 3, attend_back, 0)
        events("ab%d" % i)
    if LO_PLACE == "ab":
        lo_send(range(LO_FIRST, 4))
    gv[R_BQ:R_BQ + 1, :] = colsum(dq[...].astype(F32))
    gv[R_BV:R_BV + 1, :] = colsum(dv[...].astype(F32))

    vec_peers = [core, ypeer] + [peer_of(t) for t in range(dp_bits)]
    vstate = {"s": 0, "cp": None, "done": False}
    gvr[0, 0] = gv[...]

    def vec_step():
        s = vstate["s"]
        if s > 0:
            vstate["cp"].wait_recv()
            total = gvr[s - 1, 0] + gvr[s - 1, 1]
            if s == len(vec_peers):
                gv[...] = total
                vstate["done"] = True
                return
            gvr[s, 0] = total
        vstate["cp"] = rc(gvr.at[s, 0], gvr.at[s, 1], vec_peers[s])
        vstate["s"] = s + 1

    vec_step()

    swapped = vecf[R_LANE:R_LANE + 1, :] > 0.5
    none = jnp.zeros((L, D), BF16)
    dc[...] = jnp.where(swapped, dk[...], none)
    flow[...] = jnp.where(swapped, dv[...], none)
    dk[...] = jnp.where(swapped, none, dk[...])
    dv[...] = jnp.where(swapped, none, dv[...])
    for n, (a, x) in enumerate(((dq, None), (dk, dc), (dv, flow))):
        u = UO + 1 + n
        for own in (0, 1):
            h = p if own else 1 - p
            hs = pl.ds(al(h * DH, 128), DH)
            if n == 2:
                units[UO]["core"][own].wait_send()
                waited.append(id(units[UO]["core"][own]))
            send = part(1 + n, h)
            for dst, rows in ((send, send_rows), (gk.at[h, :, table[u][0]:table[u][0] + DH], keep_rows)):
                val = nn(tA[rows, :], a[:, hs])
                if x is not None:
                    val = val + nn(tB[rows, :], x[:, hs])
                dst[...] = val.astype(BF16)
            core_send(u, send, own)
        events("q%d" % (5 + n))
    backs[...] = (nt(dc[...], gwk[...]) + nt(flow[...], gwv[...])).astype(BF16)
    back_c = rc(backs, backr, core)
    acc[...] += nt(dq[...], gwq[...]) + nt(dk[...], gwk[...]) + nt(dv[...], gwv[...])
    events("acc")
    lo_local.wait()
    back_c.wait_recv()
    for r0 in range(0, L, TR):
        acc[r0:r0 + TR, :] += backr[r0:r0 + TR, :].astype(F32)
    xo[...] = acc[...].astype(BF16)
    gt_local = lc(xo, grad_tokens.at[p])
    gt_y = rc(xo, grad_tokens.at[p], ypeer)
    if LO_PLACE == "end":
        lo_send(range(LO_FIRST, 4))
    events("drain")
    while not vstate["done"]:
        vec_step()
    for un in units:
        un["out"].wait()
    gt_local.wait()
    gt_y.wait_recv()
    for cp in lo_y:
        cp.wait_recv()
    for cp in sent:
        if id(cp) not in waited:
            cp.wait_send()


def finish_kernel(
    lo, gt, gk, gv,
    lo_out, gt_out, g_wq, g_bq, g_wk, g_wv, g_bv, g_wo, g_bo, g_g1, g_s1, g_w1, g_b1, g_w2, g_b2, g_g2, g_s2,
    low, wide, held, sem_in, sem_out,
):
    p, b = lax.axis_index("perm"), lax.axis_index("blk")
    D = gv.shape[1]
    DH, FH = D // 2, g_w1.shape[1]
    n_cols = gk.shape[1] // DH
    loads = [pltpu.make_async_copy(gk.at[:, i * DH:(i + 1) * DH], low.at[i], sem_in.at[i]) for i in range(n_cols)]
    for load in loads:
        load.start()
    through = [pltpu.make_async_copy(src, held.at[i], sem_in.at[n_cols + i]) for i, src in enumerate((lo, gt))]
    for move in through:
        move.start()
    stores = []
    per = FH // DH
    for i in range(n_cols):
        loads[i].wait()
        if i == per:
            for j, dst in enumerate((lo_out, gt_out)):
                through[j].wait()
                stores.append(pltpu.make_async_copy(held.at[j], dst, sem_out.at[n_cols + j]))
                stores[-1].start()
        value = low[i].T if per <= i <= 2 * per else low[i]
        wide[i] = value.astype(F32)
        if i < per:
            dst = g_w1.at[:, i * DH:(i + 1) * DH]
        elif i < 2 * per:
            dst = g_w2.at[(i - per) * DH:(i - per + 1) * DH, :]
        else:
            dst = (g_wo, g_wq, g_wk, g_wv)[i - 2 * per]
        stores.append(pltpu.make_async_copy(wide.at[i], dst, sem_out.at[i]))
        stores[-1].start()

    def put(ref, row):
        ref[...] = row.reshape(ref.shape)

    for row, ref in ((R_BO, g_bo), (R_G1, g_g1), (R_S1, g_s1), (R_B2, g_b2), (R_G2, g_g2), (R_S2, g_s2)):
        put(ref, jnp.where(b == 0, gv[row:row + 1, 0:DH], gv[row:row + 1, DH:D]))
    for row, ref in ((R_BQ, g_bq), (R_BV, g_bv)):
        n = D // 4
        left = jnp.where(b == 0, gv[row:row + 1, 0:n], gv[row:row + 1, n:2 * n])
        right = jnp.where(b == 0, gv[row:row + 1, 2 * n:3 * n], gv[row:row + 1, 3 * n:D])
        put(ref, jnp.where(p == 0, left, right))
    left = jnp.where(b == 0, gv[R_B1:R_B1 + 1, :], gv[R_B1 + 1:R_B1 + 2, :])
    right = jnp.where(b == 0, gv[R_B1 + 2:R_B1 + 3, :], gv[R_B1 + 3:R_B1 + 4, :])
    put(g_b1, jnp.where(p == 0, left, right))
    for store in stores:
        store.wait()


def per_device(
    tokens, lengths, head_route, w_query, b_query, w_key, w_value, b_value, w_out, b_out,
    first_gain, first_shift, w_inner, b_inner, w_outer, b_outer, second_gain, second_shift, cotangent,
):
    L, D = tokens.shape[1:]
    FF = w_inner.shape[1] * 2
    heads = head_route.shape[0] * 2

    bits = (lax.axis_size("dp") - 1).bit_length()

    half = FF + 4 * (D // 2)
    any_ = pl.BlockSpec(memory_space=pl.ANY)
    vm = pl.BlockSpec(memory_space=pltpu.VMEM)
    smem = pl.BlockSpec(memory_space=pltpu.SMEM)
    V = pltpu.VMEM
    layer_out, grad_tokens, reduced, vectors = pl.pallas_call(
        functools.partial(layer_kernel, heads, lax.axis_size("dp")),
        out_shape=(
            jax.ShapeDtypeStruct(tokens.shape, BF16),
            jax.ShapeDtypeStruct(tokens.shape, BF16),
            jax.ShapeDtypeStruct((D // 2, half), BF16),
            jax.ShapeDtypeStruct((16, D), F32),
        ),
        in_specs=[any_, any_, smem, smem] + [any_] * 6 + [vm] * 9,
        out_specs=(any_, any_, any_, vm),
        scratch_shapes=[
            V((L, D), BF16), V((L, D), BF16), V((L, D), BF16),
            V((D, D), BF16), V((D, D), BF16), V((D, D), BF16), V((D, D), BF16), V((D, FF), BF16), V((FF, D), BF16),
            V((4, 16, D), F32), V((16, D), F32), V((2, L, 128), F32),
            V((L, D), BF16), V((L, D), BF16), V((L, D), BF16), V((L, D), BF16),
            V((L, D), BF16), V((L, D), F32), V((L, 128), F32), V((16, 1, L), F32),
            V((L, FF), BF16), V((L, FF), BF16), V((L, D), F32), V((L, D), BF16),
            V((D, L), BF16), V((D, L), BF16), V((L, D), BF16),
            V((L, D), F32), V((L, D), BF16),
            V((16, 1, 128), F32), V((FF // D, 1, D), F32), V((FF // D, 1, D), F32),
            V((2, D // 2, half), BF16), V((2, D // 2, half), BF16),
            V((2 + bits, 2, 16, D), F32),
        ] + [V(shape, BF16) for shape in stage_shapes(unit_table(D // 2, FF // 2, D), D // 2, bits)] + [
            pltpu.SemaphoreType.DMA((32,)),
            pltpu.SemaphoreType.DMA((256,)),
            pltpu.SemaphoreType.DMA((256,)),
        ],
        compiler_params=pltpu.CompilerParams(collective_id=0, has_side_effects=True, vmem_limit_bytes=62 * 2**20),
        name="layer",
    )(tokens, cotangent, lengths, head_route, w_query, w_key, w_value, w_out, w_inner, w_outer,
      b_query, b_value, b_out, first_gain, first_shift, b_outer, second_gain, second_shift, b_inner)

    DH, FH = D // 2, FF // 2
    shapes = [(DH, DH), (D // 4,), (DH, DH), (DH, DH), (D // 4,), (DH, DH), (DH,), (DH,), (DH,), (DH, FH),
              (FF // 4,), (FH, DH), (DH,), (DH,), (DH,)]
    moved = [jax.ShapeDtypeStruct(tokens.shape, BF16)] * 2
    n_cols = half // DH
    return tuple(pl.pallas_call(
        finish_kernel,
        out_shape=moved + [jax.ShapeDtypeStruct(shape, F32) for shape in shapes],
        in_specs=[any_, any_, any_, vm],
        out_specs=[any_, any_] + [any_ if len(shape) == 2 else vm for shape in shapes],
        scratch_shapes=[V((n_cols, DH, DH), BF16), V((n_cols, DH, DH), F32), V((2,) + tokens.shape, BF16),
                        pltpu.SemaphoreType.DMA((n_cols + 2,)), pltpu.SemaphoreType.DMA((n_cols + 2,))],
        compiler_params=pltpu.CompilerParams(vmem_limit_bytes=62 * 2**20),
        name="finish",
    )(layer_out, grad_tokens, reduced, vectors))


def solution(mesh):
    placed = (
        P("dp", "blk", None), P("dp"), P("perm"), P("blk", "perm"), P(("perm", "blk")), P("blk", "perm"),
        P("blk", "perm"), P(("perm", "blk")), P("perm", "blk"), P("blk"), P("blk"), P("blk"), P("blk", "perm"),
        P(("perm", "blk")), P("perm", "blk"), P("blk"), P("blk"), P("blk"), P("dp", "blk", None),
    )
    outs = (
        P("dp", "blk", None), P("dp", "blk", None), P("blk", "perm"), P(("perm", "blk")), P("blk", "perm"),
        P("blk", "perm"), P(("perm", "blk")), P("perm", "blk"), P("blk"), P("blk"), P("blk"), P("blk", "perm"),
        P(("perm", "blk")), P("perm", "blk"), P("blk"), P("blk"), P("blk"),
    )
    return jax.shard_map(per_device, mesh=mesh, in_specs=placed, out_specs=outs, check_vma=False)
```
